32 devices in a mesh: bucket: 4 (over z), blk: 8 (over y, x, core).
Axes of the slice: x: 2, y: 2, z: 4, core: 2. Of those that a mesh axis runs over, the one named last changes fastest.
Arguments:
- residual_in: bfloat16 [5120, 767], P(('bucket', 'blk'))
- out_cotangent: bfloat16 [5120, 767], P(('bucket', 'blk')), may hold values from -6 to 6
- first_gain: float32 [768], replicated, may hold values from 0.1 to 1.9
- input_weight: bfloat16 [768, 2304], replicated, may hold values from -0.21875 to 0.21875
- query_bias: float32 [768], replicated, may hold values from -3 to 3
- value_bias: float32 [768], replicated, may hold values from -0.3 to 0.3
- output_weight: bfloat16 [768, 767], replicated, may hold values from -1.25 to 1.25
- output_bias: float32 [767], replicated, may hold values from -1.8 to 1.8
- second_gain: float32 [768], replicated, may hold values from 0.1 to 1.9
- up_weight: bfloat16 [768, 3072], replicated, may hold values from -0.21875 to 0.21875
- up_bias: float32 [3072], replicated, may hold values from -1.8 to 1.8
- down_weight: bfloat16 [3072, 767], replicated, may hold values from -0.109375 to 0.109375
- down_bias: float32 [767], replicated, may hold values from -1.8 to 1.8
- lengths: int32 [4, 2], replicated, may hold values from 128 to 1152, as said below
- offsets: int32 [4, 2], P('bucket'), may hold values from 0 to 1152, as said below
- span_order: int32 [16], replicated, may hold values from 0 to 15, as said below
Outputs:
- residual_out: bfloat16 [5120, 767], P(('bucket', 'blk'))
- residual_grad: bfloat16 [5120, 767], P(('bucket', 'blk'))
- first_gain_grad: float32 [768], replicated
- input_weight_grad: float32 [768, 2304], P(('bucket', 'blk'))
- query_bias_grad: float32 [768], replicated
- value_bias_grad: float32 [768], replicated
- output_weight_grad: float32 [768, 767], P(('bucket', 'blk'))
- output_bias_grad: float32 [767], replicated
- second_gain_grad: float32 [768], replicated
- up_weight_grad: float32 [768, 3072], P(('bucket', 'blk'))
- up_bias_grad: float32 [3072], replicated
- down_weight_grad: float32 [3072, 767], P(('bucket', 'blk'))
- down_bias_grad: float32 [767], replicated
- mean_norms: float32 [2], replicated
The draws below stay inside these ranges and needn't reach their ends.
Inputs may be any that keep to these rules, and one draw needn't show every extreme that they name: Bucket b holds two sequences: sequence s covers positions offsets[b,s] to offsets[b,s] + lengths[b,s] - 1 of the bucket's 1280 positions; lengths[b,0] >= 1024; the two sequences don't intersect; other positions are padding. offsets[b,0] = 0 and offsets[b,1] >= lengths[b,0]. Each of the 16 blocks of 80 positions appears once; for device i of blk, span_order[2i] < 8 and span_order[2i+1] = 15 - span_order[2i].
All inputs are finite; a program needn't handle non-finite values.
Results may differ from the reference program's by a relative error of at most 0.014.
Values may be sent and summed in bfloat16 or wider, within the bound.
No kernel may reach another device: no remote copies, remote signals or barrier semaphores. Data moves between devices by JAX's collectives and lax.ppermute only.
A program may use at most 256 MiB of HBM per device.

```python
import math
import jax
import jax.numpy as jnp
from jax import lax

D = 768
HEADS = 12
HEAD_DIM = 64
FF = 3072
DC = 767
TOK_DEV = 160
MINSEQ = 128
BUCKETS = 4
TOKENS = 5120
N_BLK = 8


def sequence_layout(key):
    group_rows = TOK_DEV * N_BLK
    lead_key, trail_key, spare_key = jax.random.split(key, 3)
    leading = jax.random.randint(lead_key, (BUCKETS,), group_rows - group_rows // 5, group_rows - MINSEQ + 1)
    room = group_rows - leading
    trailing = jax.random.randint(trail_key, (BUCKETS,), MINSEQ, room + 1)
    spare = jax.random.randint(spare_key, (BUCKETS,), 0, room - trailing + 1)
    leading = leading.at[0].set(group_rows - MINSEQ)
    trailing = trailing.at[0].set(MINSEQ)
    spare = spare.at[0].set(0)
    sizes_out = jnp.stack([leading, trailing], axis=1).astype(jnp.int32)
    starts = jnp.stack([jnp.zeros_like(leading), leading + spare], axis=1).astype(jnp.int32)
    return (sizes_out, starts)


def draw_lengths(key, part):
    shared = sequence_layout(key)
    return shared[0]


def draw_offsets(key, part):
    shared = sequence_layout(key)
    return shared[1]


def draw_span_order(key, part):
    key = jax.random.fold_in(key, 5)
    lower = jax.random.permutation(key, jnp.arange(N_BLK, dtype=jnp.int32))
    return jnp.stack([lower, 2 * N_BLK - 1 - lower], axis=1).reshape(2 * N_BLK).astype(jnp.int32)


def draw_residual_in(key, part):
    key = jax.random.fold_in(key, 9)
    ramp = jnp.arange(TOKENS, dtype=jnp.float32)[:, None] / TOKENS
    rise = 1.0 + 2.0 * ramp
    base = jax.random.normal(key, (TOKENS, D), jnp.float32)
    following = jnp.roll(base, -1, axis=1)
    return ((base - following)[:, :D - 1] * 0.7071 * rise).astype(jnp.bfloat16)


def shard_levels(own_key, dims, cuts, least, high):
    def one(axis_at, blocks):
        heights = jax.random.uniform(jax.random.fold_in(jax.random.fold_in(own_key, 6), axis_at), (blocks,), jnp.float32, least / len(cuts), high / len(cuts))
        return jnp.repeat(jnp.exp(heights), dims[axis_at] // blocks).reshape((-1,) + (1,) * (len(dims) - axis_at - 1))

    level = one(*cuts[0])
    for cut in cuts[1:]:
        level = level * one(*cut)
    return level


def normal_values(stream_key, extent, width, limit, pieces=(), kind=jnp.bfloat16):
    values = width * jax.random.normal(stream_key, extent, jnp.float32)
    if pieces:
        values = values * shard_levels(stream_key, extent, pieces, -0.22, 0.18)
    return jnp.clip(values, -limit, limit).astype(kind)


def setup_inputs(seed: int = 0) -> dict:
    arg_keys = jax.random.split(jax.random.key(seed), 17)
    residual_in = draw_residual_in(jax.random.fold_in(arg_keys[16], 71), 0)
    out_cotangent = normal_values(arg_keys[1], (TOKENS, DC), 1.0, 6.0, ((0, 32),))
    first_gain = jnp.clip(1.0 + 0.18 * jax.random.normal(arg_keys[2], (D,), jnp.float32), 0.1, 1.9)
    input_weight = normal_values(arg_keys[3], (D, 3 * D), D ** -0.5, 0.21875)
    query_bias = normal_values(arg_keys[4], (D,), 0.5, 3.0, (), jnp.float32)
    value_bias = normal_values(arg_keys[5], (D,), 0.05, 0.3, (), jnp.float32)
    output_weight = normal_values(arg_keys[6], (D, DC), (D * 32 // (TOK_DEV * N_BLK) + 1) ** -0.5, 1.25)
    output_bias = normal_values(arg_keys[7], (DC,), 0.3, 1.8, (), jnp.float32)
    second_gain = jnp.clip(1.0 + 0.18 * jax.random.normal(arg_keys[8], (D,), jnp.float32), 0.1, 1.9)
    up_weight = normal_values(arg_keys[9], (D, FF), D ** -0.5, 0.21875)
    up_bias = normal_values(arg_keys[10], (FF,), 0.3, 1.8, (), jnp.float32)
    down_weight = normal_values(arg_keys[11], (FF, DC), FF ** -0.5, 0.109375)
    down_bias = normal_values(arg_keys[12], (DC,), 0.3, 1.8, (), jnp.float32)
    lengths = draw_lengths(jax.random.fold_in(arg_keys[16], 71), 0)
    offsets = draw_offsets(jax.random.fold_in(arg_keys[16], 71), 0)
    span_order = draw_span_order(jax.random.fold_in(arg_keys[16], 71), 0)
    return dict(residual_in=residual_in, out_cotangent=out_cotangent, first_gain=first_gain, input_weight=input_weight, query_bias=query_bias, value_bias=value_bias, output_weight=output_weight, output_bias=output_bias, second_gain=second_gain, up_weight=up_weight, up_bias=up_bias, down_weight=down_weight, down_bias=down_bias, lengths=lengths, offsets=offsets, span_order=span_order)


@jax.custom_vjp
def low(v):
    return lax.optimization_barrier(v.astype(jnp.bfloat16)).astype(jnp.float32)

@jax.custom_vjp
def low_back(v):
    return v

def low_keep(v):
    return (low(v), None)

def low_pass(kept, grad):
    return (grad,)

def back_keep(v):
    return (v, None)

def back_low(kept, grad):
    return (low(grad),)
low.defvjp(low_keep, low_pass)
low_back.defvjp(back_keep, back_low)
epsilon = 1e-05
masked_value = -1e+30
highest = lax.Precision.HIGHEST

def center_norm(resid, gain):
    full = jnp.concatenate([resid, -lax.optimization_barrier(jnp.sum(resid, axis=1, keepdims=True))], axis=1)
    root = jnp.sqrt(lax.optimization_barrier(jnp.mean(full * full, axis=1, keepdims=True)) + epsilon)
    return (full / root * gain, root[:, 0])

def matmul(left, right):
    return jnp.dot(left, right, precision=highest, preferred_element_type=jnp.float32)

def reference(residual_in, out_cotangent, first_gain, input_weight, query_bias, value_bias, output_weight, output_bias, second_gain, up_weight, up_bias, down_weight, down_bias, lengths, offsets, span_order):
    half_rows = TOK_DEV // 2
    group_rows = TOK_DEV * N_BLK
    score_scale = HEAD_DIM ** (-0.5)
    row_ids = jnp.arange(group_rows, dtype=jnp.int32)
    places = (span_order[row_ids // half_rows] * half_rows + row_ids % half_rows).astype(jnp.int32)
    ends = offsets + lengths
    first_in = (places[None, :] >= offsets[:, 0:1]) & (places[None, :] < ends[:, 0:1])
    second_in = (places[None, :] >= offsets[:, 1:2]) & (places[None, :] < ends[:, 1:2])
    documents = jnp.where(first_in, 0, jnp.where(second_in, 1, -1)).astype(jnp.int32)
    block = math.gcd(group_rows, 512)
    blocks = group_rows // block

    def attend_group(inputs):
        query_group, keys_group, values_group, docs_group = inputs
        key_heads = keys_group.reshape(group_rows, HEADS, HEAD_DIM)
        value_heads = values_group.reshape(group_rows, HEADS, HEAD_DIM)

        @jax.checkpoint
        def attend_block(parts):
            query_block, places_block, docs_block = parts
            query_heads = query_block.reshape(block, HEADS, HEAD_DIM)
            scores = low_back(jnp.einsum('qhd,khd->hqk', query_heads, key_heads, precision=highest) * score_scale)
            allowed = (docs_block[:, None] == docs_group[None, :]) & (docs_block[:, None] >= 0) & (places[None, :] <= places_block[:, None])
            masked = jnp.where(allowed[None], scores, masked_value)
            peak = lax.optimization_barrier(jnp.max(masked, axis=2, keepdims=True))
            weights = jnp.where(allowed[None], jnp.exp(masked - peak), 0.0)
            total = lax.optimization_barrier(jnp.sum(weights, axis=2))
            valid = (docs_block >= 0).astype(jnp.float32)
            summed = jnp.einsum('hqk,khd->qhd', low(weights), value_heads, precision=highest)
            denominator = total.T + 1.0 - valid[:, None]
            return (summed / denominator[:, :, None]).reshape(block, D)
        result = lax.map(attend_block, (query_group.reshape(blocks, block, D), places.reshape(blocks, block), docs_group.reshape(blocks, block)))
        return result.reshape(group_rows, D)

    def forward(resid, gain_one, weight_in, bias_query, bias_value, weight_out, bias_out, gain_two, weight_up, bias_up, weight_down, bias_down):
        normed, first_root = center_norm(resid, gain_one)
        hidden_in = low(normed)
        projected = matmul(hidden_in, weight_in)
        query = low(low_back(projected[:, :D] + bias_query))
        keys = low(low_back(projected[:, D:2 * D]))
        values = low(low_back(projected[:, 2 * D:] + bias_value))
        grouped = (BUCKETS, group_rows, D)
        attended = lax.map(attend_group, (query.reshape(grouped), keys.reshape(grouped), values.reshape(grouped), documents))
        mixed = low(low_back(attended.reshape(TOKENS, D)))
        branch = low_back(matmul(mixed, weight_out) + bias_out)
        middle = resid + branch
        normed_two, second_root = center_norm(middle, gain_two)
        hidden_two = low(normed_two)
        upward = low_back(matmul(hidden_two, weight_up) + bias_up)
        active = low(jax.nn.gelu(upward, approximate=True))
        closing = low_back(matmul(active, weight_down) + bias_down)
        result = middle + closing
        valid = (documents.reshape(TOKENS) >= 0).astype(jnp.float32)
        stats = jnp.stack([jnp.sum(valid * first_root), jnp.sum(valid * second_root)]) / jnp.sum(valid)
        return (result, stats)
    floats = (residual_in.astype(jnp.float32), first_gain, input_weight.astype(jnp.float32), query_bias, value_bias, output_weight.astype(jnp.float32), output_bias, second_gain, up_weight.astype(jnp.float32), up_bias, down_weight.astype(jnp.float32), down_bias)
    result, pullback, stats = jax.vjp(forward, *floats, has_aux=True)
    grads = pullback(out_cotangent.astype(jnp.float32))
    return (result.astype(jnp.bfloat16), grads[0].astype(jnp.bfloat16), grads[1], grads[2], grads[3], grads[4], grads[5], grads[6], grads[7], grads[8], grads[9], grads[10], grads[11], stats)
```

```python
import jax
import jax.numpy as jnp
from jax import lax
from jax.sharding import PartitionSpec as P

D = 768
HEADS = 12
HEAD_DIM = 64


epsilon = 1e-05
masked_value = -1e30


def center_norm(resid, gain):
    full = jnp.concatenate([resid, -jnp.sum(resid, axis=1, keepdims=True)], axis=1)
    root = jnp.sqrt(jnp.mean(full * full, axis=1, keepdims=True) + epsilon)
    return (full / root * gain, root[:, 0])


def gelu_tanh(inputs):
    return jax.nn.gelu(inputs, approximate=True)


def heads_of(block):
    return block.reshape(block.shape[0], HEADS, HEAD_DIM)


def places_of(span_order, begin, count, half_rows):
    spans = lax.dynamic_slice_in_dim(span_order, begin // half_rows, count // half_rows)
    inner = jnp.arange(half_rows, dtype=jnp.int32)
    return (spans[:, None] * half_rows + inner[None, :]).reshape(count)


def documents_of(places, lengths, offsets):
    first_in = (places >= offsets[0, 0]) & (places < offsets[0, 0] + lengths[0, 0])
    second_in = (places >= offsets[0, 1]) & (places < offsets[0, 1] + lengths[0, 1])
    return jnp.where(first_in, 0, jnp.where(second_in, 1, -1)).astype(jnp.int32)


def allowed_of(query_places, query_docs, key_places, key_docs):
    same = (query_docs[:, None] == key_docs[None, :]) & (query_docs[:, None] >= 0)
    return (same & (key_places[None, :] <= query_places[:, None]))[None]


def block_shape(count, unit):
    shards = count // unit
    width = max(1, 1024 // unit)
    while shards % width != 0:
        width = width - 1
    return (shards // width, width * unit)


def general_body(
    residual_in,
    out_cotangent,
    first_gain,
    input_weight,
    query_bias,
    value_bias,
    output_weight,
    output_bias,
    second_gain,
    up_weight,
    up_bias,
    down_weight,
    down_bias,
    lengths,
    offsets,
    span_order,
):
    rows = residual_in.shape[0]
    half_rows = rows // 2
    score_scale = HEAD_DIM ** (-0.5)
    index = lax.axis_index("blk")
    bucket_index = lax.axis_index("bucket")
    own_lengths = lax.dynamic_slice_in_dim(lengths, bucket_index, 1, 0)
    valid_count = jnp.sum(lengths.astype(jnp.float32))
    query_places = places_of(span_order, index * rows, rows, half_rows)
    query_docs = documents_of(query_places, own_lengths, offsets)
    valid = (query_docs >= 0).astype(jnp.float32)
    resid = residual_in.astype(jnp.float32)
    normed, first_back, first_root = jax.vjp(center_norm, resid, first_gain, has_aux=True)
    hidden_in = normed.astype(jnp.bfloat16)
    projected = jnp.dot(hidden_in, input_weight, preferred_element_type=jnp.float32)
    query = (projected[:, :D] + query_bias).astype(jnp.bfloat16)
    keys = projected[:, D : 2 * D].astype(jnp.bfloat16)
    values = (projected[:, 2 * D :] + value_bias).astype(jnp.bfloat16)
    query_heads = heads_of(query)
    key_heads = heads_of(keys)
    value_heads = heads_of(values)
    initial = (
        jnp.full((HEADS, rows), masked_value, jnp.float32),
        jnp.zeros((HEADS, rows), jnp.float32),
        jnp.zeros((HEADS, rows, HEAD_DIM), jnp.float32),
    )
    state = initial
    key_piece = lax.all_gather(keys, "blk", axis=0, tiled=True)
    value_piece = lax.all_gather(values, "blk", axis=0, tiled=True)
    count = key_piece.shape[0]
    number, width = block_shape(count, rows)
    key_places = places_of(span_order, jnp.int32(0), count, half_rows)
    key_docs = documents_of(key_places, own_lengths, offsets)

    def forward_advance(state, parts):
        key_block, value_block, places_block, docs_block = parts
        peak, total, summed = state
        scores = (
            jnp.einsum(
                "qhd,khd->hqk", query_heads, heads_of(key_block), preferred_element_type=jnp.float32
            )
            * score_scale
        )
        allowed = allowed_of(query_places, query_docs, places_block, docs_block)
        masked = jnp.where(allowed, scores, masked_value)
        new_peak = jnp.maximum(peak, jnp.max(masked, axis=2))
        decay = jnp.exp(peak - new_peak)
        weights = jnp.where(allowed, jnp.exp(masked - new_peak[:, :, None]), 0.0)
        total = total * decay + jnp.sum(weights, axis=2)
        summed = summed * decay[:, :, None] + jnp.einsum(
            "hqk,khd->hqd",
            weights.astype(jnp.bfloat16),
            heads_of(value_block),
            preferred_element_type=jnp.float32,
        )
        return ((new_peak, total, summed), None)

    state, _ = lax.scan(
        forward_advance,
        state,
        (
            key_piece.reshape(number, width, D),
            value_piece.reshape(number, width, D),
            key_places.reshape(number, width),
            key_docs.reshape(number, width),
        ),
    )
    peak, total, summed = state
    denominator = total + 1.0 - valid[None, :]
    attended = summed / denominator[:, :, None]
    log_total = peak + jnp.log(denominator)
    mixed = attended.transpose(1, 0, 2).reshape(rows, D).astype(jnp.bfloat16)
    branch = jnp.dot(mixed, output_weight, preferred_element_type=jnp.float32) + output_bias
    middle = resid + branch
    normed_two, second_back, second_root = jax.vjp(center_norm, middle, second_gain, has_aux=True)
    hidden_two = normed_two.astype(jnp.bfloat16)
    upward = jnp.dot(hidden_two, up_weight, preferred_element_type=jnp.float32) + up_bias
    active_float, gelu_back = jax.vjp(gelu_tanh, upward)
    active = active_float.astype(jnp.bfloat16)
    closing = jnp.dot(active, down_weight, preferred_element_type=jnp.float32) + down_bias
    residual_out = (middle + closing).astype(jnp.bfloat16)
    stat_sums = jnp.stack([jnp.sum(valid * first_root), jnp.sum(valid * second_root)])
    stat_sums = lax.psum(stat_sums, ("bucket", "blk"))
    cotangent = out_cotangent.astype(jnp.float32)
    down_grad = jnp.einsum("rf,rc->fc", active, out_cotangent, preferred_element_type=jnp.float32)
    down_bias_grad = jnp.sum(cotangent, axis=0)
    active_grad = jnp.einsum(
        "rc,fc->rf", out_cotangent, down_weight, preferred_element_type=jnp.float32
    )
    (upward_float,) = gelu_back(active_grad)
    upward_grad = upward_float.astype(jnp.bfloat16)
    up_grad = jnp.einsum("rd,rf->df", hidden_two, upward_grad, preferred_element_type=jnp.float32)
    up_bias_grad = jnp.sum(upward_grad.astype(jnp.float32), axis=0)
    hidden_two_grad = jnp.einsum(
        "rf,df->rd", upward_grad, up_weight, preferred_element_type=jnp.float32
    )
    middle_part, second_gain_grad = second_back(hidden_two_grad)
    middle_grad = cotangent + middle_part
    branch_grad = middle_grad.astype(jnp.bfloat16)
    output_grad = jnp.einsum("rd,rc->dc", mixed, branch_grad, preferred_element_type=jnp.float32)
    output_bias_grad = jnp.sum(branch_grad.astype(jnp.float32), axis=0)
    attended_grad = jnp.einsum(
        "rc,dc->rd", branch_grad, output_weight, preferred_element_type=jnp.float32
    ).astype(jnp.bfloat16)
    grad_heads = heads_of(attended_grad)
    delta = jnp.einsum("rhd,hrd->hr", grad_heads.astype(jnp.float32), attended)
    query_zero = jnp.zeros((rows, HEADS, HEAD_DIM), jnp.float32)
    accum = query_zero
    key_piece = lax.all_gather(keys, "blk", axis=0, tiled=True)
    value_piece = lax.all_gather(values, "blk", axis=0, tiled=True)
    count = key_piece.shape[0]
    number, width = block_shape(count, rows)
    key_places = places_of(span_order, jnp.int32(0), count, half_rows)
    key_docs = documents_of(key_places, own_lengths, offsets)

    def query_advance(accum, parts):
        key_block, value_block, places_block, docs_block = parts
        block_keys = heads_of(key_block)
        scores = (
            jnp.einsum("qhd,khd->hqk", query_heads, block_keys, preferred_element_type=jnp.float32)
            * score_scale
        )
        allowed = allowed_of(query_places, query_docs, places_block, docs_block)
        chance = jnp.where(
            allowed, jnp.exp(jnp.where(allowed, scores, masked_value) - log_total[:, :, None]), 0.0
        )
        push = jnp.einsum(
            "qhd,khd->hqk", grad_heads, heads_of(value_block), preferred_element_type=jnp.float32
        )
        slope = (chance * (push - delta[:, :, None])).astype(jnp.bfloat16)
        accum = (
            accum
            + jnp.einsum("hqk,khd->qhd", slope, block_keys, preferred_element_type=jnp.float32)
            * score_scale
        )
        return (accum, None)

    accum, _ = lax.scan(
        query_advance,
        accum,
        (
            key_piece.reshape(number, width, D),
            value_piece.reshape(number, width, D),
            key_places.reshape(number, width),
            key_docs.reshape(number, width),
        ),
    )
    log_all, delta_all = (
        lax.all_gather(log_total.T, "blk", axis=0, tiled=True),
        lax.all_gather(delta.T, "blk", axis=0, tiled=True),
    )
    key_zero = jnp.zeros((rows, HEADS, HEAD_DIM), jnp.float32)
    state = (key_zero, key_zero)
    begin = jnp.int32(0)
    query_piece = lax.all_gather(query, "blk", axis=0, tiled=True)
    grad_piece = lax.all_gather(attended_grad, "blk", axis=0, tiled=True)
    count = query_piece.shape[0]
    number, width = block_shape(count, rows)
    piece_places = places_of(span_order, begin, count, half_rows)
    piece_docs = documents_of(piece_places, own_lengths, offsets)
    piece_log = lax.dynamic_slice_in_dim(log_all, begin, count, 0)
    piece_delta = lax.dynamic_slice_in_dim(delta_all, begin, count, 0)

    def key_advance(state, parts):
        query_block, grad_block, places_block, docs_block, log_block, delta_block = parts
        key_sum, value_sum = state
        block_query = heads_of(query_block)
        block_grad = heads_of(grad_block)
        scores = (
            jnp.einsum("qhd,khd->hqk", block_query, key_heads, preferred_element_type=jnp.float32)
            * score_scale
        )
        allowed = allowed_of(places_block, docs_block, query_places, query_docs)
        chance = jnp.where(
            allowed,
            jnp.exp(jnp.where(allowed, scores, masked_value) - log_block.T[:, :, None]),
            0.0,
        )
        value_sum = value_sum + jnp.einsum(
            "hqk,qhd->khd",
            chance.astype(jnp.bfloat16),
            block_grad,
            preferred_element_type=jnp.float32,
        )
        push = jnp.einsum(
            "qhd,khd->hqk", block_grad, value_heads, preferred_element_type=jnp.float32
        )
        slope = (chance * (push - delta_block.T[:, :, None])).astype(jnp.bfloat16)
        key_sum = (
            key_sum
            + jnp.einsum("hqk,qhd->khd", slope, block_query, preferred_element_type=jnp.float32)
            * score_scale
        )
        return ((key_sum, value_sum), None)

    state, _ = lax.scan(
        key_advance,
        state,
        (
            query_piece.reshape(number, width, D),
            grad_piece.reshape(number, width, D),
            piece_places.reshape(number, width),
            piece_docs.reshape(number, width),
            piece_log.reshape(number, width, HEADS),
            piece_delta.reshape(number, width, HEADS),
        ),
    )
    key_sum, value_sum = state
    query_low = accum.reshape(rows, D).astype(jnp.bfloat16)
    key_low = key_sum.reshape(rows, D).astype(jnp.bfloat16)
    value_low = value_sum.reshape(rows, D).astype(jnp.bfloat16)
    projected_grad = jnp.concatenate([query_low, key_low, value_low], axis=1)
    input_grad = jnp.einsum(
        "rd,re->de", hidden_in, projected_grad, preferred_element_type=jnp.float32
    )
    query_bias_grad = jnp.sum(query_low.astype(jnp.float32), axis=0)
    value_bias_grad = jnp.sum(value_low.astype(jnp.float32), axis=0)
    hidden_in_grad = jnp.einsum(
        "re,de->rd", projected_grad, input_weight, preferred_element_type=jnp.float32
    )
    resid_part, first_gain_grad = first_back(hidden_in_grad)
    residual_grad = (middle_grad + resid_part).astype(jnp.bfloat16)
    input_part, output_part, up_part, down_part = (
        lax.psum_scatter(input_grad, ("bucket", "blk"), scatter_dimension=0, tiled=True),
        lax.psum_scatter(output_grad, ("bucket", "blk"), scatter_dimension=0, tiled=True),
        lax.psum_scatter(up_grad, ("bucket", "blk"), scatter_dimension=0, tiled=True),
        lax.psum_scatter(down_grad, ("bucket", "blk"), scatter_dimension=0, tiled=True),
    )
    (
        first_sum,
        query_sum_bias,
        value_sum_bias,
        output_sum_bias,
        second_sum,
        up_sum_bias,
        down_sum_bias,
    ) = lax.psum(
        (
            first_gain_grad,
            query_bias_grad,
            value_bias_grad,
            output_bias_grad,
            second_gain_grad,
            up_bias_grad,
            down_bias_grad,
        ),
        ("bucket", "blk"),
    )
    mean_norms = stat_sums / valid_count
    return (
        residual_out,
        residual_grad,
        first_sum,
        input_part,
        query_sum_bias,
        value_sum_bias,
        output_part,
        output_sum_bias,
        second_sum,
        up_part,
        up_sum_bias,
        down_part,
        down_sum_bias,
        mean_norms,
    )


SPLIT = HEADS // 4 * HEAD_DIM


def relative(blocks, me):
    pairs = blocks.reshape((2, 2) + blocks.shape[1:])
    pairs = jnp.where(me % 2 == 1, pairs[:, ::-1], pairs)
    pairs = jnp.where(me // 2 == 1, pairs[::-1], pairs)
    return pairs.reshape(blocks.shape)


def swap_chip(block, step):
    return lax.ppermute(block, "blk", [(k, k ^ (2 * step)) for k in range(8)])


def swap_core(block):
    return lax.ppermute(block, "blk", [(k, k ^ 1) for k in range(8)])


def shift_bucket(block, step):
    return lax.ppermute(block, "bucket", [(b, (b + step) % 4) for b in range(4)])


def exchange(blocks):
    return [blocks[0]] + [swap_chip(blocks[r], r) for r in (1, 2, 3)]


def gather(block):
    return exchange([block] * 4)


def pack(piece):
    half = piece.shape[0] // 2
    return jnp.concatenate([piece[:half], piece[half:]], axis=1)


def unpack(piece):
    wide = piece.shape[1] // 2
    return jnp.concatenate([piece[:, :wide], piece[:, wide:]], axis=0)


def by_chip(full):
    return full.reshape(full.shape[0], 4, full.shape[1] // 4).transpose(1, 0, 2)


def total_over_all(vector):
    vector = vector + swap_core(vector)
    vector = vector + swap_chip(vector, 1)
    vector = vector + swap_chip(vector, 2)
    vector = vector + lax.ppermute(vector, "bucket", [(0, 1), (1, 0), (2, 3), (3, 2)])
    vector = vector + lax.ppermute(vector, "bucket", [(0, 2), (2, 0), (1, 3), (3, 1)])
    return vector


def over_buckets(blocks, core, bucket):
    own = jnp.where(core == 1, blocks[:, 1], blocks[:, 0])
    other = jnp.where(core == 1, blocks[:, 0], blocks[:, 1])
    chip_sum = (own.astype(jnp.float32) + swap_core(other).astype(jnp.float32)).astype(jnp.bfloat16)
    turned = jnp.roll(chip_sum, -bucket, axis=0)
    total = turned[0].astype(jnp.float32)
    for step in (1, 2, 3):
        total = total + shift_bucket(turned[step], step).astype(jnp.float32)
    return total


def body(
    residual_in,
    out_cotangent,
    first_gain,
    input_weight,
    query_bias,
    value_bias,
    output_weight,
    output_bias,
    second_gain,
    up_weight,
    up_bias,
    down_weight,
    down_bias,
    lengths,
    offsets,
    span_order,
):
    rows = residual_in.shape[0]
    half_rows = rows // 2
    low = jnp.bfloat16
    wide = jnp.float32
    index = lax.axis_index("blk")
    bucket = lax.axis_index("bucket")
    core = index % 2
    me = index // 2
    own_lengths = lax.dynamic_slice_in_dim(lengths, bucket, 1, 0)[0]
    starts = offsets[0]
    valid_count = jnp.sum(lengths.astype(wide))
    inner = jnp.arange(half_rows, dtype=jnp.int32)
    places = (span_order[:, None] * half_rows + inner[None, :]).reshape(4, 2, rows)
    places = relative(places, me)
    same_core = jnp.where(core == 1, places[:, 1], places[:, 0])
    other_core = jnp.where(core == 1, places[:, 0], places[:, 1])
    query_places = same_core.reshape(4 * rows)
    key_places = jnp.concatenate([query_places, other_core.reshape(4 * rows)])
    first_in = (query_places >= starts[0]) & (query_places < starts[0] + own_lengths[0])
    second_in = (query_places >= starts[1]) & (query_places < starts[1] + own_lengths[1])
    low_bound = jnp.where(first_in, starts[0], starts[1])
    high_bound = jnp.where(first_in | second_in, query_places, -1)
    valid_all = (first_in | second_in).astype(wide)
    valid = valid_all[:rows]
    allowed = (key_places[None, :] >= low_bound[:, None]) & (
        key_places[None, :] <= high_bound[:, None]
    )

    resid = residual_in.astype(wide)
    normed, first_back, first_root = jax.vjp(center_norm, resid, first_gain, has_aux=True)
    hidden_in = normed.astype(low)
    projected = jnp.dot(hidden_in, input_weight, preferred_element_type=wide)
    query = ((projected[:, :D] + query_bias) * HEAD_DIM**-0.5).astype(low)
    keys = projected[:, D : 2 * D].astype(low)
    values = (projected[:, 2 * D :] + value_bias).astype(low)
    pieces = [by_chip(query), by_chip(keys), by_chip(values)]
    sent = jnp.stack(
        [jnp.concatenate([pack(p[j]) for p in pieces], axis=0) for j in range(4)]
    )
    got = exchange(relative(sent, me))
    parts = [
        jnp.concatenate([unpack(g[i * half_rows : (i + 1) * half_rows]) for g in got], axis=0)
        for i in range(3)
    ]
    head_query = parts[0]
    both = jnp.concatenate([parts[1], parts[2]], axis=1)
    other_both = swap_core(both)
    head_keys = jnp.concatenate([parts[1], other_both[:, :SPLIT]], axis=0)
    head_values = jnp.concatenate([parts[2], other_both[:, SPLIT:]], axis=0)
    hidden_all = jnp.concatenate(gather(hidden_in), axis=0)
    cot_own = jnp.pad(out_cotangent, ((0, 0), (0, 1)))
    cot_all = jnp.concatenate(gather(cot_own), axis=0)

    split_q = head_query.reshape(4 * rows, 3, HEAD_DIM)
    split_k = head_keys.reshape(8 * rows, 3, HEAD_DIM)
    split_v = head_values.reshape(8 * rows, 3, HEAD_DIM)
    scores = jnp.einsum("qhd,khd->hqk", split_q, split_k, preferred_element_type=wide)
    masked = jnp.where(allowed[None], scores, masked_value)
    peak = jnp.max(masked, axis=2, keepdims=True)
    weights = jnp.where(allowed[None], jnp.exp(masked - peak), 0.0)
    denominator = jnp.sum(weights, axis=2) + 1.0 - valid_all[None]
    chance = weights / denominator[:, :, None]
    attended = (
        jnp.einsum("hqk,khd->hqd", weights.astype(low), split_v, preferred_element_type=wide)
        / denominator[:, :, None]
    )
    mixed_heads = attended.transpose(1, 0, 2).reshape(4 * rows, SPLIT).astype(low)
    back = exchange([pack(mixed_heads[r * rows : (r + 1) * rows]) for r in range(4)])
    mixed = relative(jnp.stack([unpack(g) for g in back]), me)
    mixed = mixed.transpose(1, 0, 2).reshape(rows, D)

    branch = jnp.dot(mixed, output_weight, preferred_element_type=wide) + output_bias
    middle = resid + branch
    normed_two, second_back, second_root = jax.vjp(center_norm, middle, second_gain, has_aux=True)
    hidden_two = normed_two.astype(low)
    upward = jnp.dot(hidden_two, up_weight, preferred_element_type=wide) + up_bias
    active_float, gelu_back = jax.vjp(gelu_tanh, upward)
    active = active_float.astype(low)
    closing = jnp.dot(active, down_weight, preferred_element_type=wide) + down_bias
    residual_out = (middle + closing).astype(low)
    stat_sums = jnp.stack([jnp.sum(valid * first_root), jnp.sum(valid * second_root)])
    cotangent = out_cotangent.astype(wide)
    active_grad = jnp.einsum("rc,fc->rf", out_cotangent, down_weight, preferred_element_type=wide)
    (upward_float,) = gelu_back(active_grad)
    upward_grad = upward_float.astype(low)
    hidden_two_grad = jnp.einsum("rf,df->rd", upward_grad, up_weight, preferred_element_type=wide)
    middle_part, second_gain_grad = second_back(hidden_two_grad)
    middle_grad = cotangent + middle_part
    branch_grad = middle_grad.astype(low)

    branch_own = jnp.pad(branch_grad, ((0, 0), (0, 1)))
    branch_all = jnp.concatenate(gather(branch_own), axis=0)
    hidden_two_all = jnp.concatenate(gather(hidden_two), axis=0)
    active_sent = active.reshape(rows, 4, 4, 192).transpose(2, 0, 1, 3).reshape(4, rows, D)
    active_all = jnp.concatenate(exchange(relative(active_sent, me)), axis=0)
    upward_all = jnp.concatenate(exchange(relative(by_chip(upward_grad), me)), axis=0)

    out_rows = lax.dynamic_slice_in_dim(output_weight, me * SPLIT, SPLIT, 0)
    attended_grad = jnp.einsum(
        "rc,dc->rd", branch_all[:, : D - 1], out_rows, preferred_element_type=wide
    ).astype(low)
    split_g = attended_grad.reshape(4 * rows, 3, HEAD_DIM)
    push = jnp.einsum("qhd,khd->hqk", split_g, split_v, preferred_element_type=wide)
    delta = jnp.einsum("qhd,hqd->hq", split_g.astype(wide), attended)
    slope = (chance * (push - delta[:, :, None])).astype(low)
    query_grad = jnp.einsum("hqk,khd->qhd", slope, split_k, preferred_element_type=wide)
    key_grad = jnp.einsum("hqk,qhd->khd", slope, split_q, preferred_element_type=wide)
    value_grad = jnp.einsum("hqk,qhd->khd", chance.astype(low), split_g, preferred_element_type=wide)
    query_low = (query_grad * HEAD_DIM**-0.5).reshape(4 * rows, SPLIT).astype(low)
    both_grad = jnp.concatenate(
        [key_grad.reshape(8 * rows, SPLIT), value_grad.reshape(8 * rows, SPLIT)], axis=1
    )
    arrived = swap_core(both_grad[4 * rows :].astype(low))
    both_low = (both_grad[: 4 * rows] + arrived.astype(wide)).astype(low)
    head_grads = jnp.concatenate([query_low, both_low], axis=1)
    home = exchange(
        [
            jnp.concatenate(
                [
                    pack(head_grads[r * rows : (r + 1) * rows, i * SPLIT : (i + 1) * SPLIT])
                    for i in range(3)
                ],
                axis=0,
            )
            for r in range(4)
        ]
    )
    home = relative(jnp.stack(home), me)
    projected_grad = jnp.concatenate(
        [
            jnp.concatenate(
                [unpack(home[j, i * half_rows : (i + 1) * half_rows]) for j in range(4)], axis=1
            )
            for i in range(3)
        ],
        axis=1,
    )

    down_part = jnp.einsum("rf,rc->fc", active_all, cot_all, preferred_element_type=wide)
    down_total = over_buckets(
        down_part.astype(low).reshape(4, 2, 192 // 2, D), core, bucket
    )[:, : D - 1]
    up_part = jnp.einsum("rd,rf->df", hidden_two_all, upward_all, preferred_element_type=wide)
    up_part = up_part.astype(low).reshape(4, 4, 2, 24, D).transpose(0, 2, 1, 3, 4)
    up_sum = over_buckets(up_part, core, bucket)
    up_home = relative(jnp.stack(exchange(relative(up_sum, me))), me)
    up_total = up_home.transpose(1, 0, 2).reshape(24, 4 * D)
    out_part = jnp.einsum("rd,rc->dc", mixed_heads, branch_all, preferred_element_type=wide)
    out_sum = over_buckets(out_part.astype(low).reshape(4, 2, 24, D), core, bucket)
    out_total = lax.ppermute(
        out_sum,
        ("bucket", "blk"),
        [(b * 8 + j * 2 + c, j * 8 + b * 2 + c) for b in range(4) for j in range(4) for c in range(2)],
    )[:, : D - 1]
    in_part = jnp.einsum("rd,re->de", hidden_all, head_grads, preferred_element_type=wide)
    in_part = in_part.astype(low).reshape(4, 4, 2, 24, 3 * SPLIT).transpose(0, 2, 1, 3, 4)
    in_sum = over_buckets(in_part, core, bucket)
    in_home = relative(jnp.stack(exchange(relative(in_sum, me))), me)
    in_total = in_home.reshape(4, 24, 3, SPLIT).transpose(1, 2, 0, 3).reshape(24, 3 * D)

    hidden_in_grad = jnp.einsum(
        "re,de->rd", projected_grad, input_weight, preferred_element_type=wide
    )
    resid_part, first_gain_grad = first_back(hidden_in_grad)
    residual_grad = (middle_grad + resid_part).astype(low)
    pieces = [
        first_gain_grad,
        jnp.sum(projected_grad[:, :D].astype(wide), axis=0),
        jnp.sum(projected_grad[:, 2 * D :].astype(wide), axis=0),
        jnp.sum(branch_own.astype(wide), axis=0),
        second_gain_grad,
        jnp.sum(upward_grad.astype(wide), axis=0),
        jnp.sum(cot_own.astype(wide), axis=0),
        jnp.pad(stat_sums, (0, 126)),
    ]
    sums = total_over_all(jnp.concatenate(pieces))
    ends = [0]
    for piece in pieces:
        ends.append(ends[-1] + piece.shape[0])
    first_sum, query_sum, value_sum, output_sum, second_sum, up_sum_bias, down_sum, stats = [
        sums[a:b] for a, b in zip(ends[:-1], ends[1:])
    ]
    return (
        residual_out,
        residual_grad,
        first_sum,
        in_total,
        query_sum,
        value_sum,
        out_total,
        output_sum[: D - 1],
        second_sum,
        up_total,
        up_sum_bias,
        down_total,
        down_sum[: D - 1],
        stats[:2] / valid_count,
    )


def solution(mesh):
    placed = (
        P(("bucket", "blk"), None),
        P(("bucket", "blk"), None),
        P(),
        P(),
        P(),
        P(),
        P(),
        P(),
        P(),
        P(),
        P(),
        P(),
        P(),
        P(),
        P("bucket", None),
        P(),
    )
    return jax.shard_map(
        body if dict(mesh.shape) == {"bucket": 4, "blk": 8} else general_body,
        mesh=mesh,
        in_specs=placed,
        out_specs=(
            P(("bucket", "blk"), None),
            P(("bucket", "blk"), None),
            P(),
            P(("bucket", "blk"), None),
            P(),
            P(),
            P(("bucket", "blk"), None),
            P(),
            P(),
            P(("bucket", "blk"), None),
            P(),
            P(("bucket", "blk"), None),
            P(),
            P(),
        ),
        check_vma=False,
    )
```

```python
import jax
import jax.numpy as jnp
from jax import lax
from jax.experimental import pallas as pl
from jax.experimental.pallas import tpu as pltpu
from jax.sharding import PartitionSpec as P

D = 768
HEADS = 12
HEAD_DIM = 64


epsilon = 1e-05
masked_value = -1e30


def center_norm(resid, gain):
    full = jnp.concatenate([resid, -jnp.sum(resid, axis=1, keepdims=True)], axis=1)
    root = jnp.sqrt(jnp.mean(full * full, axis=1, keepdims=True) + epsilon)
    return (full / root * gain, root[:, 0])


def gelu_tanh(inputs):
    return jax.nn.gelu(inputs, approximate=True)


def heads_of(block):
    return block.reshape(block.shape[0], HEADS, HEAD_DIM)


def places_of(span_order, begin, count, half_rows):
    spans = lax.dynamic_slice_in_dim(span_order, begin // half_rows, count // half_rows)
    inner = jnp.arange(half_rows, dtype=jnp.int32)
    return (spans[:, None] * half_rows + inner[None, :]).reshape(count)


def documents_of(places, lengths, offsets):
    first_in = (places >= offsets[0, 0]) & (places < offsets[0, 0] + lengths[0, 0])
    second_in = (places >= offsets[0, 1]) & (places < offsets[0, 1] + lengths[0, 1])
    return jnp.where(first_in, 0, jnp.where(second_in, 1, -1)).astype(jnp.int32)


def allowed_of(query_places, query_docs, key_places, key_docs):
    same = (query_docs[:, None] == key_docs[None, :]) & (query_docs[:, None] >= 0)
    return (same & (key_places[None, :] <= query_places[:, None]))[None]


def block_shape(count, unit):
    shards = count // unit
    width = max(1, 1024 // unit)
    while shards % width != 0:
        width = width - 1
    return (shards // width, width * unit)


def general_body(
    residual_in,
    out_cotangent,
    first_gain,
    input_weight,
    query_bias,
    value_bias,
    output_weight,
    output_bias,
    second_gain,
    up_weight,
    up_bias,
    down_weight,
    down_bias,
    lengths,
    offsets,
    span_order,
):
    rows = residual_in.shape[0]
    half_rows = rows // 2
    score_scale = HEAD_DIM ** (-0.5)
    index = lax.axis_index("blk")
    bucket_index = lax.axis_index("bucket")
    own_lengths = lax.dynamic_slice_in_dim(lengths, bucket_index, 1, 0)
    valid_count = jnp.sum(lengths.astype(jnp.float32))
    query_places = places_of(span_order, index * rows, rows, half_rows)
    query_docs = documents_of(query_places, own_lengths, offsets)
    valid = (query_docs >= 0).astype(jnp.float32)
    resid = residual_in.astype(jnp.float32)
    normed, first_back, first_root = jax.vjp(center_norm, resid, first_gain, has_aux=True)
    hidden_in = normed.astype(jnp.bfloat16)
    projected = jnp.dot(hidden_in, input_weight, preferred_element_type=jnp.float32)
    query = (projected[:, :D] + query_bias).astype(jnp.bfloat16)
    keys = projected[:, D : 2 * D].astype(jnp.bfloat16)
    values = (projected[:, 2 * D :] + value_bias).astype(jnp.bfloat16)
    query_heads = heads_of(query)
    key_heads = heads_of(keys)
    value_heads = heads_of(values)
    initial = (
        jnp.full((HEADS, rows), masked_value, jnp.float32),
        jnp.zeros((HEADS, rows), jnp.float32),
        jnp.zeros((HEADS, rows, HEAD_DIM), jnp.float32),
    )
    state = initial
    key_piece = lax.all_gather(keys, "blk", axis=0, tiled=True)
    value_piece = lax.all_gather(values, "blk", axis=0, tiled=True)
    count = key_piece.shape[0]
    number, width = block_shape(count, rows)
    key_places = places_of(span_order, jnp.int32(0), count, half_rows)
    key_docs = documents_of(key_places, own_lengths, offsets)

    def forward_advance(state, parts):
        key_block, value_block, places_block, docs_block = parts
        peak, total, summed = state
        scores = (
            jnp.einsum(
                "qhd,khd->hqk", query_heads, heads_of(key_block), preferred_element_type=jnp.float32
            )
            * score_scale
        )
        allowed = allowed_of(query_places, query_docs, places_block, docs_block)
        masked = jnp.where(allowed, scores, masked_value)
        new_peak = jnp.maximum(peak, jnp.max(masked, axis=2))
        decay = jnp.exp(peak - new_peak)
        weights = jnp.where(allowed, jnp.exp(masked - new_peak[:, :, None]), 0.0)
        total = total * decay + jnp.sum(weights, axis=2)
        summed = summed * decay[:, :, None] + jnp.einsum(
            "hqk,khd->hqd",
            weights.astype(jnp.bfloat16),
            heads_of(value_block),
            preferred_element_type=jnp.float32,
        )
        return ((new_peak, total, summed), None)

    state, _ = lax.scan(
        forward_advance,
        state,
        (
            key_piece.reshape(number, width, D),
            value_piece.reshape(number, width, D),
            key_places.reshape(number, width),
            key_docs.reshape(number, width),
        ),
    )
    peak, total, summed = state
    denominator = total + 1.0 - valid[None, :]
    attended = summed / denominator[:, :, None]
    log_total = peak + jnp.log(denominator)
    mixed = attended.transpose(1, 0, 2).reshape(rows, D).astype(jnp.bfloat16)
    branch = jnp.dot(mixed, output_weight, preferred_element_type=jnp.float32) + output_bias
    middle = resid + branch
    normed_two, second_back, second_root = jax.vjp(center_norm, middle, second_gain, has_aux=True)
    hidden_two = normed_two.astype(jnp.bfloat16)
    upward = jnp.dot(hidden_two, up_weight, preferred_element_type=jnp.float32) + up_bias
    active_float, gelu_back = jax.vjp(gelu_tanh, upward)
    active = active_float.astype(jnp.bfloat16)
    closing = jnp.dot(active, down_weight, preferred_element_type=jnp.float32) + down_bias
    residual_out = (middle + closing).astype(jnp.bfloat16)
    stat_sums = jnp.stack([jnp.sum(valid * first_root), jnp.sum(valid * second_root)])
    stat_sums = lax.psum(stat_sums, ("bucket", "blk"))
    cotangent = out_cotangent.astype(jnp.float32)
    down_grad = jnp.einsum("rf,rc->fc", active, out_cotangent, preferred_element_type=jnp.float32)
    down_bias_grad = jnp.sum(cotangent, axis=0)
    active_grad = jnp.einsum(
        "rc,fc->rf", out_cotangent, down_weight, preferred_element_type=jnp.float32
    )
    (upward_float,) = gelu_back(active_grad)
    upward_grad = upward_float.astype(jnp.bfloat16)
    up_grad = jnp.einsum("rd,rf->df", hidden_two, upward_grad, preferred_element_type=jnp.float32)
    up_bias_grad = jnp.sum(upward_grad.astype(jnp.float32), axis=0)
    hidden_two_grad = jnp.einsum(
        "rf,df->rd", upward_grad, up_weight, preferred_element_type=jnp.float32
    )
    middle_part, second_gain_grad = second_back(hidden_two_grad)
    middle_grad = cotangent + middle_part
    branch_grad = middle_grad.astype(jnp.bfloat16)
    output_grad = jnp.einsum("rd,rc->dc", mixed, branch_grad, preferred_element_type=jnp.float32)
    output_bias_grad = jnp.sum(branch_grad.astype(jnp.float32), axis=0)
    attended_grad = jnp.einsum(
        "rc,dc->rd", branch_grad, output_weight, preferred_element_type=jnp.float32
    ).astype(jnp.bfloat16)
    grad_heads = heads_of(attended_grad)
    delta = jnp.einsum("rhd,hrd->hr", grad_heads.astype(jnp.float32), attended)
    query_zero = jnp.zeros((rows, HEADS, HEAD_DIM), jnp.float32)
    accum = query_zero
    key_piece = lax.all_gather(keys, "blk", axis=0, tiled=True)
    value_piece = lax.all_gather(values, "blk", axis=0, tiled=True)
    count = key_piece.shape[0]
    number, width = block_shape(count, rows)
    key_places = places_of(span_order, jnp.int32(0), count, half_rows)
    key_docs = documents_of(key_places, own_lengths, offsets)

    def query_advance(accum, parts):
        key_block, value_block, places_block, docs_block = parts
        block_keys = heads_of(key_block)
        scores = (
            jnp.einsum("qhd,khd->hqk", query_heads, block_keys, preferred_element_type=jnp.float32)
            * score_scale
        )
        allowed = allowed_of(query_places, query_docs, places_block, docs_block)
        chance = jnp.where(
            allowed, jnp.exp(jnp.where(allowed, scores, masked_value) - log_total[:, :, None]), 0.0
        )
        push = jnp.einsum(
            "qhd,khd->hqk", grad_heads, heads_of(value_block), preferred_element_type=jnp.float32
        )
        slope = (chance * (push - delta[:, :, None])).astype(jnp.bfloat16)
        accum = (
            accum
            + jnp.einsum("hqk,khd->qhd", slope, block_keys, preferred_element_type=jnp.float32)
            * score_scale
        )
        return (accum, None)

    accum, _ = lax.scan(
        query_advance,
        accum,
        (
            key_piece.reshape(number, width, D),
            value_piece.reshape(number, width, D),
            key_places.reshape(number, width),
            key_docs.reshape(number, width),
        ),
    )
    log_all, delta_all = (
        lax.all_gather(log_total.T, "blk", axis=0, tiled=True),
        lax.all_gather(delta.T, "blk", axis=0, tiled=True),
    )
    key_zero = jnp.zeros((rows, HEADS, HEAD_DIM), jnp.float32)
    state = (key_zero, key_zero)
    begin = jnp.int32(0)
    query_piece = lax.all_gather(query, "blk", axis=0, tiled=True)
    grad_piece = lax.all_gather(attended_grad, "blk", axis=0, tiled=True)
    count = query_piece.shape[0]
    number, width = block_shape(count, rows)
    piece_places = places_of(span_order, begin, count, half_rows)
    piece_docs = documents_of(piece_places, own_lengths, offsets)
    piece_log = lax.dynamic_slice_in_dim(log_all, begin, count, 0)
    piece_delta = lax.dynamic_slice_in_dim(delta_all, begin, count, 0)

    def key_advance(state, parts):
        query_block, grad_block, places_block, docs_block, log_block, delta_block = parts
        key_sum, value_sum = state
        block_query = heads_of(query_block)
        block_grad = heads_of(grad_block)
        scores = (
            jnp.einsum("qhd,khd->hqk", block_query, key_heads, preferred_element_type=jnp.float32)
            * score_scale
        )
        allowed = allowed_of(places_block, docs_block, query_places, query_docs)
        chance = jnp.where(
            allowed,
            jnp.exp(jnp.where(allowed, scores, masked_value) - log_block.T[:, :, None]),
            0.0,
        )
        value_sum = value_sum + jnp.einsum(
            "hqk,qhd->khd",
            chance.astype(jnp.bfloat16),
            block_grad,
            preferred_element_type=jnp.float32,
        )
        push = jnp.einsum(
            "qhd,khd->hqk", block_grad, value_heads, preferred_element_type=jnp.float32
        )
        slope = (chance * (push - delta_block.T[:, :, None])).astype(jnp.bfloat16)
        key_sum = (
            key_sum
            + jnp.einsum("hqk,qhd->khd", slope, block_query, preferred_element_type=jnp.float32)
            * score_scale
        )
        return ((key_sum, value_sum), None)

    state, _ = lax.scan(
        key_advance,
        state,
        (
            query_piece.reshape(number, width, D),
            grad_piece.reshape(number, width, D),
            piece_places.reshape(number, width),
            piece_docs.reshape(number, width),
            piece_log.reshape(number, width, HEADS),
            piece_delta.reshape(number, width, HEADS),
        ),
    )
    key_sum, value_sum = state
    query_low = accum.reshape(rows, D).astype(jnp.bfloat16)
    key_low = key_sum.reshape(rows, D).astype(jnp.bfloat16)
    value_low = value_sum.reshape(rows, D).astype(jnp.bfloat16)
    projected_grad = jnp.concatenate([query_low, key_low, value_low], axis=1)
    input_grad = jnp.einsum(
        "rd,re->de", hidden_in, projected_grad, preferred_element_type=jnp.float32
    )
    query_bias_grad = jnp.sum(query_low.astype(jnp.float32), axis=0)
    value_bias_grad = jnp.sum(value_low.astype(jnp.float32), axis=0)
    hidden_in_grad = jnp.einsum(
        "re,de->rd", projected_grad, input_weight, preferred_element_type=jnp.float32
    )
    resid_part, first_gain_grad = first_back(hidden_in_grad)
    residual_grad = (middle_grad + resid_part).astype(jnp.bfloat16)
    input_part, output_part, up_part, down_part = (
        lax.psum_scatter(input_grad, ("bucket", "blk"), scatter_dimension=0, tiled=True),
        lax.psum_scatter(output_grad, ("bucket", "blk"), scatter_dimension=0, tiled=True),
        lax.psum_scatter(up_grad, ("bucket", "blk"), scatter_dimension=0, tiled=True),
        lax.psum_scatter(down_grad, ("bucket", "blk"), scatter_dimension=0, tiled=True),
    )
    (
        first_sum,
        query_sum_bias,
        value_sum_bias,
        output_sum_bias,
        second_sum,
        up_sum_bias,
        down_sum_bias,
    ) = lax.psum(
        (
            first_gain_grad,
            query_bias_grad,
            value_bias_grad,
            output_bias_grad,
            second_gain_grad,
            up_bias_grad,
            down_bias_grad,
        ),
        ("bucket", "blk"),
    )
    mean_norms = stat_sums / valid_count
    return (
        residual_out,
        residual_grad,
        first_sum,
        input_part,
        query_sum_bias,
        value_sum_bias,
        output_part,
        output_sum_bias,
        second_sum,
        up_part,
        up_sum_bias,
        down_part,
        down_sum_bias,
        mean_norms,
    )


DC = 767
SPLIT = 192
FF = 3072
low = jnp.bfloat16
wide = jnp.float32
VMEM=pl.BlockSpec(memory_space=pltpu.VMEM); SMEM=pl.BlockSpec(memory_space=pltpu.SMEM)

def call(kernel, outs, ins, scratch=(), flops=1_000_000, name=None):
    shapes=[jax.ShapeDtypeStruct(s,d) for s,d in outs]
    return pl.pallas_call(kernel, out_shape=shapes, in_specs=[SMEM]+[VMEM]*(len(ins)-1), out_specs=[VMEM]*len(outs), scratch_shapes=list(scratch),
      compiler_params=pltpu.CompilerParams(vmem_limit_bytes=60*1024*1024), name=name,
      cost_estimate=pl.CostEstimate(flops=flops,bytes_accessed=sum(x.size*x.dtype.itemsize for x in ins),transcendentals=0))(*ins)

def full_of(x):
    rows=x.shape[0]
    wide_x=jnp.concatenate([x,jnp.zeros((rows,1),x.dtype)],axis=1)
    last=lax.broadcasted_iota(jnp.int32,(rows,D),1)==D-1
    return jnp.where(last,-jnp.sum(x,axis=1,keepdims=True),wide_x)

def entry_kernel(ids,resid,cot,gain,weight,qbias,vbias,s0,s1,s2,s3,pair,root_out,buf):
    me=ids[0]
    full=full_of(resid[...].astype(wide))
    root=jnp.sqrt(jnp.mean(full*full,axis=1,keepdims=True)+epsilon)
    root_out[...]=root
    hidden=(full/root*gain[...]).astype(low)
    pair[:160,:]=hidden
    pair[160:,:]=jnp.concatenate([cot[...].astype(wide),jnp.zeros((160,1),wide)],axis=1).astype(low)
    for i in range(3):
        p=jnp.dot(hidden,weight[:,i*D:(i+1)*D],preferred_element_type=wide)
        if i==0: p=(p+qbias[...])*0.125
        if i==2: p=p+vbias[...]
        for j in range(4):
            piece=p[:,j*SPLIT:(j+1)*SPLIT]
            buf[j^me,i*80:(i+1)*80,:]=jnp.concatenate([piece[:80],piece[80:]],axis=1).astype(low)
    for r,s in enumerate((s0,s1,s2,s3)):
        s[...]=buf[r]

def nt(a,b): return lax.dot_general(a,b,(((1,),(1,)),((),())),preferred_element_type=wide)
def tn(a,b): return lax.dot_general(a,b,(((0,),(0,)),((),())),preferred_element_type=wide)

def push_kernel(ids,cot,weight,out):
    for i in range(4):
        out[:,i*D:(i+1)*D]=nt(cot[...],weight[i*D:(i+1)*D,:])

def assemble_kernel(ids,p0,p1,p2,p3,query,both):
    for r,p in enumerate((p0,p1,p2,p3)):
        for i in range(3):
            piece=p[i*80:(i+1)*80,:].astype(wide)
            two=jnp.concatenate([piece[:,:SPLIT],piece[:,SPLIT:]],axis=0).astype(low)
            rows=slice(r*160,(r+1)*160)
            if i==0: query[rows,:]=two
            elif i==1: both[rows,:SPLIT]=two
            else: both[rows,SPLIT:]=two

def head_mask(x,h):
    lane=lax.broadcasted_iota(jnp.int32,x.shape,1)
    return jnp.where((lane>=h*64)&(lane<(h+1)*64),x,jnp.zeros_like(x))

def span_of(ids,chip,core,half):
    return ids[8+chip*4+core*2+half]

def limits(ids,chip,core,half):
    place=span_of(ids,chip,core,half)*80+lax.broadcasted_iota(jnp.int32,(80,1),0)
    first=(place>=ids[3])&(place<ids[5])
    second=(place>=ids[4])&(place<ids[6])
    return jnp.where(first,ids[3],ids[4]),jnp.where(first|second,place,-1)

def forward_kernel(ids,query,own,sib,chance,attended,mixed,b0,b1,b2,b3,keys,vals):
    keys[:640,:]=own[:,:SPLIT]
    keys[640:,:]=sib[:,:SPLIT]
    v=jnp.concatenate([own[:,SPLIT:].astype(wide),sib[:,SPLIT:].astype(wide)],axis=0)
    for h in range(3): vals[h]=head_mask(v,h).astype(low)
    me=ids[0]; core=ids[2]
    lane=lax.broadcasted_iota(jnp.int32,(1,1280),1)
    place=lane
    for blk in range(16):
        chip=(blk%8)//2^me
        other=core^(blk//8)
        place=jnp.where((lane>=blk*80)&(lane<(blk+1)*80),lane+(span_of(ids,chip,other,blk%2)-blk)*80,place)
    for r,b in enumerate((b0,b1,b2,b3)):
        rows=slice(r*160,(r+1)*160)
        q=query[rows,:].astype(wide)
        l0,h0=limits(ids,r^me,core,0)
        l1,h1=limits(ids,r^me,core,1)
        lo=jnp.concatenate([l0,l1],axis=0); hi=jnp.concatenate([h0,h1],axis=0)
        allowed=(place>=lo)&(place<=hi)
        acc=jnp.zeros((160,SPLIT),wide)
        for h in range(3):
            s=nt(head_mask(q,h).astype(low),keys[...])
            s=jnp.where(allowed,s,-1e30)
            peak=jnp.max(s,axis=1,keepdims=True)
            w=jnp.exp(s-peak)
            total=jnp.sum(w,axis=1,keepdims=True)
            p=(w*jnp.where(hi>=0,1.0/total,0.0)).astype(low)
            chance[h,rows,:]=p
            acc=acc+jnp.dot(p,vals[h],preferred_element_type=wide)
        attended[rows,:]=acc
        mixed[rows,:]=acc.astype(low)
        b[...]=jnp.concatenate([acc[:80],acc[80:]],axis=1).astype(low)

def middle_kernel(ids,p0,p1,p2,p3,out_weight,out_bias,resid,root_in,cot,gain,up_weight,up_bias,push,
                  m0,m1,m2,m3,active,branch_own,middle,middle_grad,vector,buf):
    me=ids[0]
    branch=out_bias[...]
    for r,p in enumerate((p0,p1,p2,p3)):
        piece=p[...].astype(wide)
        two=jnp.concatenate([piece[:,:SPLIT],piece[:,SPLIT:]],axis=0).astype(low)
        w=out_weight[pl.ds(pl.multiple_of((me^r)*SPLIT,SPLIT),SPLIT),:]
        branch=branch+jnp.dot(two,w,preferred_element_type=wide)
    mid=resid[...].astype(wide)+branch
    middle[...]=mid
    full=full_of(mid)
    root=jnp.sqrt(jnp.mean(full*full,axis=1,keepdims=True)+epsilon)
    n=full/root
    hidden=(n*gain[...]).astype(low)
    for r in range(4): buf[r,0:160,:]=hidden
    e=jnp.zeros((160,D),wide)
    c=0.7978845608028654
    up_sums=[]
    for blk in range(4):
        cols=slice(blk*D,(blk+1)*D)
        u=jnp.dot(hidden,up_weight[:,cols],preferred_element_type=wide)+up_bias[:,cols]
        t=jnp.tanh(c*(u+0.044715*u*u*u))
        act=0.5*u*(1.0+t)
        slope=0.5*(1.0+t)+0.5*u*(1.0-t*t)*(c*(1.0+3*0.044715*u*u))
        active[:,cols]=act.astype(low)
        for j in range(4):
            buf[j^me,160:320,blk*SPLIT:(blk+1)*SPLIT]=act[:,j*SPLIT:(j+1)*SPLIT].astype(low)
        g=(push[:,cols]*slope).astype(low)
        buf[blk^me,320:480,:]=g
        up_sums.append(jnp.sum(g.astype(wide),axis=0,keepdims=True))
        e=e+nt(g,up_weight[:,cols])
    for r,m in enumerate((m0,m1,m2,m3)): m[...]=buf[r]
    gain_sum=jnp.sum(e*n,axis=0,keepdims=True)
    eg=e*gain[...]
    f=(eg-n*jnp.mean(eg*n,axis=1,keepdims=True))/root
    cot_wide=jnp.concatenate([cot[...].astype(wide),jnp.zeros((160,1),wide)],axis=1)
    lane=lax.broadcasted_iota(jnp.int32,(160,D),1)
    last=jnp.sum(jnp.where(lane==D-1,f,0.0),axis=1,keepdims=True)
    grad=jnp.where(lane==D-1,0.0,cot_wide+f-last)
    middle_grad[...]=grad
    grad_low=grad.astype(low)
    branch_own[...]=grad_low
    ends=[limits(ids,me,ids[2],half)[1] for half in range(2)]
    valid=jnp.where(jnp.concatenate(ends,axis=0)>=0,1.0,0.0)
    one=jnp.sum(valid*root_in[...],axis=0,keepdims=True)
    two=jnp.sum(valid*root,axis=0,keepdims=True)
    row=lax.broadcasted_iota(jnp.int32,(1,D),1)
    stats=jnp.where(row==0,one,jnp.where(row==1,two,0.0))
    zero=jnp.zeros((1,D),wide)
    vector[...]=jnp.concatenate([zero,zero,zero,jnp.sum(grad_low.astype(wide),axis=0,keepdims=True),gain_sum]+up_sums+
       [jnp.sum(cot_wide,axis=0,keepdims=True),stats]+[zero]*5,axis=0)

def closing_kernel(ids,active,weight,middle,bias,out):
    acc=middle[...]+bias[...]
    for i in range(4):
        acc=acc+jnp.dot(active[:,i*D:(i+1)*D],weight[i*D:(i+1)*D,:],preferred_element_type=wide)
    out[...]=acc.astype(low)

def backward_kernel(ids,b0,b1,b2,b3,out_weight,query,own,sib,chance,attended,query_grad,both_grad,away,keys,vals,grads,slopes):
    me=ids[0]
    w=out_weight[pl.ds(pl.multiple_of(me*SPLIT,SPLIT),SPLIT),:].astype(wide)
    w=jnp.concatenate([w,jnp.zeros((SPLIT,1),wide)],axis=1).astype(low)
    for r,b in enumerate((b0,b1,b2,b3)):
        grads[r*160:(r+1)*160,:]=nt(b[...],w).astype(low)
    k=jnp.concatenate([own[:,:SPLIT],sib[:,:SPLIT]],axis=0).astype(wide)
    for h in range(3): keys[h]=head_mask(k,h).astype(low)
    vals[:640,:]=own[:,SPLIT:].astype(wide).astype(low)
    vals[640:,:]=sib[:,SPLIT:].astype(wide).astype(low)
    dq=jnp.zeros((640,SPLIT),wide)
    dk=jnp.zeros((1280,SPLIT),wide)
    dv=jnp.zeros((1280,SPLIT),wide)
    g=grads[...].astype(wide)
    q=query[...].astype(wide)
    for h in range(3):
        gh=head_mask(g,h)
        gl=gh.astype(low)
        delta=jnp.sum(gh*attended[...],axis=1,keepdims=True)
        for r in range(4):
            rows=slice(r*160,(r+1)*160)
            push=nt(gl[rows,:],vals[...])
            slopes[rows,:]=(chance[h,rows,:].astype(wide)*(push-delta[rows,:])).astype(low)
        dq=dq+jnp.dot(slopes[...],keys[h],preferred_element_type=wide)
        dk=dk+tn(slopes[...],head_mask(q,h).astype(low))
        dv=dv+tn(chance[h],gl)
    query_grad[...]=(dq*0.125).astype(low)
    both_grad[:,:SPLIT]=dk[:640]
    both_grad[:,SPLIT:]=dv[:640]
    away[:,:SPLIT]=dk[640:].astype(low)
    away[:,SPLIT:]=dv[640:].astype(low)

def split_pair(x):
    hi=x.astype(low)
    return hi,(x-hi.astype(wide)).astype(low)

def input_grad_kernel(ids,query_grad,both_grad,arrived,p0,p1,p2,p3,weight,gain,vector,
                      h0,h1,h2,h3,keep,send,hidden,heads,buf):
    me=ids[0]; bucket=ids[1]; core=ids[2]
    both=both_grad[...]+arrived[...].astype(wide)
    parts=[query_grad[...].astype(wide),both[:,:SPLIT],both[:,SPLIT:]]
    parts=[p.astype(low).astype(wide) for p in parts]
    for r,(p,h) in enumerate(zip((p0,p1,p2,p3),(h0,h1,h2,h3))):
        hidden[r*160:(r+1)*160,:]=p[:160,:]
        for i in range(3):
            piece=parts[i][r*160:(r+1)*160]
            h[i*80:(i+1)*80,:]=jnp.concatenate([piece[:80],piece[80:]],axis=1).astype(low)
    heads[...]=jnp.concatenate(parts,axis=1).astype(low)
    grad=tn(hidden[...],heads[...])
    parts_grad=[grad[:,i*SPLIT:(i+1)*SPLIT] for i in range(3)]
    product=jnp.zeros((D,SPLIT),wide)
    for i in range(3):
        w=jnp.zeros((D,SPLIT),wide)
        for j in range(4):
            w=jnp.where(me==j,weight[:,i*D+j*SPLIT:i*D+(j+1)*SPLIT].astype(wide),w)
        product=product+w*parts_grad[i]
    gain_row=lax.dot_general(jnp.ones((8,SPLIT),wide),product,(((1,),(1,)),((),())),precision=lax.Precision.HIGHEST,preferred_element_type=wide)[0:1]/gain[...]
    lane=lax.broadcasted_iota(jnp.int32,(1,D),1)
    mine=(lane>=me*SPLIT)&(lane<(me+1)*SPLIT)
    def column_sum(x):
        s=jnp.sum(x,axis=0,keepdims=True)
        return jnp.where(mine,jnp.concatenate([s]*4,axis=1),0.0)
    total=vector[...]
    row=lax.broadcasted_iota(jnp.int32,(16,D),0)
    total=total+jnp.where(row==0,gain_row,0.0)+jnp.where(row==1,column_sum(parts[0]),0.0)+jnp.where(row==2,column_sum(parts[2]),0.0)
    for b in range(4):
        for c in range(2):
            block=jnp.concatenate([jnp.concatenate([parts_grad[i][b*192+j*48+c*24:b*192+j*48+c*24+24] for j in range(4)],axis=1) for i in range(3)]+[jnp.zeros((8,D),wide)],axis=0)
            buf[c^core,(b-bucket)&3]=block.astype(low)
    keep[...]=buf[0]
    hi,lo=split_pair(total)
    for d in range(4): send[d*80:(d+1)*80,:]=buf[1,d]
    send[320:336,:]=hi
    send[336:352,:]=lo

def input_bucket_kernel(ids,keep,send,arrived,z0,z1,z2,z3):
    total=(send[320:336,:].astype(wide)+send[336:352,:].astype(wide))+(arrived[320:336,:].astype(wide)+arrived[336:352,:].astype(wide))
    hi,lo=split_pair(total)
    for d,z in enumerate((z0,z1,z2,z3)):
        z[0:80,:]=(keep[d].astype(wide)+arrived[d*80:(d+1)*80,:].astype(wide)).astype(low)
        z[80:96,:]=hi
        z[96:112,:]=lo

def weight_grad_kernel(ids,m0,m1,m2,m3,p0,p1,p2,p3,b0,b1,b2,b3,mixed,keep,send,left,right,buf):
    bucket=ids[1]; core=ids[2]
    def grad(lefts,rights):
        n=lefts[0].shape[1]
        for r in range(4):
            rows=slice(r*160,(r+1)*160)
            left[rows,:n]=lefts[r]
            right[rows,:]=rights[r]
        return tn(left[:,:n],right[...])
    ms=(m0,m1,m2,m3); ps=(p0,p1,p2,p3); bs=(b0,b1,b2,b3)
    down=grad([m[160:320,:] for m in ms],[p[160:320,:] for p in ps])
    for b in range(4):
        for c in range(2):
            buf[c^core,(b-bucket)&3,0:96,:]=down[b*192+c*96:b*192+(c+1)*96].astype(low)
    up=grad([m[0:160,:] for m in ms],[m[320:480,:] for m in ms])
    for r in range(4): right[r*160:(r+1)*160,:]=bs[r][...]
    out=tn(mixed[...],right[...])
    for b in range(4):
        for c in range(2):
            block=[up[b*192+j*48+c*24:b*192+j*48+c*24+24] for j in range(4)]+[out[b*48+c*24:b*48+c*24+24],jnp.zeros((8,D),wide)]
            buf[c^core,(b-bucket)&3,96:224,:]=jnp.concatenate(block,axis=0).astype(low)
    keep[...]=buf[0]
    send[...]=buf[1]

def bucket_kernel(ids,keep,arrived,z0,z1,z2,z3):
    for d,z in enumerate((z0,z1,z2,z3)):
        z[...]=(keep[d].astype(wide)+arrived[d].astype(wide)).astype(low)

def weight_sum_kernel(ids,z0,z1,z2,z3,down,up,out):
    total=z0[...].astype(wide)+z1[...].astype(wide)+z2[...].astype(wide)+z3[...].astype(wide)
    down[...]=total[0:96,:DC]
    up[...]=total[96:192]
    out[...]=total[192:216]

def final_send_kernel(ids,z0,z1,z2,z3,up,f0,f1,f2,f3,buf,vec):
    me=ids[0]; bucket=ids[1]
    zs=(z0,z1,z2,z3)
    total=sum(z[0:72,:].astype(wide) for z in zs)
    for d,z in enumerate(zs):
        vec[(bucket-d)&3]=z[80:96,:].astype(wide)+z[96:112,:].astype(wide)
    hi,lo=split_pair(vec[0]+vec[1]+vec[2]+vec[3])
    pad8=jnp.zeros((8,D),wide); padl=jnp.zeros((24,D-3*SPLIT),wide)
    for j in range(4):
        ins=jnp.concatenate([total[i*24:(i+1)*24,j*SPLIT:(j+1)*SPLIT] for i in range(3)]+[padl],axis=1)
        block=jnp.concatenate([up[j*24:(j+1)*24,:],pad8,ins,pad8],axis=0)
        buf[j^me]=block.astype(low)
    for r,f in enumerate((f0,f1,f2,f3)):
        f[0:16,:]=hi
        f[16:32,:]=lo
        f[32:96,:]=buf[r]

def final_kernel(ids,f0,f1,f2,f3,in_total,up_total,first,query,value,output,second,up_bias,down,stats,buf):
    me=ids[0]
    for r,f in enumerate((f0,f1,f2,f3)):
        buf[r^me]=f[...].astype(wide)
    total=buf[0,0:16]+buf[0,16:32]
    for j in (1,2,3): total=total+(buf[j,0:16]+buf[j,16:32])
    first[...]=total[0]
    query[...]=total[1]
    value[...]=total[2]
    output[...]=total[3,:DC]
    second[...]=total[4]
    for i in range(4): up_bias[i*D:(i+1)*D]=total[5+i]
    down[...]=total[9,:DC]
    stats[...]=total[10,:2]/ids[7].astype(wide)
    for j in range(4): up_total[:,j*D:(j+1)*D]=buf[j,32:56,:]
    for i in range(3):
        in_total[:,i*D:(i+1)*D]=jnp.concatenate([buf[j,64:88,i*SPLIT:(i+1)*SPLIT] for j in range(4)],axis=1)

def home_kernel(ids,h0,h1,h2,h3,weight,resid,gain,middle_grad,out,buf):
    me=ids[0]
    for r,h in enumerate((h0,h1,h2,h3)): buf[r^me]=h[...]
    e=jnp.zeros((160,D),wide)
    for i in range(3):
        cols=[]
        for j in range(4):
            piece=buf[j,i*80:(i+1)*80,:].astype(wide)
            cols.append(jnp.concatenate([piece[:,:SPLIT],piece[:,SPLIT:]],axis=0))
        g=jnp.concatenate(cols,axis=1).astype(low)
        e=e+nt(g,weight[:,i*D:(i+1)*D])
    full=full_of(resid[...].astype(wide))
    root=jnp.sqrt(jnp.mean(full*full,axis=1,keepdims=True)+epsilon)
    n=full/root
    eg=e*gain[...]
    f=(eg-n*jnp.mean(eg*n,axis=1,keepdims=True))/root
    lane=lax.broadcasted_iota(jnp.int32,(160,D),1)
    last=jnp.sum(jnp.where(lane==D-1,f,0.0),axis=1,keepdims=True)
    out[...]=(middle_grad[...]+f-last)[:,:DC].astype(low)

def swap_chip(block, step):
    return lax.ppermute(block, "blk", [(k, k ^ (2 * step)) for k in range(8)])


def swap_core(block):
    return lax.ppermute(block, "blk", [(k, k ^ 1) for k in range(8)])


def shift_bucket(block, step):
    return lax.ppermute(block, "bucket", [(b, (b + step) % 4) for b in range(4)])


def exchange(blocks):
    got = {r: swap_chip(blocks[r], r) for r in (3, 1, 2)}
    return [blocks[0], got[1], got[2], got[3]]


def over_buckets(blocks):
    return [blocks[0]] + [shift_bucket(blocks[d], d) for d in (1, 2, 3)]


def body(
    residual_in,
    out_cotangent,
    first_gain,
    input_weight,
    query_bias,
    value_bias,
    output_weight,
    output_bias,
    second_gain,
    up_weight,
    up_bias,
    down_weight,
    down_bias,
    lengths,
    offsets,
    span_order,
):
    index = lax.axis_index("blk")
    bucket = lax.axis_index("bucket")
    own_lengths = lax.dynamic_slice_in_dim(lengths, bucket, 1, 0)[0]
    starts = offsets[0]
    scalars = [index // 2, bucket, index % 2, starts[0], starts[1]]
    scalars += [starts[0] + own_lengths[0], starts[1] + own_lengths[1], jnp.sum(lengths)]
    ids = jnp.concatenate([jnp.stack(scalars).astype(jnp.int32), span_order, jnp.zeros((8,), jnp.int32)])
    gain_one = first_gain[None]
    gain_two = second_gain[None]

    packed = ((240, 384), low)
    s0, s1, s2, s3, pair, root_one = call(
        entry_kernel,
        [packed] * 4 + [((320, D), low), ((160, 1), wide)],
        [ids, residual_in, out_cotangent, gain_one, input_weight, query_bias[None], value_bias[None]],
        [pltpu.VMEM((4, 240, 384), low)],
        flops=2 * 160 * D * 3 * D,
    )
    got = exchange([s0, s1, s2, s3])
    (push,) = call(
        push_kernel, [((160, FF), wide)], [ids, out_cotangent, down_weight], flops=2 * 160 * D * FF
    )
    query, own_both = call(assemble_kernel, [((640, SPLIT), low), ((640, 2 * SPLIT), low)], [ids] + got)
    sib_both = swap_core(own_both)
    pairs = exchange([pair] * 4)
    backed = ((80, 384), low)
    chance, attended, mixed, b0, b1, b2, b3 = call(
        forward_kernel,
        [((3, 640, 1280), low), ((640, SPLIT), wide), ((640, SPLIT), low)] + [backed] * 4,
        [ids, query, own_both, sib_both],
        [pltpu.VMEM((1280, SPLIT), low), pltpu.VMEM((3, 1280, SPLIT), low)],
        flops=4 * 12 * 160 * 1280 * 256,
    )
    back = exchange([b0, b1, b2, b3])
    late = ((480, D), low)
    m0, m1, m2, m3, active, branch_own, middle, middle_grad, vector = call(
        middle_kernel,
        [late] * 4
        + [((160, FF), low), ((160, D), low), ((160, DC), wide), ((160, D), wide), ((16, D), wide)],
        [ids]
        + back
        + [output_weight, output_bias[None], residual_in, root_one, out_cotangent, gain_two]
        + [up_weight, up_bias[None], push],
        [pltpu.VMEM((4, 480, D), low)],
        flops=2 * 160 * D * (D + 2 * FF),
    )
    branches = exchange([branch_own] * 4)
    lates = exchange([m0, m1, m2, m3])
    (residual_out,) = call(
        closing_kernel,
        [((160, DC), low)],
        [ids, active, down_weight, middle, down_bias[None]],
        flops=2 * 160 * D * FF,
    )
    query_grad, both_grad, away = call(
        backward_kernel,
        [((640, SPLIT), low), ((640, 2 * SPLIT), wide), ((640, 2 * SPLIT), low)],
        [ids] + branches + [output_weight, query, own_both, sib_both, chance, attended],
        [
            pltpu.VMEM((3, 1280, SPLIT), low),
            pltpu.VMEM((1280, SPLIT), low),
            pltpu.VMEM((640, SPLIT), low),
            pltpu.VMEM((640, 1280), low),
        ],
        flops=10 * 12 * 160 * 1280 * 256,
    )
    arrived = swap_core(away)
    h0, h1, h2, h3, in_keep, in_send = call(
        input_grad_kernel,
        [packed] * 4 + [((4, 80, D), low), ((352, D), low)],
        [ids, query_grad, both_grad, arrived] + pairs + [input_weight, gain_one, vector],
        [
            pltpu.VMEM((640, D), low),
            pltpu.VMEM((640, 3 * SPLIT), low),
            pltpu.VMEM((2, 4, 80, D), low),
        ],
        flops=2 * 640 * D * 3 * SPLIT,
    )
    home = exchange([h0, h1, h2, h3])
    keep, send = call(
        weight_grad_kernel,
        [((4, 224, D), low)] * 2,
        [ids] + lates + pairs + branches + [mixed],
        [pltpu.VMEM((640, D), low), pltpu.VMEM((640, D), low), pltpu.VMEM((2, 4, 224, D), low)],
        flops=2 * 640 * D * (2 * D + SPLIT),
    )
    z = call(bucket_kernel, [((224, D), low)] * 4, [ids, keep, swap_core(send)])
    down_total, up_sum, out_sum = call(
        weight_sum_kernel,
        [((96, DC), wide), ((96, D), wide), ((24, D), wide)],
        [ids] + over_buckets(z),
    )
    turned = [(b * 8 + j * 2 + c, j * 8 + b * 2 + c) for b in range(4) for j in range(4) for c in range(2)]
    out_total = lax.ppermute(out_sum, ("bucket", "blk"), turned)[:, :DC]
    z = call(input_bucket_kernel, [((112, D), low)] * 4, [ids, in_keep, in_send, swap_core(in_send)])
    finals = call(
        final_send_kernel,
        [((96, D), low)] * 4,
        [ids] + over_buckets(z) + [up_sum],
        [pltpu.VMEM((4, 64, D), low), pltpu.VMEM((4, 16, D), wide)],
    )
    in_total, up_total, first, query_sum, value_sum, output, second, up_sum_bias, down, stats = call(
        final_kernel,
        [((24, 3 * D), wide), ((24, FF), wide)]
        + [((D,), wide)] * 3
        + [((DC,), wide), ((D,), wide), ((FF,), wide), ((DC,), wide), ((2,), wide)],
        [ids] + exchange(finals),
        [pltpu.VMEM((4, 96, D), wide)],
    )
    (residual_grad,) = call(
        home_kernel,
        [((160, DC), low)],
        [ids] + home + [input_weight, residual_in, gain_one, middle_grad],
        [pltpu.VMEM((4, 240, 384), low)],
        flops=2 * 160 * D * 3 * D,
    )
    return (
        residual_out,
        residual_grad,
        first,
        in_total,
        query_sum,
        value_sum,
        out_total,
        output,
        second,
        up_total,
        up_sum_bias,
        down_total,
        down,
        stats,
    )


def solution(mesh):
    placed = (
        P(("bucket", "blk"), None),
        P(("bucket", "blk"), None),
        P(),
        P(),
        P(),
        P(),
        P(),
        P(),
        P(),
        P(),
        P(),
        P(),
        P(),
        P(),
        P("bucket", None),
        P(),
    )
    return jax.shard_map(
        body if dict(mesh.shape) == {"bucket": 4, "blk": 8} else general_body,
        mesh=mesh,
        in_specs=placed,
        out_specs=(
            P(("bucket", "blk"), None),
            P(("bucket", "blk"), None),
            P(),
            P(("bucket", "blk"), None),
            P(),
            P(),
            P(("bucket", "blk"), None),
            P(),
            P(),
            P(("bucket", "blk"), None),
            P(),
            P(("bucket", "blk"), None),
            P(),
            P(),
        ),
        check_vma=False,
    )
```

```python
import jax
import jax.numpy as jnp
from jax import lax
from jax.experimental import pallas as pl
from jax.experimental.pallas import tpu as pltpu
from jax.sharding import PartitionSpec as P

D = 768
HEADS = 12
HEAD_DIM = 64


epsilon = 1e-05
masked_value = -1e30


def center_norm(resid, gain):
    full = jnp.concatenate([resid, -jnp.sum(resid, axis=1, keepdims=True)], axis=1)
    root = jnp.sqrt(jnp.mean(full * full, axis=1, keepdims=True) + epsilon)
    return (full / root * gain, root[:, 0])


def gelu_tanh(inputs):
    return jax.nn.gelu(inputs, approximate=True)


def heads_of(block):
    return block.reshape(block.shape[0], HEADS, HEAD_DIM)


def places_of(span_order, begin, count, half_rows):
    spans = lax.dynamic_slice_in_dim(span_order, begin // half_rows, count // half_rows)
    inner = jnp.arange(half_rows, dtype=jnp.int32)
    return (spans[:, None] * half_rows + inner[None, :]).reshape(count)


def documents_of(places, lengths, offsets):
    first_in = (places >= offsets[0, 0]) & (places < offsets[0, 0] + lengths[0, 0])
    second_in = (places >= offsets[0, 1]) & (places < offsets[0, 1] + lengths[0, 1])
    return jnp.where(first_in, 0, jnp.where(second_in, 1, -1)).astype(jnp.int32)


def allowed_of(query_places, query_docs, key_places, key_docs):
    same = (query_docs[:, None] == key_docs[None, :]) & (query_docs[:, None] >= 0)
    return (same & (key_places[None, :] <= query_places[:, None]))[None]


def block_shape(count, unit):
    shards = count // unit
    width = max(1, 1024 // unit)
    while shards % width != 0:
        width = width - 1
    return (shards // width, width * unit)


def general_body(
    residual_in,
    out_cotangent,
    first_gain,
    input_weight,
    query_bias,
    value_bias,
    output_weight,
    output_bias,
    second_gain,
    up_weight,
    up_bias,
    down_weight,
    down_bias,
    lengths,
    offsets,
    span_order,
):
    rows = residual_in.shape[0]
    half_rows = rows // 2
    score_scale = HEAD_DIM ** (-0.5)
    index = lax.axis_index("blk")
    bucket_index = lax.axis_index("bucket")
    own_lengths = lax.dynamic_slice_in_dim(lengths, bucket_index, 1, 0)
    valid_count = jnp.sum(lengths.astype(jnp.float32))
    query_places = places_of(span_order, index * rows, rows, half_rows)
    query_docs = documents_of(query_places, own_lengths, offsets)
    valid = (query_docs >= 0).astype(jnp.float32)
    resid = residual_in.astype(jnp.float32)
    normed, first_back, first_root = jax.vjp(center_norm, resid, first_gain, has_aux=True)
    hidden_in = normed.astype(jnp.bfloat16)
    projected = jnp.dot(hidden_in, input_weight, preferred_element_type=jnp.float32)
    query = (projected[:, :D] + query_bias).astype(jnp.bfloat16)
    keys = projected[:, D : 2 * D].astype(jnp.bfloat16)
    values = (projected[:, 2 * D :] + value_bias).astype(jnp.bfloat16)
    query_heads = heads_of(query)
    key_heads = heads_of(keys)
    value_heads = heads_of(values)
    initial = (
        jnp.full((HEADS, rows), masked_value, jnp.float32),
        jnp.zeros((HEADS, rows), jnp.float32),
        jnp.zeros((HEADS, rows, HEAD_DIM), jnp.float32),
    )
    state = initial
    key_piece = lax.all_gather(keys, "blk", axis=0, tiled=True)
    value_piece = lax.all_gather(values, "blk", axis=0, tiled=True)
    count = key_piece.shape[0]
    number, width = block_shape(count, rows)
    key_places = places_of(span_order, jnp.int32(0), count, half_rows)
    key_docs = documents_of(key_places, own_lengths, offsets)

    def forward_advance(state, parts):
        key_block, value_block, places_block, docs_block = parts
        peak, total, summed = state
        scores = (
            jnp.einsum(
                "qhd,khd->hqk", query_heads, heads_of(key_block), preferred_element_type=jnp.float32
            )
            * score_scale
        )
        allowed = allowed_of(query_places, query_docs, places_block, docs_block)
        masked = jnp.where(allowed, scores, masked_value)
        new_peak = jnp.maximum(peak, jnp.max(masked, axis=2))
        decay = jnp.exp(peak - new_peak)
        weights = jnp.where(allowed, jnp.exp(masked - new_peak[:, :, None]), 0.0)
        total = total * decay + jnp.sum(weights, axis=2)
        summed = summed * decay[:, :, None] + jnp.einsum(
            "hqk,khd->hqd",
            weights.astype(jnp.bfloat16),
            heads_of(value_block),
            preferred_element_type=jnp.float32,
        )
        return ((new_peak, total, summed), None)

    state, _ = lax.scan(
        forward_advance,
        state,
        (
            key_piece.reshape(number, width, D),
            value_piece.reshape(number, width, D),
            key_places.reshape(number, width),
            key_docs.reshape(number, width),
        ),
    )
    peak, total, summed = state
    denominator = total + 1.0 - valid[None, :]
    attended = summed / denominator[:, :, None]
    log_total = peak + jnp.log(denominator)
    mixed = attended.transpose(1, 0, 2).reshape(rows, D).astype(jnp.bfloat16)
    branch = jnp.dot(mixed, output_weight, preferred_element_type=jnp.float32) + output_bias
    middle = resid + branch
    normed_two, second_back, second_root = jax.vjp(center_norm, middle, second_gain, has_aux=True)
    hidden_two = normed_two.astype(jnp.bfloat16)
    upward = jnp.dot(hidden_two, up_weight, preferred_element_type=jnp.float32) + up_bias
    active_float, gelu_back = jax.vjp(gelu_tanh, upward)
    active = active_float.astype(jnp.bfloat16)
    closing = jnp.dot(active, down_weight, preferred_element_type=jnp.float32) + down_bias
    residual_out = (middle + closing).astype(jnp.bfloat16)
    stat_sums = jnp.stack([jnp.sum(valid * first_root), jnp.sum(valid * second_root)])
    stat_sums = lax.psum(stat_sums, ("bucket", "blk"))
    cotangent = out_cotangent.astype(jnp.float32)
    down_grad = jnp.einsum("rf,rc->fc", active, out_cotangent, preferred_element_type=jnp.float32)
    down_bias_grad = jnp.sum(cotangent, axis=0)
    active_grad = jnp.einsum(
        "rc,fc->rf", out_cotangent, down_weight, preferred_element_type=jnp.float32
    )
    (upward_float,) = gelu_back(active_grad)
    upward_grad = upward_float.astype(jnp.bfloat16)
    up_grad = jnp.einsum("rd,rf->df", hidden_two, upward_grad, preferred_element_type=jnp.float32)
    up_bias_grad = jnp.sum(upward_grad.astype(jnp.float32), axis=0)
    hidden_two_grad = jnp.einsum(
        "rf,df->rd", upward_grad, up_weight, preferred_element_type=jnp.float32
    )
    middle_part, second_gain_grad = second_back(hidden_two_grad)
    middle_grad = cotangent + middle_part
    branch_grad = middle_grad.astype(jnp.bfloat16)
    output_grad = jnp.einsum("rd,rc->dc", mixed, branch_grad, preferred_element_type=jnp.float32)
    output_bias_grad = jnp.sum(branch_grad.astype(jnp.float32), axis=0)
    attended_grad = jnp.einsum(
        "rc,dc->rd", branch_grad, output_weight, preferred_element_type=jnp.float32
    ).astype(jnp.bfloat16)
    grad_heads = heads_of(attended_grad)
    delta = jnp.einsum("rhd,hrd->hr", grad_heads.astype(jnp.float32), attended)
    query_zero = jnp.zeros((rows, HEADS, HEAD_DIM), jnp.float32)
    accum = query_zero
    key_piece = lax.all_gather(keys, "blk", axis=0, tiled=True)
    value_piece = lax.all_gather(values, "blk", axis=0, tiled=True)
    count = key_piece.shape[0]
    number, width = block_shape(count, rows)
    key_places = places_of(span_order, jnp.int32(0), count, half_rows)
    key_docs = documents_of(key_places, own_lengths, offsets)

    def query_advance(accum, parts):
        key_block, value_block, places_block, docs_block = parts
        block_keys = heads_of(key_block)
        scores = (
            jnp.einsum("qhd,khd->hqk", query_heads, block_keys, preferred_element_type=jnp.float32)
            * score_scale
        )
        allowed = allowed_of(query_places, query_docs, places_block, docs_block)
        chance = jnp.where(
            allowed, jnp.exp(jnp.where(allowed, scores, masked_value) - log_total[:, :, None]), 0.0
        )
        push = jnp.einsum(
            "qhd,khd->hqk", grad_heads, heads_of(value_block), preferred_element_type=jnp.float32
        )
        slope = (chance * (push - delta[:, :, None])).astype(jnp.bfloat16)
        accum = (
            accum
            + jnp.einsum("hqk,khd->qhd", slope, block_keys, preferred_element_type=jnp.float32)
            * score_scale
        )
        return (accum, None)

    accum, _ = lax.scan(
        query_advance,
        accum,
        (
            key_piece.reshape(number, width, D),
            value_piece.reshape(number, width, D),
            key_places.reshape(number, width),
            key_docs.reshape(number, width),
        ),
    )
    log_all, delta_all = (
        lax.all_gather(log_total.T, "blk", axis=0, tiled=True),
        lax.all_gather(delta.T, "blk", axis=0, tiled=True),
    )
    key_zero = jnp.zeros((rows, HEADS, HEAD_DIM), jnp.float32)
    state = (key_zero, key_zero)
    begin = jnp.int32(0)
    query_piece = lax.all_gather(query, "blk", axis=0, tiled=True)
    grad_piece = lax.all_gather(attended_grad, "blk", axis=0, tiled=True)
    count = query_piece.shape[0]
    number, width = block_shape(count, rows)
    piece_places = places_of(span_order, begin, count, half_rows)
    piece_docs = documents_of(piece_places, own_lengths, offsets)
    piece_log = lax.dynamic_slice_in_dim(log_all, begin, count, 0)
    piece_delta = lax.dynamic_slice_in_dim(delta_all, begin, count, 0)

    def key_advance(state, parts):
        query_block, grad_block, places_block, docs_block, log_block, delta_block = parts
        key_sum, value_sum = state
        block_query = heads_of(query_block)
        block_grad = heads_of(grad_block)
        scores = (
            jnp.einsum("qhd,khd->hqk", block_query, key_heads, preferred_element_type=jnp.float32)
            * score_scale
        )
        allowed = allowed_of(places_block, docs_block, query_places, query_docs)
        chance = jnp.where(
            allowed,
            jnp.exp(jnp.where(allowed, scores, masked_value) - log_block.T[:, :, None]),
            0.0,
        )
        value_sum = value_sum + jnp.einsum(
            "hqk,qhd->khd",
            chance.astype(jnp.bfloat16),
            block_grad,
            preferred_element_type=jnp.float32,
        )
        push = jnp.einsum(
            "qhd,khd->hqk", block_grad, value_heads, preferred_element_type=jnp.float32
        )
        slope = (chance * (push - delta_block.T[:, :, None])).astype(jnp.bfloat16)
        key_sum = (
            key_sum
            + jnp.einsum("hqk,qhd->khd", slope, block_query, preferred_element_type=jnp.float32)
            * score_scale
        )
        return ((key_sum, value_sum), None)

    state, _ = lax.scan(
        key_advance,
        state,
        (
            query_piece.reshape(number, width, D),
            grad_piece.reshape(number, width, D),
            piece_places.reshape(number, width),
            piece_docs.reshape(number, width),
            piece_log.reshape(number, width, HEADS),
            piece_delta.reshape(number, width, HEADS),
        ),
    )
    key_sum, value_sum = state
    query_low = accum.reshape(rows, D).astype(jnp.bfloat16)
    key_low = key_sum.reshape(rows, D).astype(jnp.bfloat16)
    value_low = value_sum.reshape(rows, D).astype(jnp.bfloat16)
    projected_grad = jnp.concatenate([query_low, key_low, value_low], axis=1)
    input_grad = jnp.einsum(
        "rd,re->de", hidden_in, projected_grad, preferred_element_type=jnp.float32
    )
    query_bias_grad = jnp.sum(query_low.astype(jnp.float32), axis=0)
    value_bias_grad = jnp.sum(value_low.astype(jnp.float32), axis=0)
    hidden_in_grad = jnp.einsum(
        "re,de->rd", projected_grad, input_weight, preferred_element_type=jnp.float32
    )
    resid_part, first_gain_grad = first_back(hidden_in_grad)
    residual_grad = (middle_grad + resid_part).astype(jnp.bfloat16)
    input_part, output_part, up_part, down_part = (
        lax.psum_scatter(input_grad, ("bucket", "blk"), scatter_dimension=0, tiled=True),
        lax.psum_scatter(output_grad, ("bucket", "blk"), scatter_dimension=0, tiled=True),
        lax.psum_scatter(up_grad, ("bucket", "blk"), scatter_dimension=0, tiled=True),
        lax.psum_scatter(down_grad, ("bucket", "blk"), scatter_dimension=0, tiled=True),
    )
    (
        first_sum,
        query_sum_bias,
        value_sum_bias,
        output_sum_bias,
        second_sum,
        up_sum_bias,
        down_sum_bias,
    ) = lax.psum(
        (
            first_gain_grad,
            query_bias_grad,
            value_bias_grad,
            output_bias_grad,
            second_gain_grad,
            up_bias_grad,
            down_bias_grad,
        ),
        ("bucket", "blk"),
    )
    mean_norms = stat_sums / valid_count
    return (
        residual_out,
        residual_grad,
        first_sum,
        input_part,
        query_sum_bias,
        value_sum_bias,
        output_part,
        output_sum_bias,
        second_sum,
        up_part,
        up_sum_bias,
        down_part,
        down_sum_bias,
        mean_norms,
    )


DC = 767
SPLIT = 192
FF = 3072
low = jnp.bfloat16
wide = jnp.float32
VMEM = pl.BlockSpec(memory_space=pltpu.VMEM)
SMEM = pl.BlockSpec(memory_space=pltpu.SMEM)

def padded_bytes(shape, dtype):
    shape = (1, 1) + tuple(shape)
    size = jnp.dtype(dtype).itemsize
    rows, lanes = -(-shape[-2] // 16) * 16, -(-shape[-1] // 128) * 128
    for d in shape[:-2]:
        rows = rows * d
    return rows * lanes * size


def call(kernel, outs, ins, scratch=(), extra=8, small=0):
    shapes = [jax.ShapeDtypeStruct(s, d) for s, d in outs]
    held = [(s, d) for s, d in outs] + [(x.shape, x.dtype) for x in ins[small:]]
    held += [(s.shape, s.dtype) for s in scratch]
    limit = sum(padded_bytes(s, d) for s, d in held) + extra * 1024 * 1024
    return pl.pallas_call(
        kernel,
        out_shape=shapes,
        in_specs=[SMEM] * small + [VMEM] * (len(ins) - small),
        out_specs=[VMEM] * len(outs),
        scratch_shapes=list(scratch),
        compiler_params=pltpu.CompilerParams(vmem_limit_bytes=min(limit, 60 * 1024 * 1024)),
        cost_estimate=pl.CostEstimate(
            flops=1000,
            bytes_accessed=1000,
            transcendentals=0,
        ),
    )(*ins)


def here():
    index = lax.axis_index("blk")
    return index // 2, lax.axis_index("bucket"), index % 2


def full_of(x):
    rows=x.shape[0]
    wide_x=jnp.concatenate([x,jnp.zeros((rows,1),x.dtype)],axis=1)
    last=lax.broadcasted_iota(jnp.int32,(rows,D),1)==D-1
    return jnp.where(last,-jnp.sum(x,axis=1,keepdims=True),wide_x)

def row(ref):
    return ref[...].reshape(1, ref.shape[0])


def nt(a, b):
    return lax.dot_general(a, b, (((1,), (1,)), ((), ())), preferred_element_type=wide)


def tn(a, b):
    return lax.dot_general(a, b, (((0,), (0,)), ((), ())), preferred_element_type=wide)


def packed(x):
    half = x.shape[0] // 2
    return jnp.concatenate([x[:half], x[half:]], axis=1).astype(low)


def unpacked(x):
    x = x.astype(wide)
    half = x.shape[1] // 2
    return jnp.concatenate([x[:, :half], x[:, half:]], axis=0)


def split_pair(x):
    hi = x.astype(low)
    return hi, (x - hi.astype(wide)).astype(low)


def head_mask(x, h):
    lane = lax.broadcasted_iota(jnp.int32, x.shape, 1)
    return jnp.where((lane >= h * 64) & (lane < (h + 1) * 64), x, jnp.zeros_like(x))


def limits(spans, offsets, lengths, bucket, chip, core, half):
    place = spans[chip * 4 + core * 2 + half] * 80 + lax.broadcasted_iota(jnp.int32, (80, 1), 0)
    one, two = offsets[0, 0], offsets[0, 1]
    first = (place >= one) & (place < one + lengths[bucket, 0])
    second = (place >= two) & (place < two + lengths[bucket, 1])
    return jnp.where(first, one, two), jnp.where(first | second, place, -1)


def entry_kernel(resid, gain, weight, qbias, vbias, s0, s1, s2, s3, hidden_out, root_out, buf):
    me = here()[0]
    full = full_of(resid[...].astype(wide))
    root = jnp.sqrt(jnp.mean(full * full, axis=1, keepdims=True) + epsilon)
    root_out[...] = root
    hidden = (full / root * row(gain)).astype(low)
    hidden_out[...] = hidden
    for i in range(3):
        p = jnp.dot(hidden, weight[:, i * D : (i + 1) * D], preferred_element_type=wide)
        if i == 0:
            p = (p + row(qbias)) * 0.125
        if i == 2:
            p = p + row(vbias)
        for j in range(4):
            buf[j ^ me, i * 80 : (i + 1) * 80, :] = packed(p[:, j * SPLIT : (j + 1) * SPLIT])
    for r, s in enumerate((s0, s1, s2, s3)):
        s[...] = buf[r]


def push_kernel(cot, weight, out):
    for i in range(4):
        out[:, i * D : (i + 1) * D] = nt(cot[...], weight[i * D : (i + 1) * D, :])


def columns_kernel(weight, out):
    me = here()[0]
    for j in range(4):

        @pl.when(me == j)
        def _():
            for i in range(3):
                piece = weight[:, i * D + j * SPLIT : i * D + (j + 1) * SPLIT].astype(wide)
                out[:, i * SPLIT : (i + 1) * SPLIT] = piece.astype(low)


def assemble_kernel(p0, p1, p2, p3, query, both):
    for r, p in enumerate((p0, p1, p2, p3)):
        rows = slice(r * 160, (r + 1) * 160)
        query[rows, :] = unpacked(p[0:80, :]).astype(low)
        both[rows, :SPLIT] = unpacked(p[80:160, :]).astype(low)
        both[rows, SPLIT:] = unpacked(p[160:240, :]).astype(low)


def forward_kernel(
    spans, offsets, lengths, query, own, sib, chance, attended, b0, b1, b2, b3, keys, vals, scores
):
    me, bucket, core = here()
    keys[:640, :] = own[:, :SPLIT]
    keys[640:, :] = sib[:, :SPLIT]
    v = jnp.concatenate([own[:, SPLIT:].astype(wide), sib[:, SPLIT:].astype(wide)], axis=0)
    for h in range(3):
        vals[h] = head_mask(v, h).astype(low)
    lane = lax.broadcasted_iota(jnp.int32, (1, 1280), 1)
    place = lane
    for blk in range(16):
        chip = ((blk % 8) // 2) ^ me
        span = spans[chip * 4 + (core ^ (blk // 8)) * 2 + blk % 2]
        place = jnp.where((lane >= blk * 80) & (lane < (blk + 1) * 80), lane + (span - blk) * 80, place)
    q = query[...].astype(wide)
    for h in range(3):
        scores[...] = nt(head_mask(q, h).astype(low), keys[...])
        for blk in range(8):
            rows = slice(blk * 80, (blk + 1) * 80)
            lo, hi = limits(spans, offsets, lengths, bucket, (blk // 2) ^ me, core, blk % 2)
            s = jnp.where((place >= lo) & (place <= hi), scores[rows, :], masked_value)
            peak = jnp.max(s, axis=1, keepdims=True)
            w = jnp.exp(s - peak)
            total = jnp.sum(w, axis=1, keepdims=True)
            chance[h, rows, :] = (w * jnp.where(hi >= 0, 1.0 / total, 0.0)).astype(low)
        part = jnp.dot(chance[h], vals[h], preferred_element_type=wide)
        if h == 0:
            attended[...] = part
        else:
            attended[...] += part
    acc = attended[...]
    for r, b in enumerate((b0, b1, b2, b3)):
        b[...] = packed(acc[r * 160 : (r + 1) * 160])


def middle_kernel(
    spans, offsets, lengths, p0, p1, p2, p3, out_weight, out_bias, resid, root_in, cot, gain, up_weight, up_bias, push,
    d0, d1, d2, d3, a0, a1, a2, a3, n0, n1, n2, n3, branch_own, middle, middle_grad, vector, dbuf, abuf, nbuf,
):
    me, bucket, core = here()
    branch = row(out_bias)
    for r, p in enumerate((p0, p1, p2, p3)):
        w = out_weight[pl.ds(pl.multiple_of((me ^ r) * SPLIT, SPLIT), SPLIT), :]
        branch = branch + jnp.dot(unpacked(p[...]).astype(low), w, preferred_element_type=wide)
    mid = resid[...].astype(wide) + branch
    middle[...] = mid
    full = full_of(mid)
    root = jnp.sqrt(jnp.mean(full * full, axis=1, keepdims=True) + epsilon)
    n = full / root
    hidden = (n * row(gain)).astype(low)
    for r in range(4):
        nbuf[r, 0:160, :] = hidden
    e = jnp.zeros((160, D), wide)
    c = 0.7978845608028654
    up_sums = []
    for blk in range(4):
        cols = slice(blk * D, (blk + 1) * D)
        u = jnp.dot(hidden, up_weight[:, cols], preferred_element_type=wide) + up_bias[cols].reshape(1, D)
        t = jnp.tanh(c * (u + 0.044715 * u * u * u))
        abuf[blk ^ bucket] = (0.5 * u * (1.0 + t)).astype(low)
        slope = 0.5 * (1.0 + t) + 0.5 * u * (1.0 - t * t) * (c * (1.0 + 3 * 0.044715 * u * u))
        g = (push[:, cols] * slope).astype(low)
        nbuf[blk ^ me, 160:320, :] = g
        up_sums.append(jnp.sum(g.astype(wide), axis=0, keepdims=True))
        e = e + nt(g, up_weight[:, cols])
    gain_sum = jnp.sum(e * n, axis=0, keepdims=True)
    eg = e * row(gain)
    f = (eg - n * jnp.mean(eg * n, axis=1, keepdims=True)) / root
    cot_wide = jnp.concatenate([cot[...].astype(wide), jnp.zeros((160, 1), wide)], axis=1)
    lane = lax.broadcasted_iota(jnp.int32, (160, D), 1)
    last = jnp.sum(jnp.where(lane == D - 1, f, 0.0), axis=1, keepdims=True)
    grad = jnp.where(lane == D - 1, 0.0, cot_wide + f - last)
    middle_grad[...] = grad
    grad_low = grad.astype(low)
    grad_wide = grad_low.astype(wide)
    branch_own[...] = grad_low
    back = nt(grad_wide[:, :DC].astype(low), out_weight[...])
    for j in range(4):
        dbuf[j ^ me] = packed(back[:, j * SPLIT : (j + 1) * SPLIT])
    for r in range(4):
        (d0, d1, d2, d3)[r][...] = dbuf[r]
        (a0, a1, a2, a3)[r][...] = abuf[r]
        (n0, n1, n2, n3)[r][...] = nbuf[r]
    ends = [limits(spans, offsets, lengths, bucket, me, core, half)[1] for half in range(2)]
    valid = jnp.where(jnp.concatenate(ends, axis=0) >= 0, 1.0, 0.0)
    one = jnp.sum(valid * root_in[...], axis=0, keepdims=True)
    two = jnp.sum(valid * root, axis=0, keepdims=True)
    at = lax.broadcasted_iota(jnp.int32, (1, D), 1)
    stats = jnp.where(at == 0, one, jnp.where(at == 1, two, 0.0))
    zero = jnp.zeros((1, D), wide)
    sums = [zero, zero, zero, jnp.sum(grad_wide, axis=0, keepdims=True), gain_sum] + up_sums
    sums += [jnp.sum(cot_wide, axis=0, keepdims=True), stats] + [zero] * 5
    vector[...] = jnp.concatenate(sums, axis=0)


def closing_kernel(a0, a1, a2, a3, weight, middle, bias, out):
    bucket = here()[1]
    acc = middle[...] + row(bias)
    for d, a in enumerate((a0, a1, a2, a3)):
        w = weight[pl.ds(pl.multiple_of((bucket ^ d) * D, D), D), :]
        acc = acc + jnp.dot(a[...], w, preferred_element_type=wide)
    out[...] = acc.astype(low)


def backward_kernel(
    d0, d1, d2, d3, query, own, sib, chance, attended, query_grad, both_grad, away_one, away_two, keys, vals, grads, slopes
):
    for r, d in enumerate((d0, d1, d2, d3)):
        grads[r * 160 : (r + 1) * 160, :] = unpacked(d[...]).astype(low)
    k = jnp.concatenate([own[:, :SPLIT], sib[:, :SPLIT]], axis=0).astype(wide)
    for h in range(3):
        keys[h] = head_mask(k, h).astype(low)
    vals[:640, :] = own[:, SPLIT:].astype(wide).astype(low)
    vals[640:, :] = sib[:, SPLIT:].astype(wide).astype(low)
    dq = jnp.zeros((640, SPLIT), wide)
    dk = jnp.zeros((1280, SPLIT), wide)
    dv = jnp.zeros((1280, SPLIT), wide)
    g = grads[...].astype(wide)
    q = query[...].astype(wide)
    for h in range(3):
        gh = head_mask(g, h)
        gl = gh.astype(low)
        delta = jnp.sum(gh * attended[...], axis=1, keepdims=True)
        for r in range(4):
            rows = slice(r * 160, (r + 1) * 160)
            push = nt(gl[rows, :], vals[...])
            slopes[rows, :] = (chance[h, rows, :].astype(wide) * (push - delta[rows, :])).astype(low)
        dq = dq + jnp.dot(slopes[...], keys[h], preferred_element_type=wide)
        dk = dk + tn(slopes[...], head_mask(q, h).astype(low))
        dv = dv + tn(chance[h], gl)
    query_grad[...] = (dq * 0.125).astype(low)
    both_grad[:, :SPLIT] = dk[:640]
    both_grad[:, SPLIT:] = dv[:640]
    away_one[:, :SPLIT] = dk[640:960].astype(low)
    away_one[:, SPLIT:] = dv[640:960].astype(low)
    away_two[:, :SPLIT] = dk[960:].astype(low)
    away_two[:, SPLIT:] = dv[960:].astype(low)


def late_kernel(
    query_grad, both_grad, arrive_one, arrive_two, i0, i1, i2, i3, a0, a1, a2, a3, c0, c1, c2, c3, p0, p1, p2, p3, branch_own, columns, gain, vector,
    h0, h1, h2, h3, keep_x, keep_z, send, left, right, heads, xbuf, zbuf, obuf,
):
    me, bucket, core = here()
    arrived = jnp.concatenate([arrive_one[...].astype(wide), arrive_two[...].astype(wide)], axis=0)
    both = both_grad[...] + arrived
    parts = [query_grad[...].astype(wide), both[:, :SPLIT], both[:, SPLIT:]]
    parts = [p.astype(low).astype(wide) for p in parts]
    for r, h in enumerate((h0, h1, h2, h3)):
        left[r * 160 : (r + 1) * 160, :] = (i0, i1, i2, i3)[r][...]
        for i in range(3):
            h[i * 80 : (i + 1) * 80, :] = packed(parts[i][r * 160 : (r + 1) * 160])
    heads[...] = jnp.concatenate(parts, axis=1).astype(low)
    grad = tn(left[...], heads[...])
    sums = jnp.sum(grad * columns[...].astype(wide), axis=1, keepdims=True)
    gain_row = jnp.transpose(jnp.broadcast_to(sums, (D, 128)))[0:1] / row(gain)
    lane = lax.broadcasted_iota(jnp.int32, (1, D), 1)
    mine = (lane >= me * SPLIT) & (lane < (me + 1) * SPLIT)

    def column_sum(x):
        s = jnp.sum(x, axis=0, keepdims=True)
        return jnp.where(mine, jnp.concatenate([s] * 4, axis=1), 0.0)

    at = lax.broadcasted_iota(jnp.int32, (16, D), 0)
    total = vector[...] + jnp.where(at == 0, gain_row, 0.0)
    total = total + jnp.where(at == 1, column_sum(parts[0]), 0.0)
    total = total + jnp.where(at == 2, column_sum(parts[2]), 0.0)
    thirds = [grad[:, i * SPLIT : (i + 1) * SPLIT] for i in range(3)]
    for b in range(4):
        for c in range(2):
            block = []
            for part in thirds:
                starts = [b * 192 + j * 48 + c * 24 for j in range(4)]
                block.append(jnp.concatenate([part[s : s + 24] for s in starts], axis=1))
            block.append(jnp.zeros((8, D), wide))
            zbuf[c ^ core, b ^ bucket] = jnp.concatenate(block, axis=0).astype(low)
    for d in range(4):
        cot = (c0, c1, c2, c3)[d][...].astype(wide)
        right[d * 160 : (d + 1) * 160, :] = jnp.concatenate([cot, jnp.zeros((160, 1), wide)], axis=1).astype(low)
        left[d * 160 : (d + 1) * 160, :] = (a0, a1, a2, a3)[d][...]
    down = tn(left[...], right[...])
    for j in range(4):
        for c in range(2):
            s = j * 192 + c * 96
            xbuf[c ^ core, j ^ me, 0:96, :] = down[s : s + 96].astype(low)
    for r, p in enumerate((p0, p1, p2, p3)):
        out = tn(unpacked(p[...]).astype(low), branch_own[...])
        for j in range(4):
            for c in range(2):
                s = j * 48 + c * 24
                obuf[c ^ core, j ^ me, me ^ r ^ bucket] = out[s : s + 24]
    for c in range(2):
        for r in range(4):
            xbuf[c, r, 96:192, :] = jnp.concatenate([obuf[c, r, d] for d in range(4)], axis=0).astype(low)
    keep_x[...] = xbuf[0]
    keep_z[...] = zbuf[0]
    for r in range(4):
        send[r * 192 : (r + 1) * 192, :] = xbuf[1, r]
        send[768 + r * 80 : 848 + r * 80, :] = zbuf[1, r]
    hi, lo = split_pair(total)
    send[1088:1104, :] = hi
    send[1104:1120, :] = lo


def late_sum_kernel(keep_x, keep_z, send, arrived, h0, h1, h2, h3, x0, x1, x2, x3, z0, z1, z2, z3):
    own = send[1088:1104, :].astype(wide) + send[1104:1120, :].astype(wide)
    hi, lo = split_pair(own + (arrived[1088:1104, :].astype(wide) + arrived[1104:1120, :].astype(wide)))
    for r in range(4):
        x, z, h = (x0, x1, x2, x3)[r], (z0, z1, z2, z3)[r], (h0, h1, h2, h3)[r]
        x[0:192, :] = (keep_x[r].astype(wide) + arrived[r * 192 : (r + 1) * 192, :].astype(wide)).astype(low)
        x[192:272, 0:384] = h[0:80, :]
        x[192:272, 384:768] = h[80:160, :]
        x[272:352, 0:384] = h[160:240, :]
        x[272:352, 384:768] = jnp.zeros((80, 384), low)
        came = arrived[768 + r * 80 : 848 + r * 80, :].astype(wide)
        z[0:80, :] = (keep_z[r].astype(wide) + came).astype(low)
        z[80:96, :] = hi
        z[96:112, :] = lo


def up_grad_kernel(n0, n1, n2, n3, keep, send, left, right, buf):
    me, bucket, core = here()
    for r in range(4):
        rows = slice(r * 160, (r + 1) * 160)
        n = (n0, n1, n2, n3)[r]
        left[rows, :] = n[0:160, :]
        right[rows, :] = n[160:320, :]
    up = tn(left[...], right[...])
    for b in range(4):
        for c in range(2):
            starts = [b * 192 + j * 48 + c * 24 for j in range(4)]
            block = jnp.concatenate([up[s : s + 24] for s in starts], axis=0)
            buf[c ^ core, b ^ bucket] = block.astype(low)
    keep[...] = buf[0]
    send[...] = buf[1]


def up_sum_kernel(keep, arrived, z0, z1, z2, z3):
    for d, z in enumerate((z0, z1, z2, z3)):
        z[...] = (keep[d].astype(wide) + arrived[d].astype(wide)).astype(low)


def final_send_kernel(z0, z1, z2, z3, w0, w1, w2, w3, f0, f1, f2, f3, buf, vec):
    me, bucket, core = here()
    zs = (z0, z1, z2, z3)
    ins = sum(z[0:72, :].astype(wide) for z in zs)
    ups = sum(w[...].astype(wide) for w in (w0, w1, w2, w3))
    for d, z in enumerate(zs):
        vec[bucket ^ d] = z[80:96, :].astype(wide) + z[96:112, :].astype(wide)
    hi, lo = split_pair(vec[0] + vec[1] + vec[2] + vec[3])
    pad = jnp.zeros((8, D), wide)
    rest = jnp.zeros((24, SPLIT), wide)
    for j in range(4):
        lanes = slice(j * SPLIT, (j + 1) * SPLIT)
        wide_rows = [ins[i * 24 : (i + 1) * 24, lanes] for i in range(3)] + [rest]
        block = [ups[j * 24 : (j + 1) * 24], pad, jnp.concatenate(wide_rows, axis=1), pad]
        buf[j ^ me] = jnp.concatenate(block, axis=0).astype(low)
    for r, f in enumerate((f0, f1, f2, f3)):
        f[0:16, :] = hi
        f[16:32, :] = lo
        f[32:96, :] = buf[r]


def final_kernel(
    lengths, f0, f1, f2, f3, in_total, up_total, first, query, value, output, second, up_bias, down, stats, buf
):
    me = here()[0]
    for r, f in enumerate((f0, f1, f2, f3)):
        buf[r ^ me] = f[...].astype(wide)
    total = buf[0, 0:16] + buf[0, 16:32]
    for j in (1, 2, 3):
        total = total + (buf[j, 0:16] + buf[j, 16:32])
    first[...] = total[0]
    query[...] = total[1]
    value[...] = total[2]
    output[...] = total[3, :DC]
    second[...] = total[4]
    for i in range(4):
        up_bias[i * D : (i + 1) * D] = total[5 + i]
    down[...] = total[9, :DC]
    count = lengths[0, 0] + lengths[0, 1]
    for b in (1, 2, 3):
        count = count + lengths[b, 0] + lengths[b, 1]
    stats[...] = total[10, :2] / count.astype(wide)
    for j in range(4):
        up_total[:, j * D : (j + 1) * D] = buf[j, 32:56, :]
    for i in range(3):
        piece = jnp.concatenate([buf[j, 64:88, i * SPLIT : (i + 1) * SPLIT] for j in range(4)], axis=1)
        in_total[:, i * D : (i + 1) * D] = piece


def home_kernel(x0, x1, x2, x3, weight, resid, gain, middle_grad, out, buf):
    me = here()[0]
    for r, x in enumerate((x0, x1, x2, x3)):
        buf[r ^ me, 0:80, :] = x[192:272, 0:384]
        buf[r ^ me, 80:160, :] = x[192:272, 384:768]
        buf[r ^ me, 160:240, :] = x[272:352, 0:384]
    e = jnp.zeros((160, D), wide)
    for i in range(3):
        g = jnp.concatenate([unpacked(buf[j, i * 80 : (i + 1) * 80, :]) for j in range(4)], axis=1)
        e = e + nt(g.astype(low), weight[:, i * D : (i + 1) * D])
    full = full_of(resid[...].astype(wide))
    root = jnp.sqrt(jnp.mean(full * full, axis=1, keepdims=True) + epsilon)
    n = full / root
    eg = e * row(gain)
    f = (eg - n * jnp.mean(eg * n, axis=1, keepdims=True)) / root
    lane = lax.broadcasted_iota(jnp.int32, (160, D), 1)
    last = jnp.sum(jnp.where(lane == D - 1, f, 0.0), axis=1, keepdims=True)
    out[...] = (middle_grad[...] + f - last)[:, :DC].astype(low)


def down_sum_kernel(x0, x1, x2, x3, down_total, o0, o1, o2, o3):
    total = x0[0:192, :].astype(wide)
    for x in (x1, x2, x3):
        total = total + x[0:192, :].astype(wide)
    down_total[...] = total[0:96, :DC]
    for d, o in enumerate((o0, o1, o2, o3)):
        block = [total[96 + d * 24 : 120 + d * 24], jnp.zeros((8, D), wide)]
        o[...] = jnp.concatenate(block, axis=0).astype(low)


def out_sum_kernel(o0, o1, o2, o3, out_total):
    total = o0[...].astype(wide) + o1[...].astype(wide) + o2[...].astype(wide) + o3[...].astype(wide)
    out_total[...] = total[0:24, :DC]

def swap_chip(block, step):
    return lax.ppermute(block, "blk", [(k, k ^ (2 * step)) for k in range(8)])


def swap_core(block):
    return lax.ppermute(block, "blk", [(k, k ^ 1) for k in range(8)])


def shift_bucket(block, step):
    return lax.ppermute(block, "bucket", [(b, b ^ step) for b in range(4)])


def exchange(blocks):
    got = {r: swap_chip(blocks[r], r) for r in (3, 1, 2)}
    return [blocks[0], got[1], got[2], got[3]]


def over_buckets(blocks):
    got = {d: shift_bucket(blocks[d], d) for d in (2, 1, 3)}
    return [blocks[0], got[1], got[2], got[3]]


def after(values, *others):
    return lax.optimization_barrier((tuple(values), others))[0]


def body(
    residual_in,
    out_cotangent,
    first_gain,
    input_weight,
    query_bias,
    value_bias,
    output_weight,
    output_bias,
    second_gain,
    up_weight,
    up_bias,
    down_weight,
    down_bias,
    lengths,
    offsets,
    span_order,
):
    where = [span_order, offsets, lengths]
    packed_block = ((240, 2 * SPLIT), low)
    token = ((160, D), low)
    cots = over_buckets([out_cotangent] * 4)
    s0, s1, s2, s3, hidden, root_one = call(
        entry_kernel,
        [packed_block] * 4 + [token, ((160, 1), wide)],
        [residual_in, first_gain, input_weight, query_bias, value_bias],
        [pltpu.VMEM((4, 240, 2 * SPLIT), low)],
    )
    got = exchange([s0, s1, s2, s3])
    (push,) = call(push_kernel, [((160, FF), wide)], [out_cotangent, down_weight])
    hiddens = exchange([hidden] * 4)
    got = list(after(got, push, cots[1], cots[3]))
    query, own_both = call(assemble_kernel, [((640, SPLIT), low), ((640, 2 * SPLIT), low)], got)
    sib_both = swap_core(own_both)
    backed = ((80, 2 * SPLIT), low)
    chance, attended, b0, b1, b2, b3 = call(
        forward_kernel,
        [((3, 640, 1280), low), ((640, SPLIT), wide)] + [backed] * 4,
        where + [query, own_both, sib_both],
        [pltpu.VMEM((1280, SPLIT), low), pltpu.VMEM((3, 1280, SPLIT), low), pltpu.VMEM((640, 1280), wide)],
        small=3,
    )
    back = exchange([b0, b1, b2, b3])
    back = list(after(back, cots[2], *hiddens[1:]))
    (columns,) = call(columns_kernel, [((D, 3 * SPLIT), low)], after([input_weight], b0))
    outs = call(
        middle_kernel,
        [backed] * 4
        + [token] * 4
        + [((320, D), low)] * 4
        + [token, ((160, DC), wide), ((160, D), wide), ((16, D), wide)],
        where
        + back
        + [output_weight, output_bias, residual_in, root_one, out_cotangent, second_gain]
        + [up_weight, up_bias, push],
        [pltpu.VMEM((4, 80, 2 * SPLIT), low), pltpu.VMEM((4, 160, D), low), pltpu.VMEM((4, 320, D), low)],
        small=3,
    )
    actives, lates = list(outs[4:8]), list(outs[8:12])
    branch_own, middle, middle_grad, vector = outs[12:]
    grads = exchange(outs[:4])
    (residual_out,) = call(
        closing_kernel,
        [((160, DC), low)],
        actives + [down_weight, middle, down_bias],
    )
    actives = over_buckets(actives)
    lates = exchange(after(lates, grads[1]))
    query_grad, both_grad, *away = call(
        backward_kernel,
        [((640, SPLIT), low), ((640, 2 * SPLIT), wide)] + [((320, 2 * SPLIT), low)] * 2,
        grads + [query, own_both, sib_both, chance, attended],
        [
            pltpu.VMEM((3, 1280, SPLIT), low),
            pltpu.VMEM((1280, SPLIT), low),
            pltpu.VMEM((640, SPLIT), low),
            pltpu.VMEM((640, 1280), low),
        ],
    )
    arrived = [swap_core(x) for x in after(away, *actives[1:])]
    arrived = list(after(arrived, lates[1], lates[2]))
    outs = call(
        late_kernel,
        [packed_block] * 4 + [((4, 192, D), low), ((4, 80, D), low), ((1120, D), low)],
        [query_grad, both_grad] + arrived + hiddens + actives + cots + back + [branch_own, columns, first_gain, vector],
        [
            pltpu.VMEM((640, D), low),
            pltpu.VMEM((640, D), low),
            pltpu.VMEM((640, 3 * SPLIT), low),
            pltpu.VMEM((2, 4, 192, D), low),
            pltpu.VMEM((2, 4, 80, D), low),
            pltpu.VMEM((2, 4, 4, 24, D), wide),
        ],
    )
    homes = list(outs[:4])
    keep_x, keep_z, send = outs[4:]
    outs = call(
        late_sum_kernel,
        [((352, D), low)] * 4 + [((112, D), low)] * 4,
        [keep_x, keep_z, send, swap_core(send)] + homes,
    )
    in_z = over_buckets(outs[4:])
    home = exchange(outs[:4])
    keep, send = call(
        up_grad_kernel,
        [((4, 96, D), low)] * 2,
        list(after(lates, *in_z[1:])),
        [
            pltpu.VMEM((640, D), low),
            pltpu.VMEM((640, D), low),
            pltpu.VMEM((2, 4, 96, D), low),
        ],
    )
    up_z = over_buckets(call(up_sum_kernel, [((96, D), low)] * 4, [keep, swap_core(send)]))
    down_total, *pieces = call(down_sum_kernel, [((96, DC), wide)] + [((32, D), low)] * 4, home)
    (out_total,) = call(out_sum_kernel, [((24, DC), wide)], over_buckets(pieces))
    (residual_grad,) = call(
        home_kernel,
        [((160, DC), low)],
        home + [input_weight, residual_in, first_gain, middle_grad],
        [pltpu.VMEM((4, 240, 2 * SPLIT), low)],
    )
    finals = call(
        final_send_kernel,
        [((96, D), low)] * 4,
        in_z + up_z,
        [pltpu.VMEM((4, 64, D), low), pltpu.VMEM((4, 16, D), wide)],
    )
    in_total, up_total, first, query_sum, value_sum, output, second, up_sum_bias, down, stats = call(
        final_kernel,
        [((24, 3 * D), wide), ((24, FF), wide)]
        + [((D,), wide)] * 3
        + [((DC,), wide), ((D,), wide), ((FF,), wide), ((DC,), wide), ((2,), wide)],
        [lengths] + exchange(finals),
        [pltpu.VMEM((4, 96, D), wide)],
        small=1,
    )
    return (
        residual_out,
        residual_grad,
        first,
        in_total,
        query_sum,
        value_sum,
        out_total,
        output,
        second,
        up_total,
        up_sum_bias,
        down_total,
        down,
        stats,
    )


def solution(mesh):
    placed = (
        P(("bucket", "blk"), None),
        P(("bucket", "blk"), None),
        P(),
        P(),
        P(),
        P(),
        P(),
        P(),
        P(),
        P(),
        P(),
        P(),
        P(),
        P(),
        P("bucket", None),
        P(),
    )
    return jax.shard_map(
        body if dict(mesh.shape) == {"bucket": 4, "blk": 8} else general_body,
        mesh=mesh,
        in_specs=placed,
        out_specs=(
            P(("bucket", "blk"), None),
            P(("bucket", "blk"), None),
            P(),
            P(("bucket", "blk"), None),
            P(),
            P(),
            P(("bucket", "blk"), None),
            P(),
            P(),
            P(("bucket", "blk"), None),
            P(),
            P(("bucket", "blk"), None),
            P(),
            P(),
        ),
        check_vma=False,
    )
```

```python
import jax
import jax.numpy as jnp
from jax import lax
from jax.experimental import pallas as pl
from jax.experimental.pallas import tpu as pltpu
from jax.sharding import PartitionSpec as P

D = 768
HEADS = 12
HEAD_DIM = 64


epsilon = 1e-05
masked_value = -1e30


def center_norm(resid, gain):
    full = jnp.concatenate([resid, -jnp.sum(resid, axis=1, keepdims=True)], axis=1)
    root = jnp.sqrt(jnp.mean(full * full, axis=1, keepdims=True) + epsilon)
    return (full / root * gain, root[:, 0])


def gelu_tanh(inputs):
    return jax.nn.gelu(inputs, approximate=True)


def heads_of(block):
    return block.reshape(block.shape[0], HEADS, HEAD_DIM)


def places_of(span_order, begin, count, half_rows):
    spans = lax.dynamic_slice_in_dim(span_order, begin // half_rows, count // half_rows)
    inner = jnp.arange(half_rows, dtype=jnp.int32)
    return (spans[:, None] * half_rows + inner[None, :]).reshape(count)


def documents_of(places, lengths, offsets):
    first_in = (places >= offsets[0, 0]) & (places < offsets[0, 0] + lengths[0, 0])
    second_in = (places >= offsets[0, 1]) & (places < offsets[0, 1] + lengths[0, 1])
    return jnp.where(first_in, 0, jnp.where(second_in, 1, -1)).astype(jnp.int32)


def allowed_of(query_places, query_docs, key_places, key_docs):
    same = (query_docs[:, None] == key_docs[None, :]) & (query_docs[:, None] >= 0)
    return (same & (key_places[None, :] <= query_places[:, None]))[None]


def block_shape(count, unit):
    shards = count // unit
    width = max(1, 1024 // unit)
    while shards % width != 0:
        width = width - 1
    return (shards // width, width * unit)


def general_body(
    residual_in,
    out_cotangent,
    first_gain,
    input_weight,
    query_bias,
    value_bias,
    output_weight,
    output_bias,
    second_gain,
    up_weight,
    up_bias,
    down_weight,
    down_bias,
    lengths,
    offsets,
    span_order,
):
    rows = residual_in.shape[0]
    half_rows = rows // 2
    score_scale = HEAD_DIM ** (-0.5)
    index = lax.axis_index("blk")
    bucket_index = lax.axis_index("bucket")
    own_lengths = lax.dynamic_slice_in_dim(lengths, bucket_index, 1, 0)
    valid_count = jnp.sum(lengths.astype(jnp.float32))
    query_places = places_of(span_order, index * rows, rows, half_rows)
    query_docs = documents_of(query_places, own_lengths, offsets)
    valid = (query_docs >= 0).astype(jnp.float32)
    resid = residual_in.astype(jnp.float32)
    normed, first_back, first_root = jax.vjp(center_norm, resid, first_gain, has_aux=True)
    hidden_in = normed.astype(jnp.bfloat16)
    projected = jnp.dot(hidden_in, input_weight, preferred_element_type=jnp.float32)
    query = (projected[:, :D] + query_bias).astype(jnp.bfloat16)
    keys = projected[:, D : 2 * D].astype(jnp.bfloat16)
    values = (projected[:, 2 * D :] + value_bias).astype(jnp.bfloat16)
    query_heads = heads_of(query)
    key_heads = heads_of(keys)
    value_heads = heads_of(values)
    initial = (
        jnp.full((HEADS, rows), masked_value, jnp.float32),
        jnp.zeros((HEADS, rows), jnp.float32),
        jnp.zeros((HEADS, rows, HEAD_DIM), jnp.float32),
    )
    state = initial
    key_piece = lax.all_gather(keys, "blk", axis=0, tiled=True)
    value_piece = lax.all_gather(values, "blk", axis=0, tiled=True)
    count = key_piece.shape[0]
    number, width = block_shape(count, rows)
    key_places = places_of(span_order, jnp.int32(0), count, half_rows)
    key_docs = documents_of(key_places, own_lengths, offsets)

    def forward_advance(state, parts):
        key_block, value_block, places_block, docs_block = parts
        peak, total, summed = state
        scores = (
            jnp.einsum(
                "qhd,khd->hqk", query_heads, heads_of(key_block), preferred_element_type=jnp.float32
            )
            * score_scale
        )
        allowed = allowed_of(query_places, query_docs, places_block, docs_block)
        masked = jnp.where(allowed, scores, masked_value)
        new_peak = jnp.maximum(peak, jnp.max(masked, axis=2))
        decay = jnp.exp(peak - new_peak)
        weights = jnp.where(allowed, jnp.exp(masked - new_peak[:, :, None]), 0.0)
        total = total * decay + jnp.sum(weights, axis=2)
        summed = summed * decay[:, :, None] + jnp.einsum(
            "hqk,khd->hqd",
            weights.astype(jnp.bfloat16),
            heads_of(value_block),
            preferred_element_type=jnp.float32,
        )
        return ((new_peak, total, summed), None)

    state, _ = lax.scan(
        forward_advance,
        state,
        (
            key_piece.reshape(number, width, D),
            value_piece.reshape(number, width, D),
            key_places.reshape(number, width),
            key_docs.reshape(number, width),
        ),
    )
    peak, total, summed = state
    denominator = total + 1.0 - valid[None, :]
    attended = summed / denominator[:, :, None]
    log_total = peak + jnp.log(denominator)
    mixed = attended.transpose(1, 0, 2).reshape(rows, D).astype(jnp.bfloat16)
    branch = jnp.dot(mixed, output_weight, preferred_element_type=jnp.float32) + output_bias
    middle = resid + branch
    normed_two, second_back, second_root = jax.vjp(center_norm, middle, second_gain, has_aux=True)
    hidden_two = normed_two.astype(jnp.bfloat16)
    upward = jnp.dot(hidden_two, up_weight, preferred_element_type=jnp.float32) + up_bias
    active_float, gelu_back = jax.vjp(gelu_tanh, upward)
    active = active_float.astype(jnp.bfloat16)
    closing = jnp.dot(active, down_weight, preferred_element_type=jnp.float32) + down_bias
    residual_out = (middle + closing).astype(jnp.bfloat16)
    stat_sums = jnp.stack([jnp.sum(valid * first_root), jnp.sum(valid * second_root)])
    stat_sums = lax.psum(stat_sums, ("bucket", "blk"))
    cotangent = out_cotangent.astype(jnp.float32)
    down_grad = jnp.einsum("rf,rc->fc", active, out_cotangent, preferred_element_type=jnp.float32)
    down_bias_grad = jnp.sum(cotangent, axis=0)
    active_grad = jnp.einsum(
        "rc,fc->rf", out_cotangent, down_weight, preferred_element_type=jnp.float32
    )
    (upward_float,) = gelu_back(active_grad)
    upward_grad = upward_float.astype(jnp.bfloat16)
    up_grad = jnp.einsum("rd,rf->df", hidden_two, upward_grad, preferred_element_type=jnp.float32)
    up_bias_grad = jnp.sum(upward_grad.astype(jnp.float32), axis=0)
    hidden_two_grad = jnp.einsum(
        "rf,df->rd", upward_grad, up_weight, preferred_element_type=jnp.float32
    )
    middle_part, second_gain_grad = second_back(hidden_two_grad)
    middle_grad = cotangent + middle_part
    branch_grad = middle_grad.astype(jnp.bfloat16)
    output_grad = jnp.einsum("rd,rc->dc", mixed, branch_grad, preferred_element_type=jnp.float32)
    output_bias_grad = jnp.sum(branch_grad.astype(jnp.float32), axis=0)
    attended_grad = jnp.einsum(
        "rc,dc->rd", branch_grad, output_weight, preferred_element_type=jnp.float32
    ).astype(jnp.bfloat16)
    grad_heads = heads_of(attended_grad)
    delta = jnp.einsum("rhd,hrd->hr", grad_heads.astype(jnp.float32), attended)
    query_zero = jnp.zeros((rows, HEADS, HEAD_DIM), jnp.float32)
    accum = query_zero
    key_piece = lax.all_gather(keys, "blk", axis=0, tiled=True)
    value_piece = lax.all_gather(values, "blk", axis=0, tiled=True)
    count = key_piece.shape[0]
    number, width = block_shape(count, rows)
    key_places = places_of(span_order, jnp.int32(0), count, half_rows)
    key_docs = documents_of(key_places, own_lengths, offsets)

    def query_advance(accum, parts):
        key_block, value_block, places_block, docs_block = parts
        block_keys = heads_of(key_block)
        scores = (
            jnp.einsum("qhd,khd->hqk", query_heads, block_keys, preferred_element_type=jnp.float32)
            * score_scale
        )
        allowed = allowed_of(query_places, query_docs, places_block, docs_block)
        chance = jnp.where(
            allowed, jnp.exp(jnp.where(allowed, scores, masked_value) - log_total[:, :, None]), 0.0
        )
        push = jnp.einsum(
            "qhd,khd->hqk", grad_heads, heads_of(value_block), preferred_element_type=jnp.float32
        )
        slope = (chance * (push - delta[:, :, None])).astype(jnp.bfloat16)
        accum = (
            accum
            + jnp.einsum("hqk,khd->qhd", slope, block_keys, preferred_element_type=jnp.float32)
            * score_scale
        )
        return (accum, None)

    accum, _ = lax.scan(
        query_advance,
        accum,
        (
            key_piece.reshape(number, width, D),
            value_piece.reshape(number, width, D),
            key_places.reshape(number, width),
            key_docs.reshape(number, width),
        ),
    )
    log_all, delta_all = (
        lax.all_gather(log_total.T, "blk", axis=0, tiled=True),
        lax.all_gather(delta.T, "blk", axis=0, tiled=True),
    )
    key_zero = jnp.zeros((rows, HEADS, HEAD_DIM), jnp.float32)
    state = (key_zero, key_zero)
    begin = jnp.int32(0)
    query_piece = lax.all_gather(query, "blk", axis=0, tiled=True)
    grad_piece = lax.all_gather(attended_grad, "blk", axis=0, tiled=True)
    count = query_piece.shape[0]
    number, width = block_shape(count, rows)
    piece_places = places_of(span_order, begin, count, half_rows)
    piece_docs = documents_of(piece_places, own_lengths, offsets)
    piece_log = lax.dynamic_slice_in_dim(log_all, begin, count, 0)
    piece_delta = lax.dynamic_slice_in_dim(delta_all, begin, count, 0)

    def key_advance(state, parts):
        query_block, grad_block, places_block, docs_block, log_block, delta_block = parts
        key_sum, value_sum = state
        block_query = heads_of(query_block)
        block_grad = heads_of(grad_block)
        scores = (
            jnp.einsum("qhd,khd->hqk", block_query, key_heads, preferred_element_type=jnp.float32)
            * score_scale
        )
        allowed = allowed_of(places_block, docs_block, query_places, query_docs)
        chance = jnp.where(
            allowed,
            jnp.exp(jnp.where(allowed, scores, masked_value) - log_block.T[:, :, None]),
            0.0,
        )
        value_sum = value_sum + jnp.einsum(
            "hqk,qhd->khd",
            chance.astype(jnp.bfloat16),
            block_grad,
            preferred_element_type=jnp.float32,
        )
        push = jnp.einsum(
            "qhd,khd->hqk", block_grad, value_heads, preferred_element_type=jnp.float32
        )
        slope = (chance * (push - delta_block.T[:, :, None])).astype(jnp.bfloat16)
        key_sum = (
            key_sum
            + jnp.einsum("hqk,qhd->khd", slope, block_query, preferred_element_type=jnp.float32)
            * score_scale
        )
        return ((key_sum, value_sum), None)

    state, _ = lax.scan(
        key_advance,
        state,
        (
            query_piece.reshape(number, width, D),
            grad_piece.reshape(number, width, D),
            piece_places.reshape(number, width),
            piece_docs.reshape(number, width),
            piece_log.reshape(number, width, HEADS),
            piece_delta.reshape(number, width, HEADS),
        ),
    )
    key_sum, value_sum = state
    query_low = accum.reshape(rows, D).astype(jnp.bfloat16)
    key_low = key_sum.reshape(rows, D).astype(jnp.bfloat16)
    value_low = value_sum.reshape(rows, D).astype(jnp.bfloat16)
    projected_grad = jnp.concatenate([query_low, key_low, value_low], axis=1)
    input_grad = jnp.einsum(
        "rd,re->de", hidden_in, projected_grad, preferred_element_type=jnp.float32
    )
    query_bias_grad = jnp.sum(query_low.astype(jnp.float32), axis=0)
    value_bias_grad = jnp.sum(value_low.astype(jnp.float32), axis=0)
    hidden_in_grad = jnp.einsum(
        "re,de->rd", projected_grad, input_weight, preferred_element_type=jnp.float32
    )
    resid_part, first_gain_grad = first_back(hidden_in_grad)
    residual_grad = (middle_grad + resid_part).astype(jnp.bfloat16)
    input_part, output_part, up_part, down_part = (
        lax.psum_scatter(input_grad, ("bucket", "blk"), scatter_dimension=0, tiled=True),
        lax.psum_scatter(output_grad, ("bucket", "blk"), scatter_dimension=0, tiled=True),
        lax.psum_scatter(up_grad, ("bucket", "blk"), scatter_dimension=0, tiled=True),
        lax.psum_scatter(down_grad, ("bucket", "blk"), scatter_dimension=0, tiled=True),
    )
    (
        first_sum,
        query_sum_bias,
        value_sum_bias,
        output_sum_bias,
        second_sum,
        up_sum_bias,
        down_sum_bias,
    ) = lax.psum(
        (
            first_gain_grad,
            query_bias_grad,
            value_bias_grad,
            output_bias_grad,
            second_gain_grad,
            up_bias_grad,
            down_bias_grad,
        ),
        ("bucket", "blk"),
    )
    mean_norms = stat_sums / valid_count
    return (
        residual_out,
        residual_grad,
        first_sum,
        input_part,
        query_sum_bias,
        value_sum_bias,
        output_part,
        output_sum_bias,
        second_sum,
        up_part,
        up_sum_bias,
        down_part,
        down_sum_bias,
        mean_norms,
    )


DC = 767
SPLIT = 192
FF = 3072
low = jnp.bfloat16
wide = jnp.float32
VMEM = pl.BlockSpec(memory_space=pltpu.VMEM)
SMEM = pl.BlockSpec(memory_space=pltpu.SMEM)
HBM = pl.BlockSpec(memory_space=pltpu.HBM)

def padded_bytes(shape, dtype):
    shape = (1, 1) + tuple(shape)
    size = jnp.dtype(dtype).itemsize
    rows, lanes = -(-shape[-2] // 16) * 16, -(-shape[-1] // 128) * 128
    for d in shape[:-2]:
        rows = rows * d
    return rows * lanes * size


def call(kernel, outs, ins, scratch=(), extra=6, small=0, far=(), work=0):
    shapes = [jax.ShapeDtypeStruct(s, d) for s, d in outs]
    held = [(s, d) for s, d in outs]
    held += [(x.shape, x.dtype) for i, x in enumerate(ins) if i >= small and i not in far]
    held += [(s.shape, s.dtype) for s in scratch if s.memory_space == pltpu.VMEM]
    limit = sum(padded_bytes(s, d) for s, d in held) + extra * 2**20
    return pl.pallas_call(
        kernel,
        out_shape=shapes,
        in_specs=[SMEM if i < small else HBM if i in far else VMEM for i in range(len(ins))],
        out_specs=[VMEM] * len(outs),
        scratch_shapes=list(scratch),
        compiler_params=pltpu.CompilerParams(vmem_limit_bytes=min(limit, 60 * 2**20)),
        cost_estimate=pl.CostEstimate(
            flops=int(1000 + work * 1.1e9),
            bytes_accessed=1000,
            transcendentals=0,
        ),
    )(*ins)


def here():
    index = lax.axis_index("blk")
    return index // 2, lax.axis_index("bucket"), index % 2


def full_of(x):
    rows=x.shape[0]
    wide_x=jnp.concatenate([x,jnp.zeros((rows,1),x.dtype)],axis=1)
    last=lax.broadcasted_iota(jnp.int32,(rows,D),1)==D-1
    return jnp.where(last,-jnp.sum(x,axis=1,keepdims=True),wide_x)

def row(ref):
    return ref[...].reshape(1, ref.shape[0])


def nt(a, b):
    return lax.dot_general(a, b, (((1,), (1,)), ((), ())), preferred_element_type=wide)


def tn(a, b):
    return lax.dot_general(a, b, (((0,), (0,)), ((), ())), preferred_element_type=wide)


def packed(x):
    half = x.shape[0] // 2
    return jnp.concatenate([x[:half], x[half:]], axis=1).astype(low)


def unpacked(x):
    x = x.astype(wide)
    half = x.shape[1] // 2
    return jnp.concatenate([x[:, :half], x[:, half:]], axis=0)


def split_pair(x):
    hi = x.astype(low)
    return hi, (x - hi.astype(wide)).astype(low)


def head_mask(x, h):
    lane = lax.broadcasted_iota(jnp.int32, x.shape, 1)
    return jnp.where((lane >= h * 64) & (lane < (h + 1) * 64), x, jnp.zeros_like(x))


def limits(spans, offsets, lengths, bucket, chip, core, half):
    place = spans[chip * 4 + core * 2 + half] * 80 + lax.broadcasted_iota(jnp.int32, (80, 1), 0)
    one, two = offsets[0, 0], offsets[0, 1]
    first = (place >= one) & (place < one + lengths[bucket, 0])
    second = (place >= two) & (place < two + lengths[bucket, 1])
    return jnp.where(first, one, two), jnp.where(first | second, place, -1)


def entry_kernel(
    resid_far, gain_far, weight_far, qbias_far, vbias_far, s0, s1, s2, s3, hidden_out, root_out,
    buf, resid, gain, weight, qbias, vbias, sems,
):
    me = here()[0]
    copies = [
        pltpu.make_async_copy(a, b, sems.at[i])
        for i, (a, b) in enumerate(
            [(resid_far, resid), (gain_far, gain), (qbias_far, qbias), (vbias_far, vbias)]
            + [(weight_far.at[:, pl.ds(i * D, D)], weight.at[i]) for i in range(3)]
        )
    ]
    for copy in copies:
        copy.start()
    copies[0].wait()
    full = full_of(resid[...].astype(wide))
    root = jnp.sqrt(jnp.mean(full * full, axis=1, keepdims=True) + epsilon)
    root_out[...] = root
    copies[1].wait()
    hidden = (full / root * row(gain)).astype(low)
    hidden_out[...] = hidden
    copies[2].wait()
    copies[3].wait()
    for i in range(3):
        copies[4 + i].wait()
        p = jnp.dot(hidden, weight[i], preferred_element_type=wide)
        if i == 0:
            p = (p + row(qbias)) * 0.125
        if i == 2:
            p = p + row(vbias)
        for j in range(4):
            buf[j ^ me, i * 80 : (i + 1) * 80, :] = packed(p[:, j * SPLIT : (j + 1) * SPLIT])
    for r, s in enumerate((s0, s1, s2, s3)):
        s[...] = buf[r]


def push_kernel(cot, weight, out):
    for i in range(4):
        out[:, i * D : (i + 1) * D] = nt(cot[...], weight[i * D : (i + 1) * D, :])


def columns_kernel(weight, out):
    me = here()[0]
    for j in range(4):

        @pl.when(me == j)
        def _():
            for i in range(3):
                piece = weight[:, i * D + j * SPLIT : i * D + (j + 1) * SPLIT].astype(wide)
                out[:, i * SPLIT : (i + 1) * SPLIT] = piece.astype(low)


def assemble_kernel(p0, p1, p2, p3, query, both):
    for r, p in enumerate((p0, p1, p2, p3)):
        rows = slice(r * 160, (r + 1) * 160)
        query[rows, :] = unpacked(p[0:80, :]).astype(low)
        both[rows, :SPLIT] = unpacked(p[80:160, :]).astype(low)
        both[rows, SPLIT:] = unpacked(p[160:240, :]).astype(low)


def forward_kernel(
    spans, offsets, lengths, query, own, sib, chance, attended, b0, b1, b2, b3, keys, vals, scores
):
    me, bucket, core = here()
    keys[:640, :] = own[:, :SPLIT]
    keys[640:, :] = sib[:, :SPLIT]
    v = jnp.concatenate([own[:, SPLIT:].astype(wide), sib[:, SPLIT:].astype(wide)], axis=0)
    for h in range(3):
        vals[h] = head_mask(v, h).astype(low)
    lane = lax.broadcasted_iota(jnp.int32, (1, 1280), 1)
    place = lane
    for blk in range(16):
        chip = ((blk % 8) // 2) ^ me
        span = spans[chip * 4 + (core ^ (blk // 8)) * 2 + blk % 2]
        place = jnp.where((lane >= blk * 80) & (lane < (blk + 1) * 80), lane + (span - blk) * 80, place)
    q = query[...].astype(wide)
    for h in range(3):
        scores[...] = nt(head_mask(q, h).astype(low), keys[...])
        for blk in range(8):
            rows = slice(blk * 80, (blk + 1) * 80)
            lo, hi = limits(spans, offsets, lengths, bucket, (blk // 2) ^ me, core, blk % 2)
            s = jnp.where((place >= lo) & (place <= hi), scores[rows, :], masked_value)
            peak = jnp.max(s, axis=1, keepdims=True)
            w = jnp.exp(s - peak)
            total = jnp.sum(w, axis=1, keepdims=True)
            chance[h, rows, :] = (w * jnp.where(hi >= 0, 1.0 / total, 0.0)).astype(low)
        part = jnp.dot(chance[h], vals[h], preferred_element_type=wide)
        if h == 0:
            attended[...] = part
        else:
            attended[...] += part
    acc = attended[...]
    for r, b in enumerate((b0, b1, b2, b3)):
        b[...] = packed(acc[r * 160 : (r + 1) * 160])


def middle_kernel(
    spans, offsets, lengths, p0, p1, p2, p3, out_weight, out_bias, resid, root_in, cot, gain, up_weight, up_bias, push,
    d0, d1, d2, d3, act_keep, act_send, n0, n1, n2, n3, branch_own, middle, middle_grad, vector,
    dbuf, abuf, nbuf,
):
    me, bucket, core = here()
    branch = row(out_bias)
    for r, p in enumerate((p0, p1, p2, p3)):
        w = out_weight[pl.ds(pl.multiple_of((me ^ r) * SPLIT, SPLIT), SPLIT), :]
        branch = branch + jnp.dot(unpacked(p[...]).astype(low), w, preferred_element_type=wide)
    mid = resid[...].astype(wide) + branch
    middle[...] = mid
    full = full_of(mid)
    root = jnp.sqrt(jnp.mean(full * full, axis=1, keepdims=True) + epsilon)
    n = full / root
    hidden = (n * row(gain)).astype(low)
    for r in range(4):
        nbuf[r, 0:160, :] = hidden
    e = jnp.zeros((160, D), wide)
    c = 0.7978845608028654
    up_sums = []
    for blk in range(4):
        cols = slice(blk * D, (blk + 1) * D)
        u = jnp.dot(hidden, up_weight[:, cols], preferred_element_type=wide) + up_bias[cols].reshape(1, D)
        t = jnp.tanh(c * (u + 0.044715 * u * u * u))
        abuf[blk ^ bucket] = (0.5 * u * (1.0 + t)).astype(low)
        slope = 0.5 * (1.0 + t) + 0.5 * u * (1.0 - t * t) * (c * (1.0 + 3 * 0.044715 * u * u))
        g = (push[:, cols] * slope).astype(low)
        nbuf[blk ^ me, 160:320, :] = g
        up_sums.append(jnp.sum(g.astype(wide), axis=0, keepdims=True))
        e = e + nt(g, up_weight[:, cols])
    gain_sum = jnp.sum(e * n, axis=0, keepdims=True)
    eg = e * row(gain)
    f = (eg - n * jnp.mean(eg * n, axis=1, keepdims=True)) / root
    cot_wide = jnp.concatenate([cot[...].astype(wide), jnp.zeros((160, 1), wide)], axis=1)
    lane = lax.broadcasted_iota(jnp.int32, (160, D), 1)
    last = jnp.sum(jnp.where(lane == D - 1, f, 0.0), axis=1, keepdims=True)
    grad = jnp.where(lane == D - 1, 0.0, cot_wide + f - last)
    middle_grad[...] = grad
    grad_low = grad.astype(low)
    grad_wide = grad_low.astype(wide)
    branch_own[...] = grad_low
    back = nt(grad_wide[:, :DC].astype(low), out_weight[...])
    for j in range(4):
        dbuf[j ^ me] = packed(back[:, j * SPLIT : (j + 1) * SPLIT])
    for r in range(4):
        (d0, d1, d2, d3)[r][...] = dbuf[r]
        (act_keep, act_send)[r % 2][r // 2 * 160 : r // 2 * 160 + 160, :] = abuf[r]
        (n0, n1, n2, n3)[r][...] = nbuf[r]
    ends = [limits(spans, offsets, lengths, bucket, me, core, half)[1] for half in range(2)]
    valid = jnp.where(jnp.concatenate(ends, axis=0) >= 0, 1.0, 0.0)
    one = jnp.sum(valid * root_in[...], axis=0, keepdims=True)
    two = jnp.sum(valid * root, axis=0, keepdims=True)
    at = lax.broadcasted_iota(jnp.int32, (1, D), 1)
    stats = jnp.where(at == 0, one, jnp.where(at == 1, two, 0.0))
    zero = jnp.zeros((1, D), wide)
    sums = [zero, zero, zero, jnp.sum(grad_wide, axis=0, keepdims=True), gain_sum] + up_sums
    sums += [jnp.sum(cot_wide, axis=0, keepdims=True), stats] + [zero] * 5
    vector[...] = jnp.concatenate(sums, axis=0)


def closing_kernel(act_keep, act_send, weight, middle, bias, out):
    bucket = here()[1]
    acc = middle[...] + row(bias)
    for d in range(4):
        w = weight[pl.ds(pl.multiple_of((bucket ^ d) * D, D), D), :]
        a = (act_keep, act_send)[d % 2][d // 2 * 160 : d // 2 * 160 + 160, :]
        acc = acc + jnp.dot(a, w, preferred_element_type=wide)
    out[...] = acc.astype(low)


def backward_kernel(
    d0, d1, d2, d3, query, own, sib, chance, attended, query_grad, both_grad, away_one, away_two, keys, vals, grads, slopes
):
    for r, d in enumerate((d0, d1, d2, d3)):
        grads[r * 160 : (r + 1) * 160, :] = unpacked(d[...]).astype(low)
    k = jnp.concatenate([own[:, :SPLIT], sib[:, :SPLIT]], axis=0).astype(wide)
    for h in range(3):
        keys[h] = head_mask(k, h).astype(low)
    vals[:640, :] = own[:, SPLIT:].astype(wide).astype(low)
    vals[640:, :] = sib[:, SPLIT:].astype(wide).astype(low)
    dq = jnp.zeros((640, SPLIT), wide)
    dk = jnp.zeros((1280, SPLIT), wide)
    dv = jnp.zeros((1280, SPLIT), wide)
    g = grads[...].astype(wide)
    q = query[...].astype(wide)
    for h in range(3):
        gh = head_mask(g, h)
        gl = gh.astype(low)
        delta = jnp.sum(gh * attended[...], axis=1, keepdims=True)
        for r in range(4):
            rows = slice(r * 160, (r + 1) * 160)
            push = nt(gl[rows, :], vals[...])
            slopes[rows, :] = (chance[h, rows, :].astype(wide) * (push - delta[rows, :])).astype(low)
        dq = dq + jnp.dot(slopes[...], keys[h], preferred_element_type=wide)
        dk = dk + tn(slopes[...], head_mask(q, h).astype(low))
        dv = dv + tn(chance[h], gl)
    query_grad[...] = (dq * 0.125).astype(low)
    both_grad[:, :SPLIT] = dk[:640]
    both_grad[:, SPLIT:] = dv[:640]
    away_one[:, :SPLIT] = dk[640:960].astype(low)
    away_one[:, SPLIT:] = dv[640:960].astype(low)
    away_two[:, :SPLIT] = dk[960:].astype(low)
    away_two[:, SPLIT:] = dv[960:].astype(low)


def late_kernel(
    query_grad, both_grad, arrive_one, arrive_two, i0, i1, i2, i3, act_keep, act_came, c0, c1, p0, p1, p2, p3, branch_own, columns, gain, vector,
    h0, h1, h2, h3, keep_x, keep_z, send, left, right, heads, xbuf, zbuf,
):
    me, bucket, core = here()
    arrived = jnp.concatenate([arrive_one[...].astype(wide), arrive_two[...].astype(wide)], axis=0)
    both = both_grad[...] + arrived
    parts = [query_grad[...].astype(wide), both[:, :SPLIT], both[:, SPLIT:]]
    parts = [p.astype(low).astype(wide) for p in parts]
    for r, h in enumerate((h0, h1, h2, h3)):
        left[r * 160 : (r + 1) * 160, :] = (i0, i1, i2, i3)[r][...]
        for i in range(3):
            h[i * 80 : (i + 1) * 80, :] = packed(parts[i][r * 160 : (r + 1) * 160])
    heads[...] = jnp.concatenate(parts, axis=1).astype(low)
    grad = tn(left[...], heads[...])
    sums = jnp.sum(grad * columns[...].astype(wide), axis=1, keepdims=True)
    gain_row = jnp.transpose(jnp.broadcast_to(sums, (D, 128)))[0:1] / row(gain)
    lane = lax.broadcasted_iota(jnp.int32, (1, D), 1)
    mine = (lane >= me * SPLIT) & (lane < (me + 1) * SPLIT)

    def column_sum(x):
        s = jnp.sum(x, axis=0, keepdims=True)
        return jnp.where(mine, jnp.concatenate([s] * 4, axis=1), 0.0)

    at = lax.broadcasted_iota(jnp.int32, (16, D), 0)
    total = vector[...] + jnp.where(at == 0, gain_row, 0.0)
    total = total + jnp.where(at == 1, column_sum(parts[0]), 0.0)
    total = total + jnp.where(at == 2, column_sum(parts[2]), 0.0)
    thirds = [grad[:, i * SPLIT : (i + 1) * SPLIT] for i in range(3)]
    for b in range(4):
        for c in range(2):
            block = []
            for part in thirds:
                starts = [b * 192 + j * 48 + c * 24 for j in range(4)]
                block.append(jnp.concatenate([part[s : s + 24] for s in starts], axis=1))
            zbuf[c ^ core, b ^ bucket, 0:72, :] = jnp.concatenate(block, axis=0)
    for r, p in enumerate((p0, p1, p2, p3)):
        out = tn(unpacked(p[...]).astype(low), branch_own[...])
        for j in range(4):
            for c in range(2):
                s = j * 48 + c * 24
                zbuf[c ^ core, me ^ r ^ bucket, 72 + j * 24 : 96 + j * 24, :] = out[s : s + 24]
    for d, c in enumerate((c0, c1)):
        cot = c[...].astype(wide)
        right[d * 160 : (d + 1) * 160, :] = jnp.concatenate([cot, jnp.zeros((160, 1), wide)], axis=1).astype(low)
    for half in range(2):
        left[0:160, :] = act_keep[half * 160 : half * 160 + 160, :]
        left[160:320, :] = act_came[half * 160 : half * 160 + 160, :]
        down = tn(left[0:320, :], right[0:320, :])
        for j in range(4):
            for c in range(2):
                s = j * 192 + c * 96
                xbuf[c ^ core, j ^ me, half * 96 : half * 96 + 96, :] = down[s : s + 96].astype(low)
    keep_x[...] = xbuf[0]
    for r in range(4):
        keep_z[r] = zbuf[0, r]
        send[r * 192 : (r + 1) * 192, :] = xbuf[1, r]
        block = jnp.concatenate([zbuf[1, r], jnp.zeros((8, D), wide)], axis=0)
        send[768 + r * 176 : 944 + r * 176, :] = block.astype(low)
    hi, lo = split_pair(total)
    send[1472:1488, :] = hi
    send[1488:1504, :] = lo


def late_sum_kernel(keep_x, keep_z, send, arrived, h0, h1, h2, h3, x0, x1, x2, x3, z_keep, z_send):
    own = send[1472:1488, :].astype(wide) + send[1488:1504, :].astype(wide)
    hi, lo = split_pair(own + (arrived[1472:1488, :].astype(wide) + arrived[1488:1504, :].astype(wide)))
    blocks = []
    for r in range(4):
        x, h = (x0, x1, x2, x3)[r], (h0, h1, h2, h3)[r]
        x[0:192, :] = (keep_x[r].astype(wide) + arrived[r * 192 : (r + 1) * 192, :].astype(wide)).astype(low)
        x[192:272, 0:384] = h[0:80, :]
        x[192:272, 384:768] = h[80:160, :]
        x[272:352, 0:384] = h[160:240, :]
        x[272:352, 384:768] = jnp.zeros((80, 384), low)
        came = arrived[768 + r * 176 : 944 + r * 176, :].astype(wide)
        blocks.append(keep_z[r] + came[0:168])
    z_keep[0:168, :] = blocks[0]
    z_keep[168:336, :] = blocks[2]
    sums = [hi.astype(wide)[0:12], lo.astype(wide)[0:12], jnp.zeros((8, D), wide)]
    z_send[...] = jnp.concatenate([blocks[1], blocks[3]] + sums, axis=0).astype(low)


def pair_sum(own, came, start):
    a = own[start : start + 12] + own[start + 12 : start + 24]
    b = came[start : start + 12] + came[start + 12 : start + 24]
    return a + b


def late_mid_kernel(z_keep, z_send, came, z_own, z_next):
    came = came[...].astype(wide)
    hi, lo = split_pair(pair_sum(z_send[...].astype(wide), came, 336))
    z_own[...] = z_keep[0:168, :] + came[0:168]
    block = [z_keep[168:336, :] + came[168:336], hi.astype(wide), lo.astype(wide)]
    z_next[...] = jnp.concatenate(block, axis=0).astype(low)


def up_grad_kernel(n0, n1, n2, n3, keep, send_one, send_two, send_three, left, right, buf):
    me, bucket, core = here()
    for r in range(4):
        rows = slice(r * 160, (r + 1) * 160)
        n = (n0, n1, n2, n3)[r]
        left[rows, :] = n[0:160, :]
        right[rows, :] = n[160:320, :]
    up = tn(left[...], right[...])
    for b in range(4):
        for c in range(2):
            starts = [b * 192 + j * 48 + c * 24 for j in range(4)]
            block = jnp.concatenate([up[s : s + 24] for s in starts], axis=0)
            buf[c ^ core, b ^ bucket] = block.astype(low)
    keep[...] = buf[0]
    send_one[0:96, :] = buf[1, 0]
    send_one[96:128, :] = buf[1, 1, 0:32, :]
    send_two[0:64, :] = buf[1, 1, 32:96, :]
    send_two[64:128, :] = buf[1, 2, 0:64, :]
    send_three[0:32, :] = buf[1, 2, 64:96, :]
    send_three[32:128, :] = buf[1, 3]


def up_sum_kernel(keep, arrive_one, arrive_two, arrive_three, w_keep, w_send):
    parts = [a[...].astype(wide) for a in (arrive_one, arrive_two, arrive_three)]
    arrived = jnp.concatenate(parts, axis=0)
    for d in range(4):
        total = keep[d].astype(wide) + arrived[d * 96 : (d + 1) * 96]
        if d % 2 == 0:
            w_keep[d // 2] = total
        else:
            w_send[d // 2] = total.astype(low)


def up_mid_kernel(w_keep, came, w_own, w_next):
    w_own[...] = w_keep[0] + came[0].astype(wide)
    w_next[...] = (w_keep[1] + came[1].astype(wide)).astype(low)


def final_send_kernel(z_own, z_next, z_came, w_own, w_came, f0, f1, f2, f3, buf):
    me = here()[0]
    came = z_came[...].astype(wide)
    ins = z_own[...] + came[0:168]
    ups = w_own[...] + w_came[...].astype(wide)
    hi, lo = split_pair(pair_sum(z_next[...].astype(wide), came, 168))
    sums = [hi.astype(wide), lo.astype(wide)]
    rest = jnp.zeros((24, SPLIT), wide)
    for j in range(4):
        lanes = slice(j * SPLIT, (j + 1) * SPLIT)
        wide_rows = [ins[i * 24 : (i + 1) * 24, lanes] for i in range(3)] + [rest]
        block = [ups[j * 24 : (j + 1) * 24], jnp.concatenate(wide_rows, axis=1)]
        block += [ins[72 + j * 24 : 96 + j * 24]] + sums
        buf[j ^ me] = jnp.concatenate(block, axis=0).astype(low)
    for r, f in enumerate((f0, f1, f2, f3)):
        f[...] = buf[r]


def final_kernel(
    lengths, f0, f1, f2, f3, in_total, up_total, out_total, first, query, value, output, second, up_bias, down, stats, buf
):
    me = here()[0]
    for r, f in enumerate((f0, f1, f2, f3)):
        buf[r ^ me] = f[...].astype(wide)
    total = buf[0, 72:84] + buf[0, 84:96]
    for j in (1, 2, 3):
        total = total + (buf[j, 72:84] + buf[j, 84:96])
    first[...] = total[0]
    query[...] = total[1]
    value[...] = total[2]
    output[...] = total[3, :DC]
    second[...] = total[4]
    for i in range(4):
        up_bias[i * D : (i + 1) * D] = total[5 + i]
    down[...] = total[9, :DC]
    count = lengths[0, 0] + lengths[0, 1]
    for b in (1, 2, 3):
        count = count + lengths[b, 0] + lengths[b, 1]
    stats[...] = total[10, :2] / count.astype(wide)
    out_total[...] = (buf[0, 48:72] + buf[1, 48:72] + buf[2, 48:72] + buf[3, 48:72])[:, :DC]
    for j in range(4):
        up_total[:, j * D : (j + 1) * D] = buf[j, 0:24, :]
    for i in range(3):
        piece = jnp.concatenate([buf[j, 24:48, i * SPLIT : (i + 1) * SPLIT] for j in range(4)], axis=1)
        in_total[:, i * D : (i + 1) * D] = piece


def home_kernel(x0, x1, x2, x3, weight, resid, gain, middle_grad, out, buf):
    me = here()[0]
    for r, x in enumerate((x0, x1, x2, x3)):
        buf[r ^ me, 0:80, :] = x[192:272, 0:384]
        buf[r ^ me, 80:160, :] = x[192:272, 384:768]
        buf[r ^ me, 160:240, :] = x[272:352, 0:384]
    e = jnp.zeros((160, D), wide)
    for i in range(3):
        g = jnp.concatenate([unpacked(buf[j, i * 80 : (i + 1) * 80, :]) for j in range(4)], axis=1)
        e = e + nt(g.astype(low), weight[:, i * D : (i + 1) * D])
    full = full_of(resid[...].astype(wide))
    root = jnp.sqrt(jnp.mean(full * full, axis=1, keepdims=True) + epsilon)
    n = full / root
    eg = e * row(gain)
    f = (eg - n * jnp.mean(eg * n, axis=1, keepdims=True)) / root
    lane = lax.broadcasted_iota(jnp.int32, (160, D), 1)
    last = jnp.sum(jnp.where(lane == D - 1, f, 0.0), axis=1, keepdims=True)
    out[...] = (middle_grad[...] + f - last)[:, :DC].astype(low)


def down_sum_kernel(x0, x1, x2, x3, own, other):
    total = x0[0:192, :].astype(wide)
    for x in (x1, x2, x3):
        total = total + x[0:192, :].astype(wide)
    own[...] = total[0:96]
    other[...] = total[96:192].astype(low)


def down_final_kernel(own, came, down_total):
    down_total[...] = (own[...] + came[...].astype(wide))[:, :DC]

def swap_chip(block, step):
    return lax.ppermute(block, "blk", [(k, k ^ (2 * step)) for k in range(8)])


def swap_core(block):
    return lax.ppermute(block, "blk", [(k, k ^ 1) for k in range(8)])


def shift_bucket(block, step):
    return lax.ppermute(block, "bucket", [(b, b ^ step) for b in range(4)])


def exchange(blocks):
    got = {r: swap_chip(blocks[r], r) for r in (3, 1, 2)}
    return [blocks[0], got[1], got[2], got[3]]


def after(values, *others):
    return lax.optimization_barrier((tuple(values), others))[0]


def body(
    residual_in,
    out_cotangent,
    first_gain,
    input_weight,
    query_bias,
    value_bias,
    output_weight,
    output_bias,
    second_gain,
    up_weight,
    up_bias,
    down_weight,
    down_bias,
    lengths,
    offsets,
    span_order,
):
    where = [span_order, offsets, lengths]
    packed_block = ((240, 2 * SPLIT), low)
    token = ((160, D), low)
    s0, s1, s2, s3, hidden, root_one = call(
        entry_kernel,
        [packed_block] * 4 + [token, ((160, 1), wide)],
        [residual_in, first_gain, input_weight, query_bias, value_bias],
        [
            pltpu.VMEM((4, 240, 2 * SPLIT), low),
            pltpu.VMEM((160, DC), low),
            pltpu.VMEM((D,), wide),
            pltpu.VMEM((3, D, D), low),
            pltpu.VMEM((D,), wide),
            pltpu.VMEM((D,), wide),
            pltpu.SemaphoreType.DMA((7,)),
        ],
        extra=60,
        far=range(5),
    )
    got = exchange([s0, s1, s2, s3])
    (push,) = call(push_kernel, [((160, FF), wide)], [out_cotangent, down_weight])
    hiddens = exchange([hidden] * 4)
    got = list(after(got, push))
    query, own_both = call(assemble_kernel, [((640, SPLIT), low), ((640, 2 * SPLIT), low)], got)
    sib_both = swap_core(own_both)
    backed = ((80, 2 * SPLIT), low)
    chance, attended, b0, b1, b2, b3 = call(
        forward_kernel,
        [((3, 640, 1280), low), ((640, SPLIT), wide)] + [backed] * 4,
        where + [query, own_both, sib_both],
        [pltpu.VMEM((1280, SPLIT), low), pltpu.VMEM((3, 1280, SPLIT), low), pltpu.VMEM((640, 1280), wide)],
        small=3,
        work=7,
    )
    back = exchange([b0, b1, b2, b3])
    (cot,) = after([out_cotangent], b0)
    cots = [out_cotangent, shift_bucket(cot, 1)]
    back = list(after(back, *hiddens[1:]))
    (columns,) = call(columns_kernel, [((D, 3 * SPLIT), low)], after([input_weight], b0))
    outs = call(
        middle_kernel,
        [backed] * 4
        + [((320, D), low)] * 6
        + [token, ((160, DC), wide), ((160, D), wide), ((16, D), wide)],
        where
        + back
        + [output_weight, output_bias, residual_in, root_one, out_cotangent, second_gain]
        + [up_weight, up_bias, push],
        [pltpu.VMEM((4, 80, 2 * SPLIT), low), pltpu.VMEM((4, 160, D), low), pltpu.VMEM((4, 320, D), low)],
        small=3,
    )
    act_keep, act_send = outs[4:6]
    lates = list(outs[6:10])
    branch_own, middle, middle_grad, vector = outs[10:]
    grads = exchange(outs[:4])
    grads = list(after(grads, cots[1]))
    (residual_out,) = call(
        closing_kernel,
        [((160, DC), low)],
        [act_keep, act_send, down_weight, middle, down_bias],
    )
    act_came = shift_bucket(act_send, 1)
    lates = exchange(after(lates, *grads[1:]))
    query_grad, both_grad, *away = call(
        backward_kernel,
        [((640, SPLIT), low), ((640, 2 * SPLIT), wide)] + [((320, 2 * SPLIT), low)] * 2,
        grads + [query, own_both, sib_both, chance, attended],
        [
            pltpu.VMEM((3, 1280, SPLIT), low),
            pltpu.VMEM((1280, SPLIT), low),
            pltpu.VMEM((640, SPLIT), low),
            pltpu.VMEM((640, 1280), low),
        ],
    )
    arrived = [swap_core(x) for x in after(away, act_came)]
    arrived = list(after(arrived, lates[1], lates[2]))
    outs = call(
        late_kernel,
        [packed_block] * 4 + [((4, 192, D), low), ((4, 168, D), wide), ((1504, D), low)],
        [query_grad, both_grad] + arrived + hiddens + [act_keep, act_came] + cots + back + [branch_own, columns, first_gain, vector],
        [
            pltpu.VMEM((640, D), low),
            pltpu.VMEM((640, D), low),
            pltpu.VMEM((640, 3 * SPLIT), low),
            pltpu.VMEM((2, 4, 192, D), low),
            pltpu.VMEM((2, 4, 168, D), wide),
        ],
    )
    homes = list(outs[:4])
    keep_x, keep_z, send = outs[4:]
    outs = call(
        late_sum_kernel,
        [((352, D), low)] * 4 + [((336, D), wide), ((368, D), low)],
        [keep_x, keep_z, send, swap_core(send)] + homes,
    )
    home = exchange(outs[:4])
    z_keep, z_send = outs[4:]
    z_own, z_next = call(
        late_mid_kernel,
        [((168, D), wide), ((192, D), low)],
        [z_keep, z_send, shift_bucket(z_send, 1)],
    )
    z_came = shift_bucket(z_next, 2)
    keep, *send = call(
        up_grad_kernel,
        [((4, 96, D), low)] + [((128, D), low)] * 3,
        lates,
        [pltpu.VMEM((640, D), low), pltpu.VMEM((640, D), low), pltpu.VMEM((2, 4, 96, D), low)],
    )
    w_keep, w_send = call(
        up_sum_kernel,
        [((2, 96, D), wide), ((2, 96, D), low)],
        [keep] + [swap_core(x) for x in send],
    )
    w_own, w_next = call(
        up_mid_kernel,
        [((96, D), wide), ((96, D), low)],
        [w_keep, shift_bucket(w_send, 1)],
    )
    w_came = shift_bucket(w_next, 2)
    finals = call(
        final_send_kernel,
        [((96, D), low)] * 4,
        [z_own, z_next, z_came, w_own, w_came],
        [pltpu.VMEM((4, 96, D), low)],
    )
    down_own, down_other = call(down_sum_kernel, [((96, D), wide), ((96, D), low)], home)
    (down_total,) = call(
        down_final_kernel, [((96, DC), wide)], [down_own, shift_bucket(down_other, 2)]
    )
    (residual_grad,) = call(
        home_kernel,
        [((160, DC), low)],
        home + [input_weight, residual_in, first_gain, middle_grad],
        [pltpu.VMEM((4, 240, 2 * SPLIT), low)],
    )
    in_total, up_total, out_total, first, query_sum, value_sum, output, second, up_sum_bias, down, stats = call(
        final_kernel,
        [((24, 3 * D), wide), ((24, FF), wide), ((24, DC), wide)]
        + [((D,), wide)] * 3
        + [((DC,), wide), ((D,), wide), ((FF,), wide), ((DC,), wide), ((2,), wide)],
        [lengths] + exchange(finals),
        [pltpu.VMEM((4, 96, D), wide)],
        small=1,
    )
    return (
        residual_out,
        residual_grad,
        first,
        in_total,
        query_sum,
        value_sum,
        out_total,
        output,
        second,
        up_total,
        up_sum_bias,
        down_total,
        down,
        stats,
    )


def solution(mesh):
    placed = (
        P(("bucket", "blk"), None),
        P(("bucket", "blk"), None),
        P(),
        P(),
        P(),
        P(),
        P(),
        P(),
        P(),
        P(),
        P(),
        P(),
        P(),
        P(),
        P("bucket", None),
        P(),
    )
    return jax.shard_map(
        body if dict(mesh.shape) == {"bucket": 4, "blk": 8} else general_body,
        mesh=mesh,
        in_specs=placed,
        out_specs=(
            P(("bucket", "blk"), None),
            P(("bucket", "blk"), None),
            P(),
            P(("bucket", "blk"), None),
            P(),
            P(),
            P(("bucket", "blk"), None),
            P(),
            P(),
            P(("bucket", "blk"), None),
            P(),
            P(("bucket", "blk"), None),
            P(),
            P(),
        ),
        check_vma=False,
    )
```

```python
import jax
import jax.numpy as jnp
from jax import lax
from jax.experimental import pallas as pl
from jax.experimental.pallas import tpu as pltpu
from jax.sharding import PartitionSpec as P

D = 768
HEADS = 12
HEAD_DIM = 64


epsilon = 1e-05
masked_value = -1e30


def center_norm(resid, gain):
    full = jnp.concatenate([resid, -jnp.sum(resid, axis=1, keepdims=True)], axis=1)
    root = jnp.sqrt(jnp.mean(full * full, axis=1, keepdims=True) + epsilon)
    return (full / root * gain, root[:, 0])


def gelu_tanh(inputs):
    return jax.nn.gelu(inputs, approximate=True)


def heads_of(block):
    return block.reshape(block.shape[0], HEADS, HEAD_DIM)


def places_of(span_order, begin, count, half_rows):
    spans = lax.dynamic_slice_in_dim(span_order, begin // half_rows, count // half_rows)
    inner = jnp.arange(half_rows, dtype=jnp.int32)
    return (spans[:, None] * half_rows + inner[None, :]).reshape(count)


def documents_of(places, lengths, offsets):
    first_in = (places >= offsets[0, 0]) & (places < offsets[0, 0] + lengths[0, 0])
    second_in = (places >= offsets[0, 1]) & (places < offsets[0, 1] + lengths[0, 1])
    return jnp.where(first_in, 0, jnp.where(second_in, 1, -1)).astype(jnp.int32)


def allowed_of(query_places, query_docs, key_places, key_docs):
    same = (query_docs[:, None] == key_docs[None, :]) & (query_docs[:, None] >= 0)
    return (same & (key_places[None, :] <= query_places[:, None]))[None]


def block_shape(count, unit):
    shards = count // unit
    width = max(1, 1024 // unit)
    while shards % width != 0:
        width = width - 1
    return (shards // width, width * unit)


def general_body(
    residual_in,
    out_cotangent,
    first_gain,
    input_weight,
    query_bias,
    value_bias,
    output_weight,
    output_bias,
    second_gain,
    up_weight,
    up_bias,
    down_weight,
    down_bias,
    lengths,
    offsets,
    span_order,
):
    rows = residual_in.shape[0]
    half_rows = rows // 2
    score_scale = HEAD_DIM ** (-0.5)
    index = lax.axis_index("blk")
    bucket_index = lax.axis_index("bucket")
    own_lengths = lax.dynamic_slice_in_dim(lengths, bucket_index, 1, 0)
    valid_count = jnp.sum(lengths.astype(jnp.float32))
    query_places = places_of(span_order, index * rows, rows, half_rows)
    query_docs = documents_of(query_places, own_lengths, offsets)
    valid = (query_docs >= 0).astype(jnp.float32)
    resid = residual_in.astype(jnp.float32)
    normed, first_back, first_root = jax.vjp(center_norm, resid, first_gain, has_aux=True)
    hidden_in = normed.astype(jnp.bfloat16)
    projected = jnp.dot(hidden_in, input_weight, preferred_element_type=jnp.float32)
    query = (projected[:, :D] + query_bias).astype(jnp.bfloat16)
    keys = projected[:, D : 2 * D].astype(jnp.bfloat16)
    values = (projected[:, 2 * D :] + value_bias).astype(jnp.bfloat16)
    query_heads = heads_of(query)
    key_heads = heads_of(keys)
    value_heads = heads_of(values)
    initial = (
        jnp.full((HEADS, rows), masked_value, jnp.float32),
        jnp.zeros((HEADS, rows), jnp.float32),
        jnp.zeros((HEADS, rows, HEAD_DIM), jnp.float32),
    )
    state = initial
    key_piece = lax.all_gather(keys, "blk", axis=0, tiled=True)
    value_piece = lax.all_gather(values, "blk", axis=0, tiled=True)
    count = key_piece.shape[0]
    number, width = block_shape(count, rows)
    key_places = places_of(span_order, jnp.int32(0), count, half_rows)
    key_docs = documents_of(key_places, own_lengths, offsets)

    def forward_advance(state, parts):
        key_block, value_block, places_block, docs_block = parts
        peak, total, summed = state
        scores = (
            jnp.einsum(
                "qhd,khd->hqk", query_heads, heads_of(key_block), preferred_element_type=jnp.float32
            )
            * score_scale
        )
        allowed = allowed_of(query_places, query_docs, places_block, docs_block)
        masked = jnp.where(allowed, scores, masked_value)
        new_peak = jnp.maximum(peak, jnp.max(masked, axis=2))
        decay = jnp.exp(peak - new_peak)
        weights = jnp.where(allowed, jnp.exp(masked - new_peak[:, :, None]), 0.0)
        total = total * decay + jnp.sum(weights, axis=2)
        summed = summed * decay[:, :, None] + jnp.einsum(
            "hqk,khd->hqd",
            weights.astype(jnp.bfloat16),
            heads_of(value_block),
            preferred_element_type=jnp.float32,
        )
        return ((new_peak, total, summed), None)

    state, _ = lax.scan(
        forward_advance,
        state,
        (
            key_piece.reshape(number, width, D),
            value_piece.reshape(number, width, D),
            key_places.reshape(number, width),
            key_docs.reshape(number, width),
        ),
    )
    peak, total, summed = state
    denominator = total + 1.0 - valid[None, :]
    attended = summed / denominator[:, :, None]
    log_total = peak + jnp.log(denominator)
    mixed = attended.transpose(1, 0, 2).reshape(rows, D).astype(jnp.bfloat16)
    branch = jnp.dot(mixed, output_weight, preferred_element_type=jnp.float32) + output_bias
    middle = resid + branch
    normed_two, second_back, second_root = jax.vjp(center_norm, middle, second_gain, has_aux=True)
    hidden_two = normed_two.astype(jnp.bfloat16)
    upward = jnp.dot(hidden_two, up_weight, preferred_element_type=jnp.float32) + up_bias
    active_float, gelu_back = jax.vjp(gelu_tanh, upward)
    active = active_float.astype(jnp.bfloat16)
    closing = jnp.dot(active, down_weight, preferred_element_type=jnp.float32) + down_bias
    residual_out = (middle + closing).astype(jnp.bfloat16)
    stat_sums = jnp.stack([jnp.sum(valid * first_root), jnp.sum(valid * second_root)])
    stat_sums = lax.psum(stat_sums, ("bucket", "blk"))
    cotangent = out_cotangent.astype(jnp.float32)
    down_grad = jnp.einsum("rf,rc->fc", active, out_cotangent, preferred_element_type=jnp.float32)
    down_bias_grad = jnp.sum(cotangent, axis=0)
    active_grad = jnp.einsum(
        "rc,fc->rf", out_cotangent, down_weight, preferred_element_type=jnp.float32
    )
    (upward_float,) = gelu_back(active_grad)
    upward_grad = upward_float.astype(jnp.bfloat16)
    up_grad = jnp.einsum("rd,rf->df", hidden_two, upward_grad, preferred_element_type=jnp.float32)
    up_bias_grad = jnp.sum(upward_grad.astype(jnp.float32), axis=0)
    hidden_two_grad = jnp.einsum(
        "rf,df->rd", upward_grad, up_weight, preferred_element_type=jnp.float32
    )
    middle_part, second_gain_grad = second_back(hidden_two_grad)
    middle_grad = cotangent + middle_part
    branch_grad = middle_grad.astype(jnp.bfloat16)
    output_grad = jnp.einsum("rd,rc->dc", mixed, branch_grad, preferred_element_type=jnp.float32)
    output_bias_grad = jnp.sum(branch_grad.astype(jnp.float32), axis=0)
    attended_grad = jnp.einsum(
        "rc,dc->rd", branch_grad, output_weight, preferred_element_type=jnp.float32
    ).astype(jnp.bfloat16)
    grad_heads = heads_of(attended_grad)
    delta = jnp.einsum("rhd,hrd->hr", grad_heads.astype(jnp.float32), attended)
    query_zero = jnp.zeros((rows, HEADS, HEAD_DIM), jnp.float32)
    accum = query_zero
    key_piece = lax.all_gather(keys, "blk", axis=0, tiled=True)
    value_piece = lax.all_gather(values, "blk", axis=0, tiled=True)
    count = key_piece.shape[0]
    number, width = block_shape(count, rows)
    key_places = places_of(span_order, jnp.int32(0), count, half_rows)
    key_docs = documents_of(key_places, own_lengths, offsets)

    def query_advance(accum, parts):
        key_block, value_block, places_block, docs_block = parts
        block_keys = heads_of(key_block)
        scores = (
            jnp.einsum("qhd,khd->hqk", query_heads, block_keys, preferred_element_type=jnp.float32)
            * score_scale
        )
        allowed = allowed_of(query_places, query_docs, places_block, docs_block)
        chance = jnp.where(
            allowed, jnp.exp(jnp.where(allowed, scores, masked_value) - log_total[:, :, None]), 0.0
        )
        push = jnp.einsum(
            "qhd,khd->hqk", grad_heads, heads_of(value_block), preferred_element_type=jnp.float32
        )
        slope = (chance * (push - delta[:, :, None])).astype(jnp.bfloat16)
        accum = (
            accum
            + jnp.einsum("hqk,khd->qhd", slope, block_keys, preferred_element_type=jnp.float32)
            * score_scale
        )
        return (accum, None)

    accum, _ = lax.scan(
        query_advance,
        accum,
        (
            key_piece.reshape(number, width, D),
            value_piece.reshape(number, width, D),
            key_places.reshape(number, width),
            key_docs.reshape(number, width),
        ),
    )
    log_all, delta_all = (
        lax.all_gather(log_total.T, "blk", axis=0, tiled=True),
        lax.all_gather(delta.T, "blk", axis=0, tiled=True),
    )
    key_zero = jnp.zeros((rows, HEADS, HEAD_DIM), jnp.float32)
    state = (key_zero, key_zero)
    begin = jnp.int32(0)
    query_piece = lax.all_gather(query, "blk", axis=0, tiled=True)
    grad_piece = lax.all_gather(attended_grad, "blk", axis=0, tiled=True)
    count = query_piece.shape[0]
    number, width = block_shape(count, rows)
    piece_places = places_of(span_order, begin, count, half_rows)
    piece_docs = documents_of(piece_places, own_lengths, offsets)
    piece_log = lax.dynamic_slice_in_dim(log_all, begin, count, 0)
    piece_delta = lax.dynamic_slice_in_dim(delta_all, begin, count, 0)

    def key_advance(state, parts):
        query_block, grad_block, places_block, docs_block, log_block, delta_block = parts
        key_sum, value_sum = state
        block_query = heads_of(query_block)
        block_grad = heads_of(grad_block)
        scores = (
            jnp.einsum("qhd,khd->hqk", block_query, key_heads, preferred_element_type=jnp.float32)
            * score_scale
        )
        allowed = allowed_of(places_block, docs_block, query_places, query_docs)
        chance = jnp.where(
            allowed,
            jnp.exp(jnp.where(allowed, scores, masked_value) - log_block.T[:, :, None]),
            0.0,
        )
        value_sum = value_sum + jnp.einsum(
            "hqk,qhd->khd",
            chance.astype(jnp.bfloat16),
            block_grad,
            preferred_element_type=jnp.float32,
        )
        push = jnp.einsum(
            "qhd,khd->hqk", block_grad, value_heads, preferred_element_type=jnp.float32
        )
        slope = (chance * (push - delta_block.T[:, :, None])).astype(jnp.bfloat16)
        key_sum = (
            key_sum
            + jnp.einsum("hqk,qhd->khd", slope, block_query, preferred_element_type=jnp.float32)
            * score_scale
        )
        return ((key_sum, value_sum), None)

    state, _ = lax.scan(
        key_advance,
        state,
        (
            query_piece.reshape(number, width, D),
            grad_piece.reshape(number, width, D),
            piece_places.reshape(number, width),
            piece_docs.reshape(number, width),
            piece_log.reshape(number, width, HEADS),
            piece_delta.reshape(number, width, HEADS),
        ),
    )
    key_sum, value_sum = state
    query_low = accum.reshape(rows, D).astype(jnp.bfloat16)
    key_low = key_sum.reshape(rows, D).astype(jnp.bfloat16)
    value_low = value_sum.reshape(rows, D).astype(jnp.bfloat16)
    projected_grad = jnp.concatenate([query_low, key_low, value_low], axis=1)
    input_grad = jnp.einsum(
        "rd,re->de", hidden_in, projected_grad, preferred_element_type=jnp.float32
    )
    query_bias_grad = jnp.sum(query_low.astype(jnp.float32), axis=0)
    value_bias_grad = jnp.sum(value_low.astype(jnp.float32), axis=0)
    hidden_in_grad = jnp.einsum(
        "re,de->rd", projected_grad, input_weight, preferred_element_type=jnp.float32
    )
    resid_part, first_gain_grad = first_back(hidden_in_grad)
    residual_grad = (middle_grad + resid_part).astype(jnp.bfloat16)
    input_part, output_part, up_part, down_part = (
        lax.psum_scatter(input_grad, ("bucket", "blk"), scatter_dimension=0, tiled=True),
        lax.psum_scatter(output_grad, ("bucket", "blk"), scatter_dimension=0, tiled=True),
        lax.psum_scatter(up_grad, ("bucket", "blk"), scatter_dimension=0, tiled=True),
        lax.psum_scatter(down_grad, ("bucket", "blk"), scatter_dimension=0, tiled=True),
    )
    (
        first_sum,
        query_sum_bias,
        value_sum_bias,
        output_sum_bias,
        second_sum,
        up_sum_bias,
        down_sum_bias,
    ) = lax.psum(
        (
            first_gain_grad,
            query_bias_grad,
            value_bias_grad,
            output_bias_grad,
            second_gain_grad,
            up_bias_grad,
            down_bias_grad,
        ),
        ("bucket", "blk"),
    )
    mean_norms = stat_sums / valid_count
    return (
        residual_out,
        residual_grad,
        first_sum,
        input_part,
        query_sum_bias,
        value_sum_bias,
        output_part,
        output_sum_bias,
        second_sum,
        up_part,
        up_sum_bias,
        down_part,
        down_sum_bias,
        mean_norms,
    )


DC = 767
SPLIT = 192
FF = 3072
low = jnp.bfloat16
wide = jnp.float32
VMEM = pl.BlockSpec(memory_space=pltpu.VMEM)
SMEM = pl.BlockSpec(memory_space=pltpu.SMEM)
HBM = pl.BlockSpec(memory_space=pltpu.HBM)

def padded_bytes(shape, dtype):
    shape = (1, 1) + tuple(shape)
    size = jnp.dtype(dtype).itemsize
    rows, lanes = -(-shape[-2] // 16) * 16, -(-shape[-1] // 128) * 128
    for d in shape[:-2]:
        rows = rows * d
    return rows * lanes * size


def call(kernel, outs, ins, scratch=(), extra=6, small=0, far=(), work=0):
    shapes = [jax.ShapeDtypeStruct(s, d) for s, d in outs]
    held = [(s, d) for s, d in outs]
    held += [(x.shape, x.dtype) for i, x in enumerate(ins) if i >= small and i not in far]
    held += [(s.shape, s.dtype) for s in scratch if s.memory_space == pltpu.VMEM]
    limit = sum(padded_bytes(s, d) for s, d in held) + extra * 2**20
    return pl.pallas_call(
        kernel,
        out_shape=shapes,
        in_specs=[SMEM if i < small else HBM if i in far else VMEM for i in range(len(ins))],
        out_specs=[VMEM] * len(outs),
        scratch_shapes=list(scratch),
        compiler_params=pltpu.CompilerParams(vmem_limit_bytes=min(limit, 60 * 2**20)),
        cost_estimate=pl.CostEstimate(
            flops=int(1000 + work * 1.1e9),
            bytes_accessed=1000,
            transcendentals=0,
        ),
    )(*ins)


def here():
    index = lax.axis_index("blk")
    return index // 2, lax.axis_index("bucket"), index % 2


def full_of(x):
    rows=x.shape[0]
    wide_x=jnp.concatenate([x,jnp.zeros((rows,1),x.dtype)],axis=1)
    last=lax.broadcasted_iota(jnp.int32,(rows,D),1)==D-1
    return jnp.where(last,-jnp.sum(x,axis=1,keepdims=True),wide_x)

def row(ref):
    return ref[...].reshape(1, ref.shape[0])


def nt(a, b):
    return lax.dot_general(a, b, (((1,), (1,)), ((), ())), preferred_element_type=wide)


def tn(a, b):
    return lax.dot_general(a, b, (((0,), (0,)), ((), ())), preferred_element_type=wide)


def packed(x):
    half = x.shape[0] // 2
    return jnp.concatenate([x[:half], x[half:]], axis=1).astype(low)


def unpacked(x):
    x = x.astype(wide)
    half = x.shape[1] // 2
    return jnp.concatenate([x[:, :half], x[:, half:]], axis=0)


def split_pair(x):
    hi = x.astype(low)
    return hi, (x - hi.astype(wide)).astype(low)


def head_mask(x, h):
    lane = lax.broadcasted_iota(jnp.int32, x.shape, 1)
    return jnp.where((lane >= h * 64) & (lane < (h + 1) * 64), x, jnp.zeros_like(x))


def limits(spans, offsets, lengths, bucket, chip, core, half):
    place = spans[chip * 4 + core * 2 + half] * 80 + lax.broadcasted_iota(jnp.int32, (80, 1), 0)
    one, two = offsets[0, 0], offsets[0, 1]
    first = (place >= one) & (place < one + lengths[bucket, 0])
    second = (place >= two) & (place < two + lengths[bucket, 1])
    return jnp.where(first, one, two), jnp.where(first | second, place, -1)


def entry_kernel(
    resid_far, gain_far, weight_far, qbias_far, vbias_far, s0, s1, s2, s3, hidden_out, root_out,
    buf, resid, gain, weight, qbias, vbias, sems,
):
    me = here()[0]
    copies = [
        pltpu.make_async_copy(a, b, sems.at[i])
        for i, (a, b) in enumerate(
            [(resid_far, resid), (gain_far, gain), (qbias_far, qbias), (vbias_far, vbias)]
            + [(weight_far.at[:, pl.ds(i * D, D)], weight.at[i]) for i in range(3)]
        )
    ]
    for copy in copies:
        copy.start()
    copies[0].wait()
    full = full_of(resid[...].astype(wide))
    root = jnp.sqrt(jnp.mean(full * full, axis=1, keepdims=True) + epsilon)
    root_out[...] = root
    copies[1].wait()
    hidden = (full / root * row(gain)).astype(low)
    hidden_out[...] = hidden
    copies[2].wait()
    copies[3].wait()
    for i in range(3):
        copies[4 + i].wait()
        p = jnp.dot(hidden, weight[i], preferred_element_type=wide)
        if i == 0:
            p = (p + row(qbias)) * 0.125
        if i == 2:
            p = p + row(vbias)
        for j in range(4):
            buf[j ^ me, i * 80 : (i + 1) * 80, :] = packed(p[:, j * SPLIT : (j + 1) * SPLIT])
    for r, s in enumerate((s0, s1, s2, s3)):
        s[...] = buf[r]


def push_kernel(cot, weight, out):
    for i in range(4):
        out[:, i * D : (i + 1) * D] = nt(cot[...], weight[i * D : (i + 1) * D, :])


def columns_kernel(weight, out):
    me = here()[0]
    for j in range(4):

        @pl.when(me == j)
        def _():
            for i in range(3):
                piece = weight[:, i * D + j * SPLIT : i * D + (j + 1) * SPLIT].astype(wide)
                out[:, i * SPLIT : (i + 1) * SPLIT] = piece.astype(low)


def assemble_kernel(p0, p1, p2, p3, query, both):
    for r, p in enumerate((p0, p1, p2, p3)):
        rows = slice(r * 160, (r + 1) * 160)
        query[rows, :] = unpacked(p[0:80, :]).astype(low)
        both[rows, :SPLIT] = unpacked(p[80:160, :]).astype(low)
        both[rows, SPLIT:] = unpacked(p[160:240, :]).astype(low)


def forward_kernel(
    spans, offsets, lengths, query, own, sib, chance, attended, b0, b1, b2, b3, keys, vals, scores, lows, highs
):
    me, bucket, core = here()
    keys[:640, :] = own[:, :SPLIT]
    keys[640:, :] = sib[:, :SPLIT]
    v = jnp.concatenate([own[:, SPLIT:].astype(wide), sib[:, SPLIT:].astype(wide)], axis=0)
    for h in range(3):
        vals[h] = head_mask(v, h).astype(low)
    lane = lax.broadcasted_iota(jnp.int32, (1, 1280), 1)
    place = lane
    for blk in range(16):
        chip = ((blk % 8) // 2) ^ me
        span = spans[chip * 4 + (core ^ (blk // 8)) * 2 + blk % 2]
        place = jnp.where((lane >= blk * 80) & (lane < (blk + 1) * 80), lane + (span - blk) * 80, place)
    for blk in range(8):
        rows = slice(blk * 80, (blk + 1) * 80)
        lo, hi = limits(spans, offsets, lengths, bucket, (blk // 2) ^ me, core, blk % 2)
        lows[rows, :] = lo
        highs[rows, :] = hi
    q = query[...].astype(wide)
    for h in range(3):
        scores[...] = nt(head_mask(q, h).astype(low), keys[...])
        for blk in range(8):
            rows = slice(blk * 80, (blk + 1) * 80)
            lo, hi = lows[rows, :], highs[rows, :]
            s = jnp.where((place >= lo) & (place <= hi), scores[rows, :], masked_value)
            peak = jnp.max(s, axis=1, keepdims=True)
            w = jnp.exp(s - peak)
            total = jnp.sum(w, axis=1, keepdims=True)
            chance[h, rows, :] = (w * jnp.where(hi >= 0, 1.0 / total, 0.0)).astype(low)
        part = jnp.dot(chance[h], vals[h], preferred_element_type=wide)
        if h == 0:
            attended[...] = part
        else:
            attended[...] += part
    acc = attended[...]
    for r, b in enumerate((b0, b1, b2, b3)):
        b[...] = packed(acc[r * 160 : (r + 1) * 160])


def middle_kernel(
    spans, offsets, lengths, p0, p1, p2, p3, out_weight, out_bias, resid, root_in, cot, gain, up_weight, up_bias, push,
    d0, d1, d2, d3, act_keep, act_send, n0, n1, n2, n3, branch_own, middle, middle_grad, vector,
    dbuf, abuf, nbuf,
):
    me, bucket, core = here()
    branch = row(out_bias)
    for r, p in enumerate((p0, p1, p2, p3)):
        w = out_weight[pl.ds(pl.multiple_of((me ^ r) * SPLIT, SPLIT), SPLIT), :]
        branch = branch + jnp.dot(unpacked(p[...]).astype(low), w, preferred_element_type=wide)
    mid = resid[...].astype(wide) + branch
    middle[...] = mid
    full = full_of(mid)
    root = jnp.sqrt(jnp.mean(full * full, axis=1, keepdims=True) + epsilon)
    n = full / root
    hidden = (n * row(gain)).astype(low)
    for r in range(4):
        nbuf[r, 0:160, :] = hidden
    e = jnp.zeros((160, D), wide)
    c = 0.7978845608028654
    up_sums = []
    for blk in range(4):
        cols = slice(blk * D, (blk + 1) * D)
        u = jnp.dot(hidden, up_weight[:, cols], preferred_element_type=wide) + up_bias[cols].reshape(1, D)
        t = jnp.tanh(c * (u + 0.044715 * u * u * u))
        abuf[blk ^ bucket] = (0.5 * u * (1.0 + t)).astype(low)
        slope = 0.5 * (1.0 + t) + 0.5 * u * (1.0 - t * t) * (c * (1.0 + 3 * 0.044715 * u * u))
        g = (push[:, cols] * slope).astype(low)
        nbuf[blk ^ me, 160:320, :] = g
        up_sums.append(jnp.sum(g.astype(wide), axis=0, keepdims=True))
        e = e + nt(g, up_weight[:, cols])
    gain_sum = jnp.sum(e * n, axis=0, keepdims=True)
    eg = e * row(gain)
    f = (eg - n * jnp.mean(eg * n, axis=1, keepdims=True)) / root
    cot_wide = jnp.concatenate([cot[...].astype(wide), jnp.zeros((160, 1), wide)], axis=1)
    lane = lax.broadcasted_iota(jnp.int32, (160, D), 1)
    last = jnp.sum(jnp.where(lane == D - 1, f, 0.0), axis=1, keepdims=True)
    grad = jnp.where(lane == D - 1, 0.0, cot_wide + f - last)
    middle_grad[...] = grad
    grad_low = grad.astype(low)
    grad_wide = grad_low.astype(wide)
    branch_own[...] = grad_low
    back = nt(grad_wide[:, :DC].astype(low), out_weight[...])
    for j in range(4):
        dbuf[j ^ me] = packed(back[:, j * SPLIT : (j + 1) * SPLIT])
    for r in range(4):
        (d0, d1, d2, d3)[r][...] = dbuf[r]
        (act_keep, act_send)[r % 2][r // 2 * 160 : r // 2 * 160 + 160, :] = abuf[r]
        (n0, n1, n2, n3)[r][...] = nbuf[r]
    ends = [limits(spans, offsets, lengths, bucket, me, core, half)[1] for half in range(2)]
    valid = jnp.where(jnp.concatenate(ends, axis=0) >= 0, 1.0, 0.0)
    one = jnp.sum(valid * root_in[...], axis=0, keepdims=True)
    two = jnp.sum(valid * root, axis=0, keepdims=True)
    at = lax.broadcasted_iota(jnp.int32, (1, D), 1)
    stats = jnp.where(at == 0, one, jnp.where(at == 1, two, 0.0))
    zero = jnp.zeros((1, D), wide)
    sums = [zero, zero, zero, jnp.sum(grad_wide, axis=0, keepdims=True), gain_sum] + up_sums
    sums += [jnp.sum(cot_wide, axis=0, keepdims=True), stats] + [zero] * 5
    vector[...] = jnp.concatenate(sums, axis=0)


def closing_kernel(act_keep, act_send, weight, middle, bias, out):
    bucket = here()[1]
    acc = middle[...] + row(bias)
    for d in range(4):
        w = weight[pl.ds(pl.multiple_of((bucket ^ d) * D, D), D), :]
        a = (act_keep, act_send)[d % 2][d // 2 * 160 : d // 2 * 160 + 160, :]
        acc = acc + jnp.dot(a, w, preferred_element_type=wide)
    out[...] = acc.astype(low)


def backward_kernel(
    d0, d1, d2, d3, query, own, sib, chance, attended, query_grad, both_grad, away_one, away_two,
    keys, vals, grads, slopes, keys_turned, vals_turned, pushes,
):
    for r, d in enumerate((d0, d1, d2, d3)):
        grads[r * 160 : (r + 1) * 160, :] = unpacked(d[...]).astype(low)
    k = jnp.concatenate([own[:, :SPLIT], sib[:, :SPLIT]], axis=0).astype(wide)
    for h in range(3):
        keys[h] = head_mask(k, h).astype(low)
    vals[:640, :] = own[:, SPLIT:].astype(wide).astype(low)
    vals[640:, :] = sib[:, SPLIT:].astype(wide).astype(low)
    g = grads[...].astype(wide)
    q_turned = jnp.transpose(query[...].astype(wide)).astype(low)
    g_turned = jnp.transpose(g).astype(low)
    dq = jnp.zeros((640, SPLIT), wide)
    for h in range(3):
        gh = head_mask(g, h)
        delta = jnp.sum(gh * attended[...], axis=1, keepdims=True)
        pushes[...] = nt(gh.astype(low), vals[...])
        for r in range(8):
            rows = slice(r * 80, (r + 1) * 80)
            slopes[rows, :] = (chance[h, rows, :].astype(wide) * (pushes[rows, :] - delta[rows, :])).astype(low)
        dq = dq + jnp.dot(slopes[...], keys[h], preferred_element_type=wide)
        rows = slice(h * 64, (h + 1) * 64)
        keys_turned[rows, :] = jnp.dot(q_turned[rows], slopes[...], preferred_element_type=wide)
        vals_turned[rows, :] = jnp.dot(g_turned[rows], chance[h], preferred_element_type=wide)
    query_grad[...] = (dq * 0.125).astype(low)
    dk = jnp.transpose(keys_turned[...])
    dv = jnp.transpose(vals_turned[...])
    both_grad[:, :SPLIT] = dk[:640]
    both_grad[:, SPLIT:] = dv[:640]
    away_one[:, :SPLIT] = dk[640:960].astype(low)
    away_one[:, SPLIT:] = dv[640:960].astype(low)
    away_two[:, :SPLIT] = dk[960:].astype(low)
    away_two[:, SPLIT:] = dv[960:].astype(low)


def late_kernel(
    query_grad, both_grad, arrive_one, arrive_two, i0, i1, i2, i3, act_keep, act_came, c0, c1, p0, p1, p2, p3, branch_own, columns, gain, vector,
    h0, h1, h2, h3, keep_x, keep_z, send, left, right, heads, xbuf, zbuf,
):
    me, bucket, core = here()
    arrived = jnp.concatenate([arrive_one[...].astype(wide), arrive_two[...].astype(wide)], axis=0)
    both = both_grad[...] + arrived
    parts = [query_grad[...].astype(wide), both[:, :SPLIT], both[:, SPLIT:]]
    parts = [p.astype(low).astype(wide) for p in parts]
    for r, h in enumerate((h0, h1, h2, h3)):
        left[r * 160 : (r + 1) * 160, :] = (i0, i1, i2, i3)[r][...]
        for i in range(3):
            h[i * 80 : (i + 1) * 80, :] = packed(parts[i][r * 160 : (r + 1) * 160])
    heads[...] = jnp.concatenate(parts, axis=1).astype(low)
    grad = tn(left[...], heads[...])
    sums = jnp.sum(grad * columns[...].astype(wide), axis=1, keepdims=True)
    gain_row = jnp.transpose(jnp.broadcast_to(sums, (D, 128)))[0:1] / row(gain)
    lane = lax.broadcasted_iota(jnp.int32, (1, D), 1)
    mine = (lane >= me * SPLIT) & (lane < (me + 1) * SPLIT)

    def column_sum(x):
        s = jnp.sum(x, axis=0, keepdims=True)
        return jnp.where(mine, jnp.concatenate([s] * 4, axis=1), 0.0)

    at = lax.broadcasted_iota(jnp.int32, (16, D), 0)
    total = vector[...] + jnp.where(at == 0, gain_row, 0.0)
    total = total + jnp.where(at == 1, column_sum(parts[0]), 0.0)
    total = total + jnp.where(at == 2, column_sum(parts[2]), 0.0)
    thirds = [grad[:, i * SPLIT : (i + 1) * SPLIT] for i in range(3)]
    for b in range(4):
        for c in range(2):
            block = []
            for part in thirds:
                starts = [b * 192 + j * 48 + c * 24 for j in range(4)]
                block.append(jnp.concatenate([part[s : s + 24] for s in starts], axis=1))
            zbuf[c ^ core, b ^ bucket, 0:72, :] = jnp.concatenate(block, axis=0)
    for r, p in enumerate((p0, p1, p2, p3)):
        out = tn(unpacked(p[...]).astype(low), branch_own[...])
        for j in range(4):
            for c in range(2):
                s = j * 48 + c * 24
                zbuf[c ^ core, me ^ r ^ bucket, 72 + j * 24 : 96 + j * 24, :] = out[s : s + 24]
    for d, c in enumerate((c0, c1)):
        cot = c[...].astype(wide)
        right[d * 160 : (d + 1) * 160, :] = jnp.concatenate([cot, jnp.zeros((160, 1), wide)], axis=1).astype(low)
    for half in range(2):
        left[0:160, :] = act_keep[half * 160 : half * 160 + 160, :]
        left[160:320, :] = act_came[half * 160 : half * 160 + 160, :]
        down = tn(left[0:320, :], right[0:320, :])
        for j in range(4):
            for c in range(2):
                s = j * 192 + c * 96
                xbuf[c ^ core, j ^ me, half * 96 : half * 96 + 96, :] = down[s : s + 96].astype(low)
    keep_x[...] = xbuf[0]
    for r in range(4):
        keep_z[r] = zbuf[0, r]
        send[r * 192 : (r + 1) * 192, :] = xbuf[1, r]
        block = jnp.concatenate([zbuf[1, r], jnp.zeros((8, D), wide)], axis=0)
        send[768 + r * 176 : 944 + r * 176, :] = block.astype(low)
    hi, lo = split_pair(total)
    send[1472:1488, :] = hi
    send[1488:1504, :] = lo


def late_sum_kernel(keep_x, keep_z, send, arrived, h0, h1, h2, h3, x0, x1, x2, x3, z_keep, z_send):
    own = send[1472:1488, :].astype(wide) + send[1488:1504, :].astype(wide)
    hi, lo = split_pair(own + (arrived[1472:1488, :].astype(wide) + arrived[1488:1504, :].astype(wide)))
    blocks = []
    for r in range(4):
        x, h = (x0, x1, x2, x3)[r], (h0, h1, h2, h3)[r]
        x[0:192, :] = (keep_x[r].astype(wide) + arrived[r * 192 : (r + 1) * 192, :].astype(wide)).astype(low)
        x[192:272, 0:384] = h[0:80, :]
        x[192:272, 384:768] = h[80:160, :]
        x[272:352, 0:384] = h[160:240, :]
        x[272:352, 384:768] = jnp.zeros((80, 384), low)
        came = arrived[768 + r * 176 : 944 + r * 176, :].astype(wide)
        blocks.append(keep_z[r] + came[0:168])
    z_keep[0:168, :] = blocks[0]
    z_keep[168:336, :] = blocks[2]
    sums = [hi.astype(wide)[0:12], lo.astype(wide)[0:12], jnp.zeros((8, D), wide)]
    z_send[...] = jnp.concatenate([blocks[1], blocks[3]] + sums, axis=0).astype(low)


def pair_sum(own, came, start):
    a = own[start : start + 12] + own[start + 12 : start + 24]
    b = came[start : start + 12] + came[start + 12 : start + 24]
    return a + b


def late_mid_kernel(z_keep, z_send, came, z_own, z_next):
    came = came[...].astype(wide)
    hi, lo = split_pair(pair_sum(z_send[...].astype(wide), came, 336))
    z_own[...] = z_keep[0:168, :] + came[0:168]
    block = [z_keep[168:336, :] + came[168:336], hi.astype(wide), lo.astype(wide)]
    z_next[...] = jnp.concatenate(block, axis=0).astype(low)


def up_grad_kernel(n0, n1, n2, n3, keep, send_one, send_two, send_three, left, right, buf):
    me, bucket, core = here()
    for r in range(4):
        rows = slice(r * 160, (r + 1) * 160)
        n = (n0, n1, n2, n3)[r]
        left[rows, :] = n[0:160, :]
        right[rows, :] = n[160:320, :]
    up = tn(left[...], right[...])
    for b in range(4):
        for c in range(2):
            starts = [b * 192 + j * 48 + c * 24 for j in range(4)]
            block = jnp.concatenate([up[s : s + 24] for s in starts], axis=0)
            buf[c ^ core, b ^ bucket] = block.astype(low)
    keep[...] = buf[0]
    send_one[0:96, :] = buf[1, 0]
    send_one[96:128, :] = buf[1, 1, 0:32, :]
    send_two[0:64, :] = buf[1, 1, 32:96, :]
    send_two[64:128, :] = buf[1, 2, 0:64, :]
    send_three[0:32, :] = buf[1, 2, 64:96, :]
    send_three[32:128, :] = buf[1, 3]


def up_sum_kernel(keep, arrive_one, arrive_two, arrive_three, w_keep, w_send):
    parts = [a[...].astype(wide) for a in (arrive_one, arrive_two, arrive_three)]
    arrived = jnp.concatenate(parts, axis=0)
    for d in range(4):
        total = keep[d].astype(wide) + arrived[d * 96 : (d + 1) * 96]
        if d % 2 == 0:
            w_keep[d // 2] = total
        else:
            w_send[d // 2] = total.astype(low)


def up_mid_kernel(w_keep, came, w_own, w_next):
    w_own[...] = w_keep[0] + came[0].astype(wide)
    w_next[...] = (w_keep[1] + came[1].astype(wide)).astype(low)


def final_send_kernel(z_own, z_next, z_came, w_own, w_came, f0, f1, f2, f3, buf):
    me = here()[0]
    came = z_came[...].astype(wide)
    ins = z_own[...] + came[0:168]
    ups = w_own[...] + w_came[...].astype(wide)
    hi, lo = split_pair(pair_sum(z_next[...].astype(wide), came, 168))
    sums = [hi.astype(wide), lo.astype(wide)]
    rest = jnp.zeros((24, SPLIT), wide)
    for j in range(4):
        lanes = slice(j * SPLIT, (j + 1) * SPLIT)
        wide_rows = [ins[i * 24 : (i + 1) * 24, lanes] for i in range(3)] + [rest]
        block = [ups[j * 24 : (j + 1) * 24], jnp.concatenate(wide_rows, axis=1)]
        block += [ins[72 + j * 24 : 96 + j * 24]] + sums
        buf[j ^ me] = jnp.concatenate(block, axis=0).astype(low)
    for r, f in enumerate((f0, f1, f2, f3)):
        f[...] = buf[r]


def final_kernel(
    lengths, f0, f1, f2, f3, in_total, up_total, out_total, first, query, value, output, second, up_bias, down, stats, buf
):
    me = here()[0]
    for r, f in enumerate((f0, f1, f2, f3)):
        buf[r ^ me] = f[...].astype(wide)
    total = buf[0, 72:84] + buf[0, 84:96]
    for j in (1, 2, 3):
        total = total + (buf[j, 72:84] + buf[j, 84:96])
    first[...] = total[0]
    query[...] = total[1]
    value[...] = total[2]
    output[...] = total[3, :DC]
    second[...] = total[4]
    for i in range(4):
        up_bias[i * D : (i + 1) * D] = total[5 + i]
    down[...] = total[9, :DC]
    count = lengths[0, 0] + lengths[0, 1]
    for b in (1, 2, 3):
        count = count + lengths[b, 0] + lengths[b, 1]
    stats[...] = total[10, :2] / count.astype(wide)
    out_total[...] = (buf[0, 48:72] + buf[1, 48:72] + buf[2, 48:72] + buf[3, 48:72])[:, :DC]
    for j in range(4):
        up_total[:, j * D : (j + 1) * D] = buf[j, 0:24, :]
    for i in range(3):
        piece = jnp.concatenate([buf[j, 24:48, i * SPLIT : (i + 1) * SPLIT] for j in range(4)], axis=1)
        in_total[:, i * D : (i + 1) * D] = piece


def home_kernel(x0, x1, x2, x3, weight, resid, gain, middle_grad, out, buf):
    me = here()[0]
    for r, x in enumerate((x0, x1, x2, x3)):
        buf[r ^ me, 0:80, :] = x[192:272, 0:384]
        buf[r ^ me, 80:160, :] = x[192:272, 384:768]
        buf[r ^ me, 160:240, :] = x[272:352, 0:384]
    e = jnp.zeros((160, D), wide)
    for i in range(3):
        g = jnp.concatenate([unpacked(buf[j, i * 80 : (i + 1) * 80, :]) for j in range(4)], axis=1)
        e = e + nt(g.astype(low), weight[:, i * D : (i + 1) * D])
    full = full_of(resid[...].astype(wide))
    root = jnp.sqrt(jnp.mean(full * full, axis=1, keepdims=True) + epsilon)
    n = full / root
    eg = e * row(gain)
    f = (eg - n * jnp.mean(eg * n, axis=1, keepdims=True)) / root
    lane = lax.broadcasted_iota(jnp.int32, (160, D), 1)
    last = jnp.sum(jnp.where(lane == D - 1, f, 0.0), axis=1, keepdims=True)
    out[...] = (middle_grad[...] + f - last)[:, :DC].astype(low)


def down_sum_kernel(x0, x1, x2, x3, own, other):
    total = x0[0:192, :].astype(wide)
    for x in (x1, x2, x3):
        total = total + x[0:192, :].astype(wide)
    own[...] = total[0:96]
    other[...] = total[96:192].astype(low)


def down_final_kernel(own, came, down_total):
    down_total[...] = (own[...] + came[...].astype(wide))[:, :DC]

def swap_chip(block, step):
    return lax.ppermute(block, "blk", [(k, k ^ (2 * step)) for k in range(8)])


def swap_core(block):
    return lax.ppermute(block, "blk", [(k, k ^ 1) for k in range(8)])


def shift_bucket(block, step):
    return lax.ppermute(block, "bucket", [(b, b ^ step) for b in range(4)])


def exchange(blocks):
    got = {r: swap_chip(blocks[r], r) for r in (3, 1, 2)}
    return [blocks[0], got[1], got[2], got[3]]


def after(values, *others):
    return lax.optimization_barrier((tuple(values), others))[0]


def body(
    residual_in,
    out_cotangent,
    first_gain,
    input_weight,
    query_bias,
    value_bias,
    output_weight,
    output_bias,
    second_gain,
    up_weight,
    up_bias,
    down_weight,
    down_bias,
    lengths,
    offsets,
    span_order,
):
    where = [span_order, offsets, lengths]
    packed_block = ((240, 2 * SPLIT), low)
    token = ((160, D), low)
    s0, s1, s2, s3, hidden, root_one = call(
        entry_kernel,
        [packed_block] * 4 + [token, ((160, 1), wide)],
        [residual_in, first_gain, input_weight, query_bias, value_bias],
        [
            pltpu.VMEM((4, 240, 2 * SPLIT), low),
            pltpu.VMEM((160, DC), low),
            pltpu.VMEM((D,), wide),
            pltpu.VMEM((3, D, D), low),
            pltpu.VMEM((D,), wide),
            pltpu.VMEM((D,), wide),
            pltpu.SemaphoreType.DMA((7,)),
        ],
        extra=60,
        far=range(5),
    )
    got = exchange([s0, s1, s2, s3])
    (push,) = call(push_kernel, [((160, FF), wide)], [out_cotangent, down_weight])
    hiddens = exchange([hidden] * 4)
    got = list(after(got, push))
    query, own_both = call(assemble_kernel, [((640, SPLIT), low), ((640, 2 * SPLIT), low)], got)
    sib_both = swap_core(own_both)
    backed = ((80, 2 * SPLIT), low)
    chance, attended, b0, b1, b2, b3 = call(
        forward_kernel,
        [((3, 640, 1280), low), ((640, SPLIT), wide)] + [backed] * 4,
        where + [query, own_both, sib_both],
        [pltpu.VMEM((1280, SPLIT), low), pltpu.VMEM((3, 1280, SPLIT), low), pltpu.VMEM((640, 1280), wide)]
        + [pltpu.VMEM((640, 1), jnp.int32)] * 2,
        small=3,
        work=7,
    )
    back = exchange([b0, b1, b2, b3])
    (cot,) = after([out_cotangent], b0)
    cots = [out_cotangent, shift_bucket(cot, 1)]
    back = list(after(back, *hiddens[1:]))
    (columns,) = call(columns_kernel, [((D, 3 * SPLIT), low)], after([input_weight], b0))
    outs = call(
        middle_kernel,
        [backed] * 4
        + [((320, D), low)] * 6
        + [token, ((160, DC), wide), ((160, D), wide), ((16, D), wide)],
        where
        + back
        + [output_weight, output_bias, residual_in, root_one, out_cotangent, second_gain]
        + [up_weight, up_bias, push],
        [pltpu.VMEM((4, 80, 2 * SPLIT), low), pltpu.VMEM((4, 160, D), low), pltpu.VMEM((4, 320, D), low)],
        small=3,
    )
    act_keep, act_send = outs[4:6]
    lates = list(outs[6:10])
    branch_own, middle, middle_grad, vector = outs[10:]
    grads = exchange(outs[:4])
    grads = list(after(grads, cots[1]))
    (residual_out,) = call(
        closing_kernel,
        [((160, DC), low)],
        [act_keep, act_send, down_weight, middle, down_bias],
    )
    act_came = shift_bucket(act_send, 1)
    lates = exchange(after(lates, *grads[1:]))
    query_grad, both_grad, *away = call(
        backward_kernel,
        [((640, SPLIT), low), ((640, 2 * SPLIT), wide)] + [((320, 2 * SPLIT), low)] * 2,
        grads + [query, own_both, sib_both, chance, attended],
        [
            pltpu.VMEM((3, 1280, SPLIT), low),
            pltpu.VMEM((1280, SPLIT), low),
            pltpu.VMEM((640, SPLIT), low),
            pltpu.VMEM((640, 1280), low),
            pltpu.VMEM((SPLIT, 1280), wide),
            pltpu.VMEM((SPLIT, 1280), wide),
            pltpu.VMEM((640, 1280), wide),
        ],
    )
    arrived = [swap_core(x) for x in after(away, act_came)]
    arrived = list(after(arrived, lates[1], lates[2]))
    outs = call(
        late_kernel,
        [packed_block] * 4 + [((4, 192, D), low), ((4, 168, D), wide), ((1504, D), low)],
        [query_grad, both_grad] + arrived + hiddens + [act_keep, act_came] + cots + back + [branch_own, columns, first_gain, vector],
        [
            pltpu.VMEM((640, D), low),
            pltpu.VMEM((640, D), low),
            pltpu.VMEM((640, 3 * SPLIT), low),
            pltpu.VMEM((2, 4, 192, D), low),
            pltpu.VMEM((2, 4, 168, D), wide),
        ],
    )
    homes = list(outs[:4])
    keep_x, keep_z, send = outs[4:]
    outs = call(
        late_sum_kernel,
        [((352, D), low)] * 4 + [((336, D), wide), ((368, D), low)],
        [keep_x, keep_z, send, swap_core(send)] + homes,
    )
    home = exchange(outs[:4])
    z_keep, z_send = outs[4:]
    z_own, z_next = call(
        late_mid_kernel,
        [((168, D), wide), ((192, D), low)],
        [z_keep, z_send, shift_bucket(z_send, 1)],
    )
    z_came = shift_bucket(z_next, 2)
    keep, *send = call(
        up_grad_kernel,
        [((4, 96, D), low)] + [((128, D), low)] * 3,
        lates,
        [pltpu.VMEM((640, D), low), pltpu.VMEM((640, D), low), pltpu.VMEM((2, 4, 96, D), low)],
    )
    w_keep, w_send = call(
        up_sum_kernel,
        [((2, 96, D), wide), ((2, 96, D), low)],
        [keep] + [swap_core(x) for x in send],
    )
    w_own, w_next = call(
        up_mid_kernel,
        [((96, D), wide), ((96, D), low)],
        [w_keep, shift_bucket(w_send, 1)],
    )
    w_came = shift_bucket(w_next, 2)
    finals = call(
        final_send_kernel,
        [((96, D), low)] * 4,
        [z_own, z_next, z_came, w_own, w_came],
        [pltpu.VMEM((4, 96, D), low)],
    )
    down_own, down_other = call(down_sum_kernel, [((96, D), wide), ((96, D), low)], home)
    (down_total,) = call(
        down_final_kernel, [((96, DC), wide)], [down_own, shift_bucket(down_other, 2)]
    )
    (residual_grad,) = call(
        home_kernel,
        [((160, DC), low)],
        home + [input_weight, residual_in, first_gain, middle_grad],
        [pltpu.VMEM((4, 240, 2 * SPLIT), low)],
    )
    in_total, up_total, out_total, first, query_sum, value_sum, output, second, up_sum_bias, down, stats = call(
        final_kernel,
        [((24, 3 * D), wide), ((24, FF), wide), ((24, DC), wide)]
        + [((D,), wide)] * 3
        + [((DC,), wide), ((D,), wide), ((FF,), wide), ((DC,), wide), ((2,), wide)],
        [lengths] + exchange(finals),
        [pltpu.VMEM((4, 96, D), wide)],
        small=1,
    )
    return (
        residual_out,
        residual_grad,
        first,
        in_total,
        query_sum,
        value_sum,
        out_total,
        output,
        second,
        up_total,
        up_sum_bias,
        down_total,
        down,
        stats,
    )


def solution(mesh):
    placed = (
        P(("bucket", "blk"), None),
        P(("bucket", "blk"), None),
        P(),
        P(),
        P(),
        P(),
        P(),
        P(),
        P(),
        P(),
        P(),
        P(),
        P(),
        P(),
        P("bucket", None),
        P(),
    )
    return jax.shard_map(
        body if dict(mesh.shape) == {"bucket": 4, "blk": 8} else general_body,
        mesh=mesh,
        in_specs=placed,
        out_specs=(
            P(("bucket", "blk"), None),
            P(("bucket", "blk"), None),
            P(),
            P(("bucket", "blk"), None),
            P(),
            P(),
            P(("bucket", "blk"), None),
            P(),
            P(),
            P(("bucket", "blk"), None),
            P(),
            P(("bucket", "blk"), None),
            P(),
            P(),
        ),
        check_vma=False,
    )
```

```python
import jax
import jax.numpy as jnp
from jax import lax
from jax.experimental import pallas as pl
from jax.experimental.pallas import tpu as pltpu
from jax.sharding import PartitionSpec as P

D = 768
HEADS = 12
HEAD_DIM = 64


epsilon = 1e-05
masked_value = -1e30


def center_norm(resid, gain):
    full = jnp.concatenate([resid, -jnp.sum(resid, axis=1, keepdims=True)], axis=1)
    root = jnp.sqrt(jnp.mean(full * full, axis=1, keepdims=True) + epsilon)
    return (full / root * gain, root[:, 0])


def gelu_tanh(inputs):
    return jax.nn.gelu(inputs, approximate=True)


def heads_of(block):
    return block.reshape(block.shape[0], HEADS, HEAD_DIM)


def places_of(span_order, begin, count, half_rows):
    spans = lax.dynamic_slice_in_dim(span_order, begin // half_rows, count // half_rows)
    inner = jnp.arange(half_rows, dtype=jnp.int32)
    return (spans[:, None] * half_rows + inner[None, :]).reshape(count)


def documents_of(places, lengths, offsets):
    first_in = (places >= offsets[0, 0]) & (places < offsets[0, 0] + lengths[0, 0])
    second_in = (places >= offsets[0, 1]) & (places < offsets[0, 1] + lengths[0, 1])
    return jnp.where(first_in, 0, jnp.where(second_in, 1, -1)).astype(jnp.int32)


def allowed_of(query_places, query_docs, key_places, key_docs):
    same = (query_docs[:, None] == key_docs[None, :]) & (query_docs[:, None] >= 0)
    return (same & (key_places[None, :] <= query_places[:, None]))[None]


def block_shape(count, unit):
    shards = count // unit
    width = max(1, 1024 // unit)
    while shards % width != 0:
        width = width - 1
    return (shards // width, width * unit)


def general_body(
    residual_in,
    out_cotangent,
    first_gain,
    input_weight,
    query_bias,
    value_bias,
    output_weight,
    output_bias,
    second_gain,
    up_weight,
    up_bias,
    down_weight,
    down_bias,
    lengths,
    offsets,
    span_order,
):
    rows = residual_in.shape[0]
    half_rows = rows // 2
    score_scale = HEAD_DIM ** (-0.5)
    index = lax.axis_index("blk")
    bucket_index = lax.axis_index("bucket")
    own_lengths = lax.dynamic_slice_in_dim(lengths, bucket_index, 1, 0)
    valid_count = jnp.sum(lengths.astype(jnp.float32))
    query_places = places_of(span_order, index * rows, rows, half_rows)
    query_docs = documents_of(query_places, own_lengths, offsets)
    valid = (query_docs >= 0).astype(jnp.float32)
    resid = residual_in.astype(jnp.float32)
    normed, first_back, first_root = jax.vjp(center_norm, resid, first_gain, has_aux=True)
    hidden_in = normed.astype(jnp.bfloat16)
    projected = jnp.dot(hidden_in, input_weight, preferred_element_type=jnp.float32)
    query = (projected[:, :D] + query_bias).astype(jnp.bfloat16)
    keys = projected[:, D : 2 * D].astype(jnp.bfloat16)
    values = (projected[:, 2 * D :] + value_bias).astype(jnp.bfloat16)
    query_heads = heads_of(query)
    key_heads = heads_of(keys)
    value_heads = heads_of(values)
    initial = (
        jnp.full((HEADS, rows), masked_value, jnp.float32),
        jnp.zeros((HEADS, rows), jnp.float32),
        jnp.zeros((HEADS, rows, HEAD_DIM), jnp.float32),
    )
    state = initial
    key_piece = lax.all_gather(keys, "blk", axis=0, tiled=True)
    value_piece = lax.all_gather(values, "blk", axis=0, tiled=True)
    count = key_piece.shape[0]
    number, width = block_shape(count, rows)
    key_places = places_of(span_order, jnp.int32(0), count, half_rows)
    key_docs = documents_of(key_places, own_lengths, offsets)

    def forward_advance(state, parts):
        key_block, value_block, places_block, docs_block = parts
        peak, total, summed = state
        scores = (
            jnp.einsum(
                "qhd,khd->hqk", query_heads, heads_of(key_block), preferred_element_type=jnp.float32
            )
            * score_scale
        )
        allowed = allowed_of(query_places, query_docs, places_block, docs_block)
        masked = jnp.where(allowed, scores, masked_value)
        new_peak = jnp.maximum(peak, jnp.max(masked, axis=2))
        decay = jnp.exp(peak - new_peak)
        weights = jnp.where(allowed, jnp.exp(masked - new_peak[:, :, None]), 0.0)
        total = total * decay + jnp.sum(weights, axis=2)
        summed = summed * decay[:, :, None] + jnp.einsum(
            "hqk,khd->hqd",
            weights.astype(jnp.bfloat16),
            heads_of(value_block),
            preferred_element_type=jnp.float32,
        )
        return ((new_peak, total, summed), None)

    state, _ = lax.scan(
        forward_advance,
        state,
        (
            key_piece.reshape(number, width, D),
            value_piece.reshape(number, width, D),
            key_places.reshape(number, width),
            key_docs.reshape(number, width),
        ),
    )
    peak, total, summed = state
    denominator = total + 1.0 - valid[None, :]
    attended = summed / denominator[:, :, None]
    log_total = peak + jnp.log(denominator)
    mixed = attended.transpose(1, 0, 2).reshape(rows, D).astype(jnp.bfloat16)
    branch = jnp.dot(mixed, output_weight, preferred_element_type=jnp.float32) + output_bias
    middle = resid + branch
    normed_two, second_back, second_root = jax.vjp(center_norm, middle, second_gain, has_aux=True)
    hidden_two = normed_two.astype(jnp.bfloat16)
    upward = jnp.dot(hidden_two, up_weight, preferred_element_type=jnp.float32) + up_bias
    active_float, gelu_back = jax.vjp(gelu_tanh, upward)
    active = active_float.astype(jnp.bfloat16)
    closing = jnp.dot(active, down_weight, preferred_element_type=jnp.float32) + down_bias
    residual_out = (middle + closing).astype(jnp.bfloat16)
    stat_sums = jnp.stack([jnp.sum(valid * first_root), jnp.sum(valid * second_root)])
    stat_sums = lax.psum(stat_sums, ("bucket", "blk"))
    cotangent = out_cotangent.astype(jnp.float32)
    down_grad = jnp.einsum("rf,rc->fc", active, out_cotangent, preferred_element_type=jnp.float32)
    down_bias_grad = jnp.sum(cotangent, axis=0)
    active_grad = jnp.einsum(
        "rc,fc->rf", out_cotangent, down_weight, preferred_element_type=jnp.float32
    )
    (upward_float,) = gelu_back(active_grad)
    upward_grad = upward_float.astype(jnp.bfloat16)
    up_grad = jnp.einsum("rd,rf->df", hidden_two, upward_grad, preferred_element_type=jnp.float32)
    up_bias_grad = jnp.sum(upward_grad.astype(jnp.float32), axis=0)
    hidden_two_grad = jnp.einsum(
        "rf,df->rd", upward_grad, up_weight, preferred_element_type=jnp.float32
    )
    middle_part, second_gain_grad = second_back(hidden_two_grad)
    middle_grad = cotangent + middle_part
    branch_grad = middle_grad.astype(jnp.bfloat16)
    output_grad = jnp.einsum("rd,rc->dc", mixed, branch_grad, preferred_element_type=jnp.float32)
    output_bias_grad = jnp.sum(branch_grad.astype(jnp.float32), axis=0)
    attended_grad = jnp.einsum(
        "rc,dc->rd", branch_grad, output_weight, preferred_element_type=jnp.float32
    ).astype(jnp.bfloat16)
    grad_heads = heads_of(attended_grad)
    delta = jnp.einsum("rhd,hrd->hr", grad_heads.astype(jnp.float32), attended)
    query_zero = jnp.zeros((rows, HEADS, HEAD_DIM), jnp.float32)
    accum = query_zero
    key_piece = lax.all_gather(keys, "blk", axis=0, tiled=True)
    value_piece = lax.all_gather(values, "blk", axis=0, tiled=True)
    count = key_piece.shape[0]
    number, width = block_shape(count, rows)
    key_places = places_of(span_order, jnp.int32(0), count, half_rows)
    key_docs = documents_of(key_places, own_lengths, offsets)

    def query_advance(accum, parts):
        key_block, value_block, places_block, docs_block = parts
        block_keys = heads_of(key_block)
        scores = (
            jnp.einsum("qhd,khd->hqk", query_heads, block_keys, preferred_element_type=jnp.float32)
            * score_scale
        )
        allowed = allowed_of(query_places, query_docs, places_block, docs_block)
        chance = jnp.where(
            allowed, jnp.exp(jnp.where(allowed, scores, masked_value) - log_total[:, :, None]), 0.0
        )
        push = jnp.einsum(
            "qhd,khd->hqk", grad_heads, heads_of(value_block), preferred_element_type=jnp.float32
        )
        slope = (chance * (push - delta[:, :, None])).astype(jnp.bfloat16)
        accum = (
            accum
            + jnp.einsum("hqk,khd->qhd", slope, block_keys, preferred_element_type=jnp.float32)
            * score_scale
        )
        return (accum, None)

    accum, _ = lax.scan(
        query_advance,
        accum,
        (
            key_piece.reshape(number, width, D),
            value_piece.reshape(number, width, D),
            key_places.reshape(number, width),
            key_docs.reshape(number, width),
        ),
    )
    log_all, delta_all = (
        lax.all_gather(log_total.T, "blk", axis=0, tiled=True),
        lax.all_gather(delta.T, "blk", axis=0, tiled=True),
    )
    key_zero = jnp.zeros((rows, HEADS, HEAD_DIM), jnp.float32)
    state = (key_zero, key_zero)
    begin = jnp.int32(0)
    query_piece = lax.all_gather(query, "blk", axis=0, tiled=True)
    grad_piece = lax.all_gather(attended_grad, "blk", axis=0, tiled=True)
    count = query_piece.shape[0]
    number, width = block_shape(count, rows)
    piece_places = places_of(span_order, begin, count, half_rows)
    piece_docs = documents_of(piece_places, own_lengths, offsets)
    piece_log = lax.dynamic_slice_in_dim(log_all, begin, count, 0)
    piece_delta = lax.dynamic_slice_in_dim(delta_all, begin, count, 0)

    def key_advance(state, parts):
        query_block, grad_block, places_block, docs_block, log_block, delta_block = parts
        key_sum, value_sum = state
        block_query = heads_of(query_block)
        block_grad = heads_of(grad_block)
        scores = (
            jnp.einsum("qhd,khd->hqk", block_query, key_heads, preferred_element_type=jnp.float32)
            * score_scale
        )
        allowed = allowed_of(places_block, docs_block, query_places, query_docs)
        chance = jnp.where(
            allowed,
            jnp.exp(jnp.where(allowed, scores, masked_value) - log_block.T[:, :, None]),
            0.0,
        )
        value_sum = value_sum + jnp.einsum(
            "hqk,qhd->khd",
            chance.astype(jnp.bfloat16),
            block_grad,
            preferred_element_type=jnp.float32,
        )
        push = jnp.einsum(
            "qhd,khd->hqk", block_grad, value_heads, preferred_element_type=jnp.float32
        )
        slope = (chance * (push - delta_block.T[:, :, None])).astype(jnp.bfloat16)
        key_sum = (
            key_sum
            + jnp.einsum("hqk,qhd->khd", slope, block_query, preferred_element_type=jnp.float32)
            * score_scale
        )
        return ((key_sum, value_sum), None)

    state, _ = lax.scan(
        key_advance,
        state,
        (
            query_piece.reshape(number, width, D),
            grad_piece.reshape(number, width, D),
            piece_places.reshape(number, width),
            piece_docs.reshape(number, width),
            piece_log.reshape(number, width, HEADS),
            piece_delta.reshape(number, width, HEADS),
        ),
    )
    key_sum, value_sum = state
    query_low = accum.reshape(rows, D).astype(jnp.bfloat16)
    key_low = key_sum.reshape(rows, D).astype(jnp.bfloat16)
    value_low = value_sum.reshape(rows, D).astype(jnp.bfloat16)
    projected_grad = jnp.concatenate([query_low, key_low, value_low], axis=1)
    input_grad = jnp.einsum(
        "rd,re->de", hidden_in, projected_grad, preferred_element_type=jnp.float32
    )
    query_bias_grad = jnp.sum(query_low.astype(jnp.float32), axis=0)
    value_bias_grad = jnp.sum(value_low.astype(jnp.float32), axis=0)
    hidden_in_grad = jnp.einsum(
        "re,de->rd", projected_grad, input_weight, preferred_element_type=jnp.float32
    )
    resid_part, first_gain_grad = first_back(hidden_in_grad)
    residual_grad = (middle_grad + resid_part).astype(jnp.bfloat16)
    input_part, output_part, up_part, down_part = (
        lax.psum_scatter(input_grad, ("bucket", "blk"), scatter_dimension=0, tiled=True),
        lax.psum_scatter(output_grad, ("bucket", "blk"), scatter_dimension=0, tiled=True),
        lax.psum_scatter(up_grad, ("bucket", "blk"), scatter_dimension=0, tiled=True),
        lax.psum_scatter(down_grad, ("bucket", "blk"), scatter_dimension=0, tiled=True),
    )
    (
        first_sum,
        query_sum_bias,
        value_sum_bias,
        output_sum_bias,
        second_sum,
        up_sum_bias,
        down_sum_bias,
    ) = lax.psum(
        (
            first_gain_grad,
            query_bias_grad,
            value_bias_grad,
            output_bias_grad,
            second_gain_grad,
            up_bias_grad,
            down_bias_grad,
        ),
        ("bucket", "blk"),
    )
    mean_norms = stat_sums / valid_count
    return (
        residual_out,
        residual_grad,
        first_sum,
        input_part,
        query_sum_bias,
        value_sum_bias,
        output_part,
        output_sum_bias,
        second_sum,
        up_part,
        up_sum_bias,
        down_part,
        down_sum_bias,
        mean_norms,
    )


DC = 767
SPLIT = 192
FF = 3072
low = jnp.bfloat16
wide = jnp.float32
VMEM = pl.BlockSpec(memory_space=pltpu.VMEM)
SMEM = pl.BlockSpec(memory_space=pltpu.SMEM)
HBM = pl.BlockSpec(memory_space=pltpu.HBM)

def padded_bytes(shape, dtype):
    shape = (1, 1) + tuple(shape)
    size = jnp.dtype(dtype).itemsize
    rows, lanes = -(-shape[-2] // 16) * 16, -(-shape[-1] // 128) * 128
    for d in shape[:-2]:
        rows = rows * d
    return rows * lanes * size


def call(kernel, outs, ins, scratch=(), extra=6, small=0, far=(), work=0):
    shapes = [jax.ShapeDtypeStruct(s, d) for s, d in outs]
    held = [(s, d) for s, d in outs]
    held += [(x.shape, x.dtype) for i, x in enumerate(ins) if i >= small and i not in far]
    held += [(s.shape, s.dtype) for s in scratch if s.memory_space == pltpu.VMEM]
    limit = sum(padded_bytes(s, d) for s, d in held) + extra * 2**20
    return pl.pallas_call(
        kernel,
        out_shape=shapes,
        in_specs=[SMEM if i < small else HBM if i in far else VMEM for i in range(len(ins))],
        out_specs=[VMEM] * len(outs),
        scratch_shapes=list(scratch),
        compiler_params=pltpu.CompilerParams(vmem_limit_bytes=min(limit, 60 * 2**20)),
        cost_estimate=pl.CostEstimate(
            flops=int(1000 + work * 1.1e9),
            bytes_accessed=1000,
            transcendentals=0,
        ),
    )(*ins)


def here():
    index = lax.axis_index("blk")
    return index // 2, lax.axis_index("bucket"), index % 2


def full_of(x):
    rows=x.shape[0]
    wide_x=jnp.concatenate([x,jnp.zeros((rows,1),x.dtype)],axis=1)
    last=lax.broadcasted_iota(jnp.int32,(rows,D),1)==D-1
    return jnp.where(last,-jnp.sum(x,axis=1,keepdims=True),wide_x)

def row(ref):
    return ref[...].reshape(1, ref.shape[0])


def nt(a, b):
    return lax.dot_general(a, b, (((1,), (1,)), ((), ())), preferred_element_type=wide)


def tn(a, b):
    return lax.dot_general(a, b, (((0,), (0,)), ((), ())), preferred_element_type=wide)


def packed(x):
    half = x.shape[0] // 2
    return jnp.concatenate([x[:half], x[half:]], axis=1).astype(low)


def unpacked(x):
    x = x.astype(wide)
    half = x.shape[1] // 2
    return jnp.concatenate([x[:, :half], x[:, half:]], axis=0)


def split_pair(x):
    hi = x.astype(low)
    return hi, (x - hi.astype(wide)).astype(low)


def head_mask(x, h):
    lane = lax.broadcasted_iota(jnp.int32, x.shape, 1)
    return jnp.where((lane >= h * 64) & (lane < (h + 1) * 64), x, jnp.zeros_like(x))


def limits(spans, offsets, lengths, bucket, chip, core, half):
    place = spans[chip * 4 + core * 2 + half] * 80 + lax.broadcasted_iota(jnp.int32, (80, 1), 0)
    one, two = offsets[0, 0], offsets[0, 1]
    first = (place >= one) & (place < one + lengths[bucket, 0])
    second = (place >= two) & (place < two + lengths[bucket, 1])
    return jnp.where(first, one, two), jnp.where(first | second, place, -1)


def entry_kernel(
    resid_far, gain_far, weight_far, qbias_far, vbias_far, s0, s1, s2, s3, hidden_out, root_out,
    buf, resid, gain, weight, qbias, vbias, sems,
):
    me = here()[0]
    copies = [
        pltpu.make_async_copy(a, b, sems.at[i])
        for i, (a, b) in enumerate(
            [(resid_far, resid), (gain_far, gain), (qbias_far, qbias), (vbias_far, vbias)]
            + [(weight_far.at[:, pl.ds(i * D, D)], weight.at[i]) for i in range(3)]
        )
    ]
    for copy in copies:
        copy.start()
    copies[0].wait()
    full = full_of(resid[...].astype(wide))
    root = jnp.sqrt(jnp.mean(full * full, axis=1, keepdims=True) + epsilon)
    root_out[...] = root
    copies[1].wait()
    hidden = (full / root * row(gain)).astype(low)
    hidden_out[...] = hidden
    copies[2].wait()
    copies[3].wait()
    for i in range(3):
        copies[4 + i].wait()
        p = jnp.dot(hidden, weight[i], preferred_element_type=wide)
        if i == 0:
            p = (p + row(qbias)) * 0.125
        if i == 2:
            p = p + row(vbias)
        for j in range(4):
            buf[j ^ me, i * 80 : (i + 1) * 80, :] = packed(p[:, j * SPLIT : (j + 1) * SPLIT])
    for r, s in enumerate((s0, s1, s2, s3)):
        s[...] = buf[r]


def push_kernel(spans, offsets, lengths, cot, weight, out, bounds, places):
    me, bucket, core = here()
    for i in range(4):
        out[:, i * D : (i + 1) * D] = nt(cot[...], weight[i * D : (i + 1) * D, :])
    lane = lax.broadcasted_iota(jnp.int32, (1, 1280), 1)
    place = lane
    for blk in range(16):
        chip = ((blk % 8) // 2) ^ me
        span = spans[chip * 4 + (core ^ (blk // 8)) * 2 + blk % 2]
        place = jnp.where((lane >= blk * 80) & (lane < (blk + 1) * 80), lane + (span - blk) * 80, place)
    places[...] = place
    for blk in range(8):
        lo, hi = limits(spans, offsets, lengths, bucket, (blk // 2) ^ me, core, blk % 2)
        bounds[blk * 80 : (blk + 1) * 80, 0:1] = lo
        bounds[blk * 80 : (blk + 1) * 80, 1:2] = hi


def columns_kernel(weight, out):
    me = here()[0]
    for j in range(4):

        @pl.when(me == j)
        def _():
            for i in range(3):
                piece = weight[:, i * D + j * SPLIT : i * D + (j + 1) * SPLIT].astype(wide)
                out[:, i * SPLIT : (i + 1) * SPLIT] = piece.astype(low)


def assemble_kernel(p0, p1, p2, p3, query, both):
    for r, p in enumerate((p0, p1, p2, p3)):
        rows = slice(r * 160, (r + 1) * 160)
        query[rows, :] = unpacked(p[0:80, :]).astype(low)
        both[rows, :SPLIT] = unpacked(p[80:160, :]).astype(low)
        both[rows, SPLIT:] = unpacked(p[160:240, :]).astype(low)


def forward_kernel(
    bounds, places, query, own, sib, chance, attended, b0, b1, b2, b3, keys, vals, scores
):
    keys[:640, :] = own[:, :SPLIT]
    keys[640:, :] = sib[:, :SPLIT]
    v = jnp.concatenate([own[:, SPLIT:].astype(wide), sib[:, SPLIT:].astype(wide)], axis=0)
    for h in range(3):
        vals[h] = head_mask(v, h).astype(low)
    place = places[...]
    q = query[...].astype(wide)
    for h in range(3):
        scores[...] = nt(head_mask(q, h).astype(low), keys[...])
        for blk in range(8):
            rows = slice(blk * 80, (blk + 1) * 80)
            lo, hi = bounds[rows, 0:1], bounds[rows, 1:2]
            s = jnp.where((place >= lo) & (place <= hi), scores[rows, :], masked_value)
            peak = jnp.max(s, axis=1, keepdims=True)
            w = jnp.exp(s - peak)
            total = jnp.sum(w, axis=1, keepdims=True)
            chance[h, rows, :] = (w * jnp.where(hi >= 0, 1.0 / total, 0.0)).astype(low)
        part = jnp.dot(chance[h], vals[h], preferred_element_type=wide)
        if h == 0:
            attended[...] = part
        else:
            attended[...] += part
    acc = attended[...]
    for r, b in enumerate((b0, b1, b2, b3)):
        b[...] = packed(acc[r * 160 : (r + 1) * 160])


def middle_kernel(
    bounds, p0, p1, p2, p3, out_weight, out_bias, resid, root_in, cot, gain, up_weight, up_bias, push,
    d0, d1, d2, d3, act_keep, act_send, n0, n1, n2, n3, branch_own, middle, middle_grad, vector,
    dbuf, abuf, nbuf,
):
    me, bucket, core = here()
    branch = row(out_bias)
    for r, p in enumerate((p0, p1, p2, p3)):
        w = out_weight[pl.ds(pl.multiple_of((me ^ r) * SPLIT, SPLIT), SPLIT), :]
        branch = branch + jnp.dot(unpacked(p[...]).astype(low), w, preferred_element_type=wide)
    mid = resid[...].astype(wide) + branch
    middle[...] = mid
    full = full_of(mid)
    root = jnp.sqrt(jnp.mean(full * full, axis=1, keepdims=True) + epsilon)
    n = full / root
    hidden = (n * row(gain)).astype(low)
    for r in range(4):
        nbuf[r, 0:160, :] = hidden
    e = jnp.zeros((160, D), wide)
    c = 0.7978845608028654
    up_sums = []
    for blk in range(4):
        cols = slice(blk * D, (blk + 1) * D)
        u = jnp.dot(hidden, up_weight[:, cols], preferred_element_type=wide) + up_bias[cols].reshape(1, D)
        square = u * u
        t = jnp.tanh(u * (c + (c * 0.044715) * square))
        gate = 0.5 + 0.5 * t
        act = u * gate
        abuf[blk ^ bucket] = act.astype(low)
        slope = gate + act * (1.0 - t) * (c + (3 * c * 0.044715) * square)
        g = (push[:, cols] * slope).astype(low)
        nbuf[blk ^ me, 160:320, :] = g
        up_sums.append(jnp.sum(g.astype(wide), axis=0, keepdims=True))
        e = e + nt(g, up_weight[:, cols])
    gain_sum = jnp.sum(e * n, axis=0, keepdims=True)
    eg = e * row(gain)
    f = (eg - n * jnp.mean(eg * n, axis=1, keepdims=True)) / root
    cot_wide = jnp.concatenate([cot[...].astype(wide), jnp.zeros((160, 1), wide)], axis=1)
    lane = lax.broadcasted_iota(jnp.int32, (160, D), 1)
    last = jnp.sum(jnp.where(lane == D - 1, f, 0.0), axis=1, keepdims=True)
    grad = jnp.where(lane == D - 1, 0.0, cot_wide + f - last)
    middle_grad[...] = grad
    grad_low = grad.astype(low)
    grad_wide = grad_low.astype(wide)
    branch_own[...] = grad_low
    back = nt(grad_wide[:, :DC].astype(low), out_weight[...])
    for j in range(4):
        dbuf[j ^ me] = packed(back[:, j * SPLIT : (j + 1) * SPLIT])
    for r in range(4):
        (d0, d1, d2, d3)[r][...] = dbuf[r]
        (act_keep, act_send)[r % 2][r // 2 * 160 : r // 2 * 160 + 160, :] = abuf[r]
        (n0, n1, n2, n3)[r][...] = nbuf[r]
    valid = jnp.where(bounds[0:160, 1:2] >= 0, 1.0, 0.0)
    one = jnp.sum(valid * root_in[...], axis=0, keepdims=True)
    two = jnp.sum(valid * root, axis=0, keepdims=True)
    at = lax.broadcasted_iota(jnp.int32, (1, D), 1)
    stats = jnp.where(at == 0, one, jnp.where(at == 1, two, 0.0))
    zero = jnp.zeros((1, D), wide)
    sums = [zero, zero, zero, jnp.sum(grad_wide, axis=0, keepdims=True), gain_sum] + up_sums
    sums += [jnp.sum(cot_wide, axis=0, keepdims=True), stats] + [zero] * 5
    vector[...] = jnp.concatenate(sums, axis=0)


def closing_kernel(act_keep, act_send, weight, middle, bias, out):
    bucket = here()[1]
    acc = middle[...] + row(bias)
    for d in range(4):
        w = weight[pl.ds(pl.multiple_of((bucket ^ d) * D, D), D), :]
        a = (act_keep, act_send)[d % 2][d // 2 * 160 : d // 2 * 160 + 160, :]
        acc = acc + jnp.dot(a, w, preferred_element_type=wide)
    out[...] = acc.astype(low)


def backward_kernel(
    d0, d1, d2, d3, query, own, sib, chance, attended, query_grad, both_grad, away_one, away_two,
    keys, vals, grads, slopes, keys_turned, vals_turned, pushes,
):
    for r, d in enumerate((d0, d1, d2, d3)):
        grads[r * 160 : (r + 1) * 160, :] = unpacked(d[...]).astype(low)
    k = jnp.concatenate([own[:, :SPLIT], sib[:, :SPLIT]], axis=0).astype(wide)
    for h in range(3):
        keys[h] = head_mask(k, h).astype(low)
    vals[:640, :] = own[:, SPLIT:].astype(wide).astype(low)
    vals[640:, :] = sib[:, SPLIT:].astype(wide).astype(low)
    g = grads[...].astype(wide)
    q_turned = jnp.transpose(query[...].astype(wide)).astype(low)
    g_turned = jnp.transpose(g).astype(low)
    dq = jnp.zeros((640, SPLIT), wide)
    for h in range(3):
        gh = head_mask(g, h)
        delta = jnp.sum(gh * attended[...], axis=1, keepdims=True)
        pushes[...] = nt(gh.astype(low), vals[...])
        for r in range(8):
            rows = slice(r * 80, (r + 1) * 80)
            slopes[rows, :] = (chance[h, rows, :].astype(wide) * (pushes[rows, :] - delta[rows, :])).astype(low)
        dq = dq + jnp.dot(slopes[...], keys[h], preferred_element_type=wide)
        rows = slice(h * 64, (h + 1) * 64)
        keys_turned[rows, :] = jnp.dot(q_turned[rows], slopes[...], preferred_element_type=wide)
        vals_turned[rows, :] = jnp.dot(g_turned[rows], chance[h], preferred_element_type=wide)
    query_grad[...] = (dq * 0.125).astype(low)
    dk = jnp.transpose(keys_turned[...])
    dv = jnp.transpose(vals_turned[...])
    both_grad[:, :SPLIT] = dk[:640]
    both_grad[:, SPLIT:] = dv[:640]
    away_one[:, :SPLIT] = dk[640:960].astype(low)
    away_one[:, SPLIT:] = dv[640:960].astype(low)
    away_two[:, :SPLIT] = dk[960:].astype(low)
    away_two[:, SPLIT:] = dv[960:].astype(low)


def late_kernel(
    query_grad, both_grad, arrive_one, arrive_two, i0, i1, i2, i3, act_keep, act_came, c0, c1, p0, p1, p2, p3, branch_own, columns, gain, vector,
    h0, h1, h2, h3, keep_x, keep_z, send, left, right, heads, xbuf, zbuf,
):
    me, bucket, core = here()
    arrived = jnp.concatenate([arrive_one[...].astype(wide), arrive_two[...].astype(wide)], axis=0)
    both = both_grad[...] + arrived
    parts = [query_grad[...].astype(wide), both[:, :SPLIT], both[:, SPLIT:]]
    parts = [p.astype(low).astype(wide) for p in parts]
    for r, h in enumerate((h0, h1, h2, h3)):
        left[r * 160 : (r + 1) * 160, :] = (i0, i1, i2, i3)[r][...]
        for i in range(3):
            h[i * 80 : (i + 1) * 80, :] = packed(parts[i][r * 160 : (r + 1) * 160])
    heads[...] = jnp.concatenate(parts, axis=1).astype(low)
    grad = tn(left[...], heads[...])
    sums = jnp.sum(grad * columns[...].astype(wide), axis=1, keepdims=True)
    gain_row = jnp.transpose(jnp.broadcast_to(sums, (D, 128)))[0:1] / row(gain)
    lane = lax.broadcasted_iota(jnp.int32, (1, D), 1)
    mine = (lane >= me * SPLIT) & (lane < (me + 1) * SPLIT)

    def column_sum(x):
        s = jnp.sum(x, axis=0, keepdims=True)
        return jnp.where(mine, jnp.concatenate([s] * 4, axis=1), 0.0)

    at = lax.broadcasted_iota(jnp.int32, (16, D), 0)
    total = vector[...] + jnp.where(at == 0, gain_row, 0.0)
    total = total + jnp.where(at == 1, column_sum(parts[0]), 0.0)
    total = total + jnp.where(at == 2, column_sum(parts[2]), 0.0)
    thirds = [grad[:, i * SPLIT : (i + 1) * SPLIT] for i in range(3)]
    for b in range(4):
        for c in range(2):
            block = []
            for part in thirds:
                starts = [b * 192 + j * 48 + c * 24 for j in range(4)]
                block.append(jnp.concatenate([part[s : s + 24] for s in starts], axis=1))
            zbuf[c ^ core, b ^ bucket, 0:72, :] = jnp.concatenate(block, axis=0)
    for r, p in enumerate((p0, p1, p2, p3)):
        out = tn(unpacked(p[...]).astype(low), branch_own[...])
        for j in range(4):
            for c in range(2):
                s = j * 48 + c * 24
                zbuf[c ^ core, me ^ r ^ bucket, 72 + j * 24 : 96 + j * 24, :] = out[s : s + 24]
    for d, c in enumerate((c0, c1)):
        cot = c[...].astype(wide)
        right[d * 160 : (d + 1) * 160, :] = jnp.concatenate([cot, jnp.zeros((160, 1), wide)], axis=1).astype(low)
    for half in range(2):
        left[0:160, :] = act_keep[half * 160 : half * 160 + 160, :]
        left[160:320, :] = act_came[half * 160 : half * 160 + 160, :]
        down = tn(left[0:320, :], right[0:320, :])
        for j in range(4):
            for c in range(2):
                s = j * 192 + c * 96
                xbuf[c ^ core, j ^ me, half * 96 : half * 96 + 96, :] = down[s : s + 96].astype(low)
    keep_x[...] = xbuf[0]
    for r in range(4):
        keep_z[r] = zbuf[0, r]
        send[r * 192 : (r + 1) * 192, :] = xbuf[1, r]
        block = jnp.concatenate([zbuf[1, r], jnp.zeros((8, D), wide)], axis=0)
        send[768 + r * 176 : 944 + r * 176, :] = block.astype(low)
    hi, lo = split_pair(total)
    send[1472:1488, :] = hi
    send[1488:1504, :] = lo


def late_sum_kernel(keep_x, keep_z, send, arrived, h0, h1, h2, h3, x0, x1, x2, x3, z_keep, z_send):
    own = send[1472:1488, :].astype(wide) + send[1488:1504, :].astype(wide)
    hi, lo = split_pair(own + (arrived[1472:1488, :].astype(wide) + arrived[1488:1504, :].astype(wide)))
    blocks = []
    for r in range(4):
        x, h = (x0, x1, x2, x3)[r], (h0, h1, h2, h3)[r]
        x[0:192, :] = (keep_x[r].astype(wide) + arrived[r * 192 : (r + 1) * 192, :].astype(wide)).astype(low)
        x[192:272, 0:384] = h[0:80, :]
        x[192:272, 384:768] = h[80:160, :]
        x[272:352, 0:384] = h[160:240, :]
        x[272:352, 384:768] = jnp.zeros((80, 384), low)
        came = arrived[768 + r * 176 : 944 + r * 176, :].astype(wide)
        blocks.append(keep_z[r] + came[0:168])
    z_keep[0:168, :] = blocks[0]
    z_keep[168:336, :] = blocks[2]
    sums = [hi.astype(wide)[0:12], lo.astype(wide)[0:12], jnp.zeros((8, D), wide)]
    z_send[...] = jnp.concatenate([blocks[1], blocks[3]] + sums, axis=0).astype(low)


def pair_sum(own, came, start):
    a = own[start : start + 12] + own[start + 12 : start + 24]
    b = came[start : start + 12] + came[start + 12 : start + 24]
    return a + b


def late_mid_kernel(z_keep, z_send, came, z_own, z_next):
    came = came[...].astype(wide)
    hi, lo = split_pair(pair_sum(z_send[...].astype(wide), came, 336))
    z_own[...] = z_keep[0:168, :] + came[0:168]
    block = [z_keep[168:336, :] + came[168:336], hi.astype(wide), lo.astype(wide)]
    z_next[...] = jnp.concatenate(block, axis=0).astype(low)


def up_grad_kernel(n0, n1, n2, n3, keep, send_one, send_two, send_three, left, right, buf):
    me, bucket, core = here()
    for r in range(4):
        rows = slice(r * 160, (r + 1) * 160)
        n = (n0, n1, n2, n3)[r]
        left[rows, :] = n[0:160, :]
        right[rows, :] = n[160:320, :]
    up = tn(left[...], right[...])
    for b in range(4):
        for c in range(2):
            starts = [b * 192 + j * 48 + c * 24 for j in range(4)]
            block = jnp.concatenate([up[s : s + 24] for s in starts], axis=0)
            buf[c ^ core, b ^ bucket] = block.astype(low)
    keep[...] = buf[0]
    send_one[0:96, :] = buf[1, 0]
    send_one[96:128, :] = buf[1, 1, 0:32, :]
    send_two[0:64, :] = buf[1, 1, 32:96, :]
    send_two[64:128, :] = buf[1, 2, 0:64, :]
    send_three[0:32, :] = buf[1, 2, 64:96, :]
    send_three[32:128, :] = buf[1, 3]


def up_sum_kernel(keep, arrive_one, arrive_two, arrive_three, w_keep, w_send):
    parts = [a[...].astype(wide) for a in (arrive_one, arrive_two, arrive_three)]
    arrived = jnp.concatenate(parts, axis=0)
    for d in range(4):
        total = keep[d].astype(wide) + arrived[d * 96 : (d + 1) * 96]
        if d % 2 == 0:
            w_keep[d // 2] = total
        else:
            w_send[d // 2] = total.astype(low)


def up_mid_kernel(w_keep, came, w_own, w_next):
    w_own[...] = w_keep[0] + came[0].astype(wide)
    w_next[...] = (w_keep[1] + came[1].astype(wide)).astype(low)


def final_send_kernel(z_own, z_next, z_came, w_own, w_came, f0, f1, f2, f3, buf):
    me = here()[0]
    came = z_came[...].astype(wide)
    ins = z_own[...] + came[0:168]
    ups = w_own[...] + w_came[...].astype(wide)
    hi, lo = split_pair(pair_sum(z_next[...].astype(wide), came, 168))
    sums = [hi.astype(wide), lo.astype(wide)]
    rest = jnp.zeros((24, SPLIT), wide)
    for j in range(4):
        lanes = slice(j * SPLIT, (j + 1) * SPLIT)
        wide_rows = [ins[i * 24 : (i + 1) * 24, lanes] for i in range(3)] + [rest]
        block = [ups[j * 24 : (j + 1) * 24], jnp.concatenate(wide_rows, axis=1)]
        block += [ins[72 + j * 24 : 96 + j * 24]] + sums
        buf[j ^ me] = jnp.concatenate(block, axis=0).astype(low)
    for r, f in enumerate((f0, f1, f2, f3)):
        f[...] = buf[r]


def final_kernel(
    lengths, f0, f1, f2, f3, in_total, up_total, out_total, first, query, value, output, second, up_bias, down, stats, buf
):
    me = here()[0]
    for r, f in enumerate((f0, f1, f2, f3)):
        buf[r ^ me] = f[...].astype(wide)
    total = buf[0, 72:84] + buf[0, 84:96]
    for j in (1, 2, 3):
        total = total + (buf[j, 72:84] + buf[j, 84:96])
    first[...] = total[0]
    query[...] = total[1]
    value[...] = total[2]
    output[...] = total[3, :DC]
    second[...] = total[4]
    for i in range(4):
        up_bias[i * D : (i + 1) * D] = total[5 + i]
    down[...] = total[9, :DC]
    count = lengths[0, 0] + lengths[0, 1]
    for b in (1, 2, 3):
        count = count + lengths[b, 0] + lengths[b, 1]
    stats[...] = total[10, :2] / count.astype(wide)
    out_total[...] = (buf[0, 48:72] + buf[1, 48:72] + buf[2, 48:72] + buf[3, 48:72])[:, :DC]
    for j in range(4):
        up_total[:, j * D : (j + 1) * D] = buf[j, 0:24, :]
    for i in range(3):
        piece = jnp.concatenate([buf[j, 24:48, i * SPLIT : (i + 1) * SPLIT] for j in range(4)], axis=1)
        in_total[:, i * D : (i + 1) * D] = piece


def home_kernel(x0, x1, x2, x3, weight, resid, gain, middle_grad, out, buf):
    me = here()[0]
    for r, x in enumerate((x0, x1, x2, x3)):
        buf[r ^ me, 0:80, :] = x[192:272, 0:384]
        buf[r ^ me, 80:160, :] = x[192:272, 384:768]
        buf[r ^ me, 160:240, :] = x[272:352, 0:384]
    e = jnp.zeros((160, D), wide)
    for i in range(3):
        g = jnp.concatenate([unpacked(buf[j, i * 80 : (i + 1) * 80, :]) for j in range(4)], axis=1)
        e = e + nt(g.astype(low), weight[:, i * D : (i + 1) * D])
    full = full_of(resid[...].astype(wide))
    root = jnp.sqrt(jnp.mean(full * full, axis=1, keepdims=True) + epsilon)
    n = full / root
    eg = e * row(gain)
    f = (eg - n * jnp.mean(eg * n, axis=1, keepdims=True)) / root
    lane = lax.broadcasted_iota(jnp.int32, (160, D), 1)
    last = jnp.sum(jnp.where(lane == D - 1, f, 0.0), axis=1, keepdims=True)
    out[...] = (middle_grad[...] + f - last)[:, :DC].astype(low)


def down_sum_kernel(x0, x1, x2, x3, own, other):
    total = x0[0:192, :].astype(wide)
    for x in (x1, x2, x3):
        total = total + x[0:192, :].astype(wide)
    own[...] = total[0:96]
    other[...] = total[96:192].astype(low)


def down_final_kernel(own, came, down_total):
    down_total[...] = (own[...] + came[...].astype(wide))[:, :DC]

def swap_chip(block, step):
    return lax.ppermute(block, "blk", [(k, k ^ (2 * step)) for k in range(8)])


def swap_core(block):
    return lax.ppermute(block, "blk", [(k, k ^ 1) for k in range(8)])


def shift_bucket(block, step):
    return lax.ppermute(block, "bucket", [(b, b ^ step) for b in range(4)])


def exchange(blocks):
    got = {r: swap_chip(blocks[r], r) for r in (3, 1, 2)}
    return [blocks[0], got[1], got[2], got[3]]


def after(values, *others):
    return lax.optimization_barrier((tuple(values), others))[0]


def body(
    residual_in,
    out_cotangent,
    first_gain,
    input_weight,
    query_bias,
    value_bias,
    output_weight,
    output_bias,
    second_gain,
    up_weight,
    up_bias,
    down_weight,
    down_bias,
    lengths,
    offsets,
    span_order,
):
    where = [span_order, offsets, lengths]
    packed_block = ((240, 2 * SPLIT), low)
    token = ((160, D), low)
    s0, s1, s2, s3, hidden, root_one = call(
        entry_kernel,
        [packed_block] * 4 + [token, ((160, 1), wide)],
        [residual_in, first_gain, input_weight, query_bias, value_bias],
        [
            pltpu.VMEM((4, 240, 2 * SPLIT), low),
            pltpu.VMEM((160, DC), low),
            pltpu.VMEM((D,), wide),
            pltpu.VMEM((3, D, D), low),
            pltpu.VMEM((D,), wide),
            pltpu.VMEM((D,), wide),
            pltpu.SemaphoreType.DMA((7,)),
        ],
        extra=60,
        far=range(5),
    )
    got = exchange([s0, s1, s2, s3])
    push, bounds, places = call(
        push_kernel,
        [((160, FF), wide), ((640, 2), jnp.int32), ((1, 1280), jnp.int32)],
        where + [out_cotangent, down_weight],
        small=3,
    )
    hiddens = exchange([hidden] * 4)
    got = list(after(got, push))
    query, own_both = call(assemble_kernel, [((640, SPLIT), low), ((640, 2 * SPLIT), low)], got)
    sib_both = swap_core(own_both)
    backed = ((80, 2 * SPLIT), low)
    chance, attended, b0, b1, b2, b3 = call(
        forward_kernel,
        [((3, 640, 1280), low), ((640, SPLIT), wide)] + [backed] * 4,
        [bounds, places, query, own_both, sib_both],
        [pltpu.VMEM((1280, SPLIT), low), pltpu.VMEM((3, 1280, SPLIT), low), pltpu.VMEM((640, 1280), wide)],
        work=7,
    )
    back = exchange([b0, b1, b2, b3])
    (cot,) = after([out_cotangent], b0)
    cots = [out_cotangent, shift_bucket(cot, 1)]
    back = list(after(back, *hiddens[1:]))
    (columns,) = call(columns_kernel, [((D, 3 * SPLIT), low)], after([input_weight], b0))
    outs = call(
        middle_kernel,
        [backed] * 4
        + [((320, D), low)] * 6
        + [token, ((160, DC), wide), ((160, D), wide), ((16, D), wide)],
        [bounds]
        + back
        + [output_weight, output_bias, residual_in, root_one, out_cotangent, second_gain]
        + [up_weight, up_bias, push],
        [pltpu.VMEM((4, 80, 2 * SPLIT), low), pltpu.VMEM((4, 160, D), low), pltpu.VMEM((4, 320, D), low)],
    )
    act_keep, act_send = outs[4:6]
    lates = list(outs[6:10])
    branch_own, middle, middle_grad, vector = outs[10:]
    grads = exchange(outs[:4])
    grads = list(after(grads, cots[1]))
    (residual_out,) = call(
        closing_kernel,
        [((160, DC), low)],
        [act_keep, act_send, down_weight, middle, down_bias],
    )
    act_came = shift_bucket(act_send, 1)
    lates = exchange(after(lates, *grads[1:]))
    query_grad, both_grad, *away = call(
        backward_kernel,
        [((640, SPLIT), low), ((640, 2 * SPLIT), wide)] + [((320, 2 * SPLIT), low)] * 2,
        grads + [query, own_both, sib_both, chance, attended],
        [
            pltpu.VMEM((3, 1280, SPLIT), low),
            pltpu.VMEM((1280, SPLIT), low),
            pltpu.VMEM((640, SPLIT), low),
            pltpu.VMEM((640, 1280), low),
            pltpu.VMEM((SPLIT, 1280), wide),
            pltpu.VMEM((SPLIT, 1280), wide),
            pltpu.VMEM((640, 1280), wide),
        ],
    )
    arrived = [swap_core(x) for x in after(away, act_came)]
    arrived = list(after(arrived, lates[1], lates[2]))
    outs = call(
        late_kernel,
        [packed_block] * 4 + [((4, 192, D), low), ((4, 168, D), wide), ((1504, D), low)],
        [query_grad, both_grad] + arrived + hiddens + [act_keep, act_came] + cots + back + [branch_own, columns, first_gain, vector],
        [
            pltpu.VMEM((640, D), low),
            pltpu.VMEM((640, D), low),
            pltpu.VMEM((640, 3 * SPLIT), low),
            pltpu.VMEM((2, 4, 192, D), low),
            pltpu.VMEM((2, 4, 168, D), wide),
        ],
    )
    homes = list(outs[:4])
    keep_x, keep_z, send = outs[4:]
    outs = call(
        late_sum_kernel,
        [((352, D), low)] * 4 + [((336, D), wide), ((368, D), low)],
        [keep_x, keep_z, send, swap_core(send)] + homes,
    )
    home = exchange(outs[:4])
    z_keep, z_send = outs[4:]
    z_own, z_next = call(
        late_mid_kernel,
        [((168, D), wide), ((192, D), low)],
        [z_keep, z_send, shift_bucket(z_send, 1)],
    )
    z_came = shift_bucket(z_next, 2)
    keep, *send = call(
        up_grad_kernel,
        [((4, 96, D), low)] + [((128, D), low)] * 3,
        lates,
        [pltpu.VMEM((640, D), low), pltpu.VMEM((640, D), low), pltpu.VMEM((2, 4, 96, D), low)],
    )
    w_keep, w_send = call(
        up_sum_kernel,
        [((2, 96, D), wide), ((2, 96, D), low)],
        [keep] + [swap_core(x) for x in send],
    )
    w_own, w_next = call(
        up_mid_kernel,
        [((96, D), wide), ((96, D), low)],
        [w_keep, shift_bucket(w_send, 1)],
    )
    w_came = shift_bucket(w_next, 2)
    finals = call(
        final_send_kernel,
        [((96, D), low)] * 4,
        [z_own, z_next, z_came, w_own, w_came],
        [pltpu.VMEM((4, 96, D), low)],
    )
    down_own, down_other = call(down_sum_kernel, [((96, D), wide), ((96, D), low)], home)
    (down_total,) = call(
        down_final_kernel, [((96, DC), wide)], [down_own, shift_bucket(down_other, 2)]
    )
    (residual_grad,) = call(
        home_kernel,
        [((160, DC), low)],
        home + [input_weight, residual_in, first_gain, middle_grad],
        [pltpu.VMEM((4, 240, 2 * SPLIT), low)],
    )
    in_total, up_total, out_total, first, query_sum, value_sum, output, second, up_sum_bias, down, stats = call(
        final_kernel,
        [((24, 3 * D), wide), ((24, FF), wide), ((24, DC), wide)]
        + [((D,), wide)] * 3
        + [((DC,), wide), ((D,), wide), ((FF,), wide), ((DC,), wide), ((2,), wide)],
        [lengths] + exchange(finals),
        [pltpu.VMEM((4, 96, D), wide)],
        small=1,
    )
    return (
        residual_out,
        residual_grad,
        first,
        in_total,
        query_sum,
        value_sum,
        out_total,
        output,
        second,
        up_total,
        up_sum_bias,
        down_total,
        down,
        stats,
    )


def solution(mesh):
    placed = (
        P(("bucket", "blk"), None),
        P(("bucket", "blk"), None),
        P(),
        P(),
        P(),
        P(),
        P(),
        P(),
        P(),
        P(),
        P(),
        P(),
        P(),
        P(),
        P("bucket", None),
        P(),
    )
    return jax.shard_map(
        body if dict(mesh.shape) == {"bucket": 4, "blk": 8} else general_body,
        mesh=mesh,
        in_specs=placed,
        out_specs=(
            P(("bucket", "blk"), None),
            P(("bucket", "blk"), None),
            P(),
            P(("bucket", "blk"), None),
            P(),
            P(),
            P(("bucket", "blk"), None),
            P(),
            P(),
            P(("bucket", "blk"), None),
            P(),
            P(("bucket", "blk"), None),
            P(),
            P(),
        ),
        check_vma=False,
    )
```

```python
import jax
import jax.numpy as jnp
from jax import lax
from jax.experimental import pallas as pl
from jax.experimental.pallas import tpu as pltpu
from jax.sharding import PartitionSpec as P

D = 768
HEADS = 12
HEAD_DIM = 64


epsilon = 1e-05
masked_value = -1e30


def center_norm(resid, gain):
    full = jnp.concatenate([resid, -jnp.sum(resid, axis=1, keepdims=True)], axis=1)
    root = jnp.sqrt(jnp.mean(full * full, axis=1, keepdims=True) + epsilon)
    return (full / root * gain, root[:, 0])


def gelu_tanh(inputs):
    return jax.nn.gelu(inputs, approximate=True)


def heads_of(block):
    return block.reshape(block.shape[0], HEADS, HEAD_DIM)


def places_of(span_order, begin, count, half_rows):
    spans = lax.dynamic_slice_in_dim(span_order, begin // half_rows, count // half_rows)
    inner = jnp.arange(half_rows, dtype=jnp.int32)
    return (spans[:, None] * half_rows + inner[None, :]).reshape(count)


def documents_of(places, lengths, offsets):
    first_in = (places >= offsets[0, 0]) & (places < offsets[0, 0] + lengths[0, 0])
    second_in = (places >= offsets[0, 1]) & (places < offsets[0, 1] + lengths[0, 1])
    return jnp.where(first_in, 0, jnp.where(second_in, 1, -1)).astype(jnp.int32)


def allowed_of(query_places, query_docs, key_places, key_docs):
    same = (query_docs[:, None] == key_docs[None, :]) & (query_docs[:, None] >= 0)
    return (same & (key_places[None, :] <= query_places[:, None]))[None]


def block_shape(count, unit):
    shards = count // unit
    width = max(1, 1024 // unit)
    while shards % width != 0:
        width = width - 1
    return (shards // width, width * unit)


def general_body(
    residual_in,
    out_cotangent,
    first_gain,
    input_weight,
    query_bias,
    value_bias,
    output_weight,
    output_bias,
    second_gain,
    up_weight,
    up_bias,
    down_weight,
    down_bias,
    lengths,
    offsets,
    span_order,
):
    rows = residual_in.shape[0]
    half_rows = rows // 2
    score_scale = HEAD_DIM ** (-0.5)
    index = lax.axis_index("blk")
    bucket_index = lax.axis_index("bucket")
    own_lengths = lax.dynamic_slice_in_dim(lengths, bucket_index, 1, 0)
    valid_count = jnp.sum(lengths.astype(jnp.float32))
    query_places = places_of(span_order, index * rows, rows, half_rows)
    query_docs = documents_of(query_places, own_lengths, offsets)
    valid = (query_docs >= 0).astype(jnp.float32)
    resid = residual_in.astype(jnp.float32)
    normed, first_back, first_root = jax.vjp(center_norm, resid, first_gain, has_aux=True)
    hidden_in = normed.astype(jnp.bfloat16)
    projected = jnp.dot(hidden_in, input_weight, preferred_element_type=jnp.float32)
    query = (projected[:, :D] + query_bias).astype(jnp.bfloat16)
    keys = projected[:, D : 2 * D].astype(jnp.bfloat16)
    values = (projected[:, 2 * D :] + value_bias).astype(jnp.bfloat16)
    query_heads = heads_of(query)
    key_heads = heads_of(keys)
    value_heads = heads_of(values)
    initial = (
        jnp.full((HEADS, rows), masked_value, jnp.float32),
        jnp.zeros((HEADS, rows), jnp.float32),
        jnp.zeros((HEADS, rows, HEAD_DIM), jnp.float32),
    )
    state = initial
    key_piece = lax.all_gather(keys, "blk", axis=0, tiled=True)
    value_piece = lax.all_gather(values, "blk", axis=0, tiled=True)
    count = key_piece.shape[0]
    number, width = block_shape(count, rows)
    key_places = places_of(span_order, jnp.int32(0), count, half_rows)
    key_docs = documents_of(key_places, own_lengths, offsets)

    def forward_advance(state, parts):
        key_block, value_block, places_block, docs_block = parts
        peak, total, summed = state
        scores = (
            jnp.einsum(
                "qhd,khd->hqk", query_heads, heads_of(key_block), preferred_element_type=jnp.float32
            )
            * score_scale
        )
        allowed = allowed_of(query_places, query_docs, places_block, docs_block)
        masked = jnp.where(allowed, scores, masked_value)
        new_peak = jnp.maximum(peak, jnp.max(masked, axis=2))
        decay = jnp.exp(peak - new_peak)
        weights = jnp.where(allowed, jnp.exp(masked - new_peak[:, :, None]), 0.0)
        total = total * decay + jnp.sum(weights, axis=2)
        summed = summed * decay[:, :, None] + jnp.einsum(
            "hqk,khd->hqd",
            weights.astype(jnp.bfloat16),
            heads_of(value_block),
            preferred_element_type=jnp.float32,
        )
        return ((new_peak, total, summed), None)

    state, _ = lax.scan(
        forward_advance,
        state,
        (
            key_piece.reshape(number, width, D),
            value_piece.reshape(number, width, D),
            key_places.reshape(number, width),
            key_docs.reshape(number, width),
        ),
    )
    peak, total, summed = state
    denominator = total + 1.0 - valid[None, :]
    attended = summed / denominator[:, :, None]
    log_total = peak + jnp.log(denominator)
    mixed = attended.transpose(1, 0, 2).reshape(rows, D).astype(jnp.bfloat16)
    branch = jnp.dot(mixed, output_weight, preferred_element_type=jnp.float32) + output_bias
    middle = resid + branch
    normed_two, second_back, second_root = jax.vjp(center_norm, middle, second_gain, has_aux=True)
    hidden_two = normed_two.astype(jnp.bfloat16)
    upward = jnp.dot(hidden_two, up_weight, preferred_element_type=jnp.float32) + up_bias
    active_float, gelu_back = jax.vjp(gelu_tanh, upward)
    active = active_float.astype(jnp.bfloat16)
    closing = jnp.dot(active, down_weight, preferred_element_type=jnp.float32) + down_bias
    residual_out = (middle + closing).astype(jnp.bfloat16)
    stat_sums = jnp.stack([jnp.sum(valid * first_root), jnp.sum(valid * second_root)])
    stat_sums = lax.psum(stat_sums, ("bucket", "blk"))
    cotangent = out_cotangent.astype(jnp.float32)
    down_grad = jnp.einsum("rf,rc->fc", active, out_cotangent, preferred_element_type=jnp.float32)
    down_bias_grad = jnp.sum(cotangent, axis=0)
    active_grad = jnp.einsum(
        "rc,fc->rf", out_cotangent, down_weight, preferred_element_type=jnp.float32
    )
    (upward_float,) = gelu_back(active_grad)
    upward_grad = upward_float.astype(jnp.bfloat16)
    up_grad = jnp.einsum("rd,rf->df", hidden_two, upward_grad, preferred_element_type=jnp.float32)
    up_bias_grad = jnp.sum(upward_grad.astype(jnp.float32), axis=0)
    hidden_two_grad = jnp.einsum(
        "rf,df->rd", upward_grad, up_weight, preferred_element_type=jnp.float32
    )
    middle_part, second_gain_grad = second_back(hidden_two_grad)
    middle_grad = cotangent + middle_part
    branch_grad = middle_grad.astype(jnp.bfloat16)
    output_grad = jnp.einsum("rd,rc->dc", mixed, branch_grad, preferred_element_type=jnp.float32)
    output_bias_grad = jnp.sum(branch_grad.astype(jnp.float32), axis=0)
    attended_grad = jnp.einsum(
        "rc,dc->rd", branch_grad, output_weight, preferred_element_type=jnp.float32
    ).astype(jnp.bfloat16)
    grad_heads = heads_of(attended_grad)
    delta = jnp.einsum("rhd,hrd->hr", grad_heads.astype(jnp.float32), attended)
    query_zero = jnp.zeros((rows, HEADS, HEAD_DIM), jnp.float32)
    accum = query_zero
    key_piece = lax.all_gather(keys, "blk", axis=0, tiled=True)
    value_piece = lax.all_gather(values, "blk", axis=0, tiled=True)
    count = key_piece.shape[0]
    number, width = block_shape(count, rows)
    key_places = places_of(span_order, jnp.int32(0), count, half_rows)
    key_docs = documents_of(key_places, own_lengths, offsets)

    def query_advance(accum, parts):
        key_block, value_block, places_block, docs_block = parts
        block_keys = heads_of(key_block)
        scores = (
            jnp.einsum("qhd,khd->hqk", query_heads, block_keys, preferred_element_type=jnp.float32)
            * score_scale
        )
        allowed = allowed_of(query_places, query_docs, places_block, docs_block)
        chance = jnp.where(
            allowed, jnp.exp(jnp.where(allowed, scores, masked_value) - log_total[:, :, None]), 0.0
        )
        push = jnp.einsum(
            "qhd,khd->hqk", grad_heads, heads_of(value_block), preferred_element_type=jnp.float32
        )
        slope = (chance * (push - delta[:, :, None])).astype(jnp.bfloat16)
        accum = (
            accum
            + jnp.einsum("hqk,khd->qhd", slope, block_keys, preferred_element_type=jnp.float32)
            * score_scale
        )
        return (accum, None)

    accum, _ = lax.scan(
        query_advance,
        accum,
        (
            key_piece.reshape(number, width, D),
            value_piece.reshape(number, width, D),
            key_places.reshape(number, width),
            key_docs.reshape(number, width),
        ),
    )
    log_all, delta_all = (
        lax.all_gather(log_total.T, "blk", axis=0, tiled=True),
        lax.all_gather(delta.T, "blk", axis=0, tiled=True),
    )
    key_zero = jnp.zeros((rows, HEADS, HEAD_DIM), jnp.float32)
    state = (key_zero, key_zero)
    begin = jnp.int32(0)
    query_piece = lax.all_gather(query, "blk", axis=0, tiled=True)
    grad_piece = lax.all_gather(attended_grad, "blk", axis=0, tiled=True)
    count = query_piece.shape[0]
    number, width = block_shape(count, rows)
    piece_places = places_of(span_order, begin, count, half_rows)
    piece_docs = documents_of(piece_places, own_lengths, offsets)
    piece_log = lax.dynamic_slice_in_dim(log_all, begin, count, 0)
    piece_delta = lax.dynamic_slice_in_dim(delta_all, begin, count, 0)

    def key_advance(state, parts):
        query_block, grad_block, places_block, docs_block, log_block, delta_block = parts
        key_sum, value_sum = state
        block_query = heads_of(query_block)
        block_grad = heads_of(grad_block)
        scores = (
            jnp.einsum("qhd,khd->hqk", block_query, key_heads, preferred_element_type=jnp.float32)
            * score_scale
        )
        allowed = allowed_of(places_block, docs_block, query_places, query_docs)
        chance = jnp.where(
            allowed,
            jnp.exp(jnp.where(allowed, scores, masked_value) - log_block.T[:, :, None]),
            0.0,
        )
        value_sum = value_sum + jnp.einsum(
            "hqk,qhd->khd",
            chance.astype(jnp.bfloat16),
            block_grad,
            preferred_element_type=jnp.float32,
        )
        push = jnp.einsum(
            "qhd,khd->hqk", block_grad, value_heads, preferred_element_type=jnp.float32
        )
        slope = (chance * (push - delta_block.T[:, :, None])).astype(jnp.bfloat16)
        key_sum = (
            key_sum
            + jnp.einsum("hqk,qhd->khd", slope, block_query, preferred_element_type=jnp.float32)
            * score_scale
        )
        return ((key_sum, value_sum), None)

    state, _ = lax.scan(
        key_advance,
        state,
        (
            query_piece.reshape(number, width, D),
            grad_piece.reshape(number, width, D),
            piece_places.reshape(number, width),
            piece_docs.reshape(number, width),
            piece_log.reshape(number, width, HEADS),
            piece_delta.reshape(number, width, HEADS),
        ),
    )
    key_sum, value_sum = state
    query_low = accum.reshape(rows, D).astype(jnp.bfloat16)
    key_low = key_sum.reshape(rows, D).astype(jnp.bfloat16)
    value_low = value_sum.reshape(rows, D).astype(jnp.bfloat16)
    projected_grad = jnp.concatenate([query_low, key_low, value_low], axis=1)
    input_grad = jnp.einsum(
        "rd,re->de", hidden_in, projected_grad, preferred_element_type=jnp.float32
    )
    query_bias_grad = jnp.sum(query_low.astype(jnp.float32), axis=0)
    value_bias_grad = jnp.sum(value_low.astype(jnp.float32), axis=0)
    hidden_in_grad = jnp.einsum(
        "re,de->rd", projected_grad, input_weight, preferred_element_type=jnp.float32
    )
    resid_part, first_gain_grad = first_back(hidden_in_grad)
    residual_grad = (middle_grad + resid_part).astype(jnp.bfloat16)
    input_part, output_part, up_part, down_part = (
        lax.psum_scatter(input_grad, ("bucket", "blk"), scatter_dimension=0, tiled=True),
        lax.psum_scatter(output_grad, ("bucket", "blk"), scatter_dimension=0, tiled=True),
        lax.psum_scatter(up_grad, ("bucket", "blk"), scatter_dimension=0, tiled=True),
        lax.psum_scatter(down_grad, ("bucket", "blk"), scatter_dimension=0, tiled=True),
    )
    (
        first_sum,
        query_sum_bias,
        value_sum_bias,
        output_sum_bias,
        second_sum,
        up_sum_bias,
        down_sum_bias,
    ) = lax.psum(
        (
            first_gain_grad,
            query_bias_grad,
            value_bias_grad,
            output_bias_grad,
            second_gain_grad,
            up_bias_grad,
            down_bias_grad,
        ),
        ("bucket", "blk"),
    )
    mean_norms = stat_sums / valid_count
    return (
        residual_out,
        residual_grad,
        first_sum,
        input_part,
        query_sum_bias,
        value_sum_bias,
        output_part,
        output_sum_bias,
        second_sum,
        up_part,
        up_sum_bias,
        down_part,
        down_sum_bias,
        mean_norms,
    )


DC = 767
SPLIT = 192
FF = 3072
low = jnp.bfloat16
wide = jnp.float32
VMEM = pl.BlockSpec(memory_space=pltpu.VMEM)
SMEM = pl.BlockSpec(memory_space=pltpu.SMEM)
HBM = pl.BlockSpec(memory_space=pltpu.HBM)

def padded_bytes(shape, dtype):
    shape = (1, 1) + tuple(shape)
    size = jnp.dtype(dtype).itemsize
    rows, lanes = -(-shape[-2] // 16) * 16, -(-shape[-1] // 128) * 128
    for d in shape[:-2]:
        rows = rows * d
    return rows * lanes * size


def call(kernel, outs, ins, scratch=(), extra=6, small=0, far=(), work=0):
    shapes = [jax.ShapeDtypeStruct(s, d) for s, d in outs]
    held = [(s, d) for s, d in outs]
    held += [(x.shape, x.dtype) for i, x in enumerate(ins) if i >= small and i not in far]
    held += [(s.shape, s.dtype) for s in scratch if s.memory_space == pltpu.VMEM]
    limit = sum(padded_bytes(s, d) for s, d in held) + extra * 2**20
    return pl.pallas_call(
        kernel,
        out_shape=shapes,
        in_specs=[SMEM if i < small else HBM if i in far else VMEM for i in range(len(ins))],
        out_specs=[VMEM] * len(outs),
        scratch_shapes=list(scratch),
        compiler_params=pltpu.CompilerParams(vmem_limit_bytes=min(limit, 60 * 2**20)),
        cost_estimate=pl.CostEstimate(
            flops=int(1000 + work * 1.1e9),
            bytes_accessed=1000,
            transcendentals=0,
        ),
    )(*ins)


def here():
    index = lax.axis_index("blk")
    return index // 2, lax.axis_index("bucket"), index % 2


def full_of(x):
    rows=x.shape[0]
    wide_x=jnp.concatenate([x,jnp.zeros((rows,1),x.dtype)],axis=1)
    last=lax.broadcasted_iota(jnp.int32,(rows,D),1)==D-1
    return jnp.where(last,-jnp.sum(x,axis=1,keepdims=True),wide_x)

def row(ref):
    return ref[...].reshape(1, ref.shape[0])


def nt(a, b):
    return lax.dot_general(a, b, (((1,), (1,)), ((), ())), preferred_element_type=wide)


def tn(a, b):
    return lax.dot_general(a, b, (((0,), (0,)), ((), ())), preferred_element_type=wide)


def packed(x):
    half = x.shape[0] // 2
    return jnp.concatenate([x[:half], x[half:]], axis=1).astype(low)


def unpacked(x):
    x = x.astype(wide)
    half = x.shape[1] // 2
    return jnp.concatenate([x[:, :half], x[:, half:]], axis=0)


def split_pair(x):
    hi = x.astype(low)
    return hi, (x - hi.astype(wide)).astype(low)


def head_mask(x, h):
    lane = lax.broadcasted_iota(jnp.int32, x.shape, 1)
    return jnp.where((lane >= h * 64) & (lane < (h + 1) * 64), x, jnp.zeros_like(x))


def limits(spans, offsets, lengths, bucket, chip, core, half):
    place = spans[chip * 4 + core * 2 + half] * 80 + lax.broadcasted_iota(jnp.int32, (80, 1), 0)
    one, two = offsets[0, 0], offsets[0, 1]
    first = (place >= one) & (place < one + lengths[bucket, 0])
    second = (place >= two) & (place < two + lengths[bucket, 1])
    return jnp.where(first, one, two), jnp.where(first | second, place, -1)


def entry_kernel(
    resid_far, gain_far, weight_far, qbias_far, vbias_far, s0, s1, s2, s3, hidden_out, root_out,
    buf, resid, gain, weight, qbias, vbias, sems,
):
    me = here()[0]
    copies = [
        pltpu.make_async_copy(a, b, sems.at[i])
        for i, (a, b) in enumerate(
            [(resid_far, resid), (gain_far, gain), (qbias_far, qbias), (vbias_far, vbias)]
            + [(weight_far.at[:, pl.ds(i * D, D)], weight.at[i]) for i in range(3)]
        )
    ]
    for copy in copies:
        copy.start()
    copies[0].wait()
    full = full_of(resid[...].astype(wide))
    root = jnp.sqrt(jnp.mean(full * full, axis=1, keepdims=True) + epsilon)
    root_out[...] = root
    copies[1].wait()
    hidden = (full / root * row(gain)).astype(low)
    hidden_out[...] = hidden
    copies[2].wait()
    copies[3].wait()
    for i in range(3):
        copies[4 + i].wait()
        p = jnp.dot(hidden, weight[i], preferred_element_type=wide)
        if i == 0:
            p = (p + row(qbias)) * 0.125
        if i == 2:
            p = p + row(vbias)
        for j in range(4):
            buf[j ^ me, i * 80 : (i + 1) * 80, :] = packed(p[:, j * SPLIT : (j + 1) * SPLIT])
    for r, s in enumerate((s0, s1, s2, s3)):
        s[...] = buf[r]


def push_kernel(spans, offsets, lengths, cot, weight, out, bounds, places):
    me, bucket, core = here()
    for i in range(4):
        out[:, i * D : (i + 1) * D] = nt(cot[...], weight[i * D : (i + 1) * D, :])
    lane = lax.broadcasted_iota(jnp.int32, (1, 1280), 1)
    place = lane
    for blk in range(16):
        chip = ((blk % 8) // 2) ^ me
        span = spans[chip * 4 + (core ^ (blk // 8)) * 2 + blk % 2]
        place = jnp.where((lane >= blk * 80) & (lane < (blk + 1) * 80), lane + (span - blk) * 80, place)
    places[...] = place
    for blk in range(8):
        lo, hi = limits(spans, offsets, lengths, bucket, (blk // 2) ^ me, core, blk % 2)
        bounds[blk * 80 : (blk + 1) * 80, 0:1] = lo
        bounds[blk * 80 : (blk + 1) * 80, 1:2] = hi


def columns_kernel(weight, out):
    me = here()[0]
    for j in range(4):

        @pl.when(me == j)
        def _():
            for i in range(3):
                piece = weight[:, i * D + j * SPLIT : i * D + (j + 1) * SPLIT].astype(wide)
                out[:, i * SPLIT : (i + 1) * SPLIT] = piece.astype(low)


def assemble_kernel(p0, p1, p2, p3, query, both):
    for r, p in enumerate((p0, p1, p2, p3)):
        rows = slice(r * 160, (r + 1) * 160)
        query[rows, :] = unpacked(p[0:80, :]).astype(low)
        both[rows, :SPLIT] = unpacked(p[80:160, :]).astype(low)
        both[rows, SPLIT:] = unpacked(p[160:240, :]).astype(low)


def forward_kernel(
    bounds, places, query, own, sib, chance, attended, b0, b1, b2, b3, keys, vals, scores
):
    keys[:640, :] = own[:, :SPLIT]
    keys[640:, :] = sib[:, :SPLIT]
    v = jnp.concatenate([own[:, SPLIT:].astype(wide), sib[:, SPLIT:].astype(wide)], axis=0)
    for h in range(3):
        vals[h] = head_mask(v, h).astype(low)
    place = places[...]
    q = query[...].astype(wide)
    for h in range(3):
        scores[...] = nt(head_mask(q, h).astype(low), keys[...])
        for blk in range(8):
            rows = slice(blk * 80, (blk + 1) * 80)
            lo, hi = bounds[rows, 0:1], bounds[rows, 1:2]
            s = jnp.where((place >= lo) & (place <= hi), scores[rows, :], masked_value)
            peak = jnp.max(s, axis=1, keepdims=True)
            w = jnp.exp(s - peak)
            total = jnp.sum(w, axis=1, keepdims=True)
            chance[h, rows, :] = (w * jnp.where(hi >= 0, 1.0 / total, 0.0)).astype(low)
        part = jnp.dot(chance[h], vals[h], preferred_element_type=wide)
        if h == 0:
            attended[...] = part
        else:
            attended[...] += part
    acc = attended[...]
    for r, b in enumerate((b0, b1, b2, b3)):
        b[...] = packed(acc[r * 160 : (r + 1) * 160])


def middle_kernel(
    bounds, p0, p1, p2, p3, out_weight, out_bias, resid, root_in, cot, gain, up_weight, up_bias, push,
    d0, d1, d2, d3, act_keep, act_send, n0, n1, n2, n3, branch_own, middle, middle_grad, vector,
    dbuf, abuf, nbuf,
):
    me, bucket, core = here()
    branch = row(out_bias)
    for r, p in enumerate((p0, p1, p2, p3)):
        w = out_weight[pl.ds(pl.multiple_of((me ^ r) * SPLIT, SPLIT), SPLIT), :]
        branch = branch + jnp.dot(unpacked(p[...]).astype(low), w, preferred_element_type=wide)
    mid = resid[...].astype(wide) + branch
    middle[...] = mid
    full = full_of(mid)
    root = jnp.sqrt(jnp.mean(full * full, axis=1, keepdims=True) + epsilon)
    n = full / root
    hidden = (n * row(gain)).astype(low)
    for r in range(4):
        nbuf[r, 0:160, :] = hidden
    e = jnp.zeros((160, D), wide)
    c = 0.7978845608028654
    up_sums = []
    for blk in range(4):
        cols = slice(blk * D, (blk + 1) * D)
        u = jnp.dot(hidden, up_weight[:, cols], preferred_element_type=wide) + up_bias[cols].reshape(1, D)
        square = u * u
        t = jnp.tanh(u * (c + (c * 0.044715) * square))
        gate = 0.5 + 0.5 * t
        act = u * gate
        abuf[blk ^ bucket] = act.astype(low)
        slope = gate + act * (1.0 - t) * (c + (3 * c * 0.044715) * square)
        g = (push[:, cols] * slope).astype(low)
        nbuf[blk ^ me, 160:320, :] = g
        up_sums.append(jnp.sum(g.astype(wide), axis=0, keepdims=True))
        e = e + nt(g, up_weight[:, cols])
    gain_sum = jnp.sum(e * n, axis=0, keepdims=True)
    eg = e * row(gain)
    f = (eg - n * jnp.mean(eg * n, axis=1, keepdims=True)) / root
    cot_wide = jnp.concatenate([cot[...].astype(wide), jnp.zeros((160, 1), wide)], axis=1)
    lane = lax.broadcasted_iota(jnp.int32, (160, D), 1)
    last = jnp.sum(jnp.where(lane == D - 1, f, 0.0), axis=1, keepdims=True)
    grad = jnp.where(lane == D - 1, 0.0, cot_wide + f - last)
    middle_grad[...] = grad
    grad_low = grad.astype(low)
    grad_wide = grad_low.astype(wide)
    branch_own[...] = grad_low
    back = nt(grad_wide[:, :DC].astype(low), out_weight[...])
    for j in range(4):
        dbuf[j ^ me] = packed(back[:, j * SPLIT : (j + 1) * SPLIT])
    for r in range(4):
        (d0, d1, d2, d3)[r][...] = dbuf[r]
        (act_keep, act_send)[r % 2][r // 2 * 160 : r // 2 * 160 + 160, :] = abuf[r]
        (n0, n1, n2, n3)[r][...] = nbuf[r]
    valid = jnp.where(bounds[0:160, 1:2] >= 0, 1.0, 0.0)
    one = jnp.sum(valid * root_in[...], axis=0, keepdims=True)
    two = jnp.sum(valid * root, axis=0, keepdims=True)
    at = lax.broadcasted_iota(jnp.int32, (1, D), 1)
    stats = jnp.where(at == 0, one, jnp.where(at == 1, two, 0.0))
    zero = jnp.zeros((1, D), wide)
    sums = [zero, zero, zero, jnp.sum(grad_wide, axis=0, keepdims=True), gain_sum] + up_sums
    sums += [jnp.sum(cot_wide, axis=0, keepdims=True), stats] + [zero] * 5
    vector[...] = jnp.concatenate(sums, axis=0)


def closing_kernel(act_keep, act_send, weight, middle, bias, out):
    bucket = here()[1]
    acc = middle[...] + row(bias)
    for d in range(4):
        w = weight[pl.ds(pl.multiple_of((bucket ^ d) * D, D), D), :]
        a = (act_keep, act_send)[d % 2][d // 2 * 160 : d // 2 * 160 + 160, :]
        acc = acc + jnp.dot(a, w, preferred_element_type=wide)
    out[...] = acc.astype(low)


def backward_kernel(
    d0, d1, d2, d3, query, own, sib, chance, attended, query_grad, both_grad, away_one, away_two,
    keys, vals, grads, slopes, keys_turned, vals_turned, pushes,
):
    for r, d in enumerate((d0, d1, d2, d3)):
        grads[r * 160 : (r + 1) * 160, :] = unpacked(d[...]).astype(low)
    k = jnp.concatenate([own[:, :SPLIT], sib[:, :SPLIT]], axis=0).astype(wide)
    for h in range(3):
        keys[h] = head_mask(k, h).astype(low)
    vals[:640, :] = own[:, SPLIT:].astype(wide).astype(low)
    vals[640:, :] = sib[:, SPLIT:].astype(wide).astype(low)
    g = grads[...].astype(wide)
    q_turned = jnp.transpose(query[...].astype(wide)).astype(low)
    g_turned = jnp.transpose(g).astype(low)
    dq = jnp.zeros((640, SPLIT), wide)
    for h in range(3):
        gh = head_mask(g, h)
        delta = jnp.sum(gh * attended[...], axis=1, keepdims=True)
        pushes[...] = nt(gh.astype(low), vals[...])
        for r in range(8):
            rows = slice(r * 80, (r + 1) * 80)
            slopes[rows, :] = (chance[h, rows, :].astype(wide) * (pushes[rows, :] - delta[rows, :])).astype(low)
        dq = dq + jnp.dot(slopes[...], keys[h], preferred_element_type=wide)
        rows = slice(h * 64, (h + 1) * 64)
        keys_turned[rows, :] = jnp.dot(q_turned[rows], slopes[...], preferred_element_type=wide)
        vals_turned[rows, :] = jnp.dot(g_turned[rows], chance[h], preferred_element_type=wide)
    query_grad[...] = (dq * 0.125).astype(low)
    dk = jnp.transpose(keys_turned[...])
    dv = jnp.transpose(vals_turned[...])
    both_grad[:, :SPLIT] = dk[:640]
    both_grad[:, SPLIT:] = dv[:640]
    away_one[:, :SPLIT] = dk[640:960].astype(low)
    away_one[:, SPLIT:] = dv[640:960].astype(low)
    away_two[:, :SPLIT] = dk[960:].astype(low)
    away_two[:, SPLIT:] = dv[960:].astype(low)


def late_kernel(
    query_grad, both_grad, arrive_one, arrive_two, i0, i1, i2, i3, act_keep, act_came, c0, c1, p0, p1, p2, p3, branch_own, columns, gain, vector,
    h0, h1, h2, h3, keep_x, keep_z, send, left, right, heads, xbuf, zbuf,
):
    me, bucket, core = here()
    arrived = jnp.concatenate([arrive_one[...].astype(wide), arrive_two[...].astype(wide)], axis=0)
    both = both_grad[...] + arrived
    parts = [query_grad[...].astype(wide), both[:, :SPLIT], both[:, SPLIT:]]
    parts = [p.astype(low).astype(wide) for p in parts]
    for r, h in enumerate((h0, h1, h2, h3)):
        left[r * 160 : (r + 1) * 160, :] = (i0, i1, i2, i3)[r][...]
        for i in range(3):
            h[i * 80 : (i + 1) * 80, :] = packed(parts[i][r * 160 : (r + 1) * 160])
    heads[...] = jnp.concatenate(parts, axis=1).astype(low)
    grad = tn(left[...], heads[...])
    sums = jnp.sum(grad * columns[...].astype(wide), axis=1, keepdims=True)
    gain_row = jnp.transpose(jnp.broadcast_to(sums, (D, 128)))[0:1] / row(gain)
    lane = lax.broadcasted_iota(jnp.int32, (1, D), 1)
    mine = (lane >= me * SPLIT) & (lane < (me + 1) * SPLIT)

    def column_sum(x):
        s = jnp.sum(x, axis=0, keepdims=True)
        return jnp.where(mine, jnp.concatenate([s] * 4, axis=1), 0.0)

    at = lax.broadcasted_iota(jnp.int32, (16, D), 0)
    total = vector[...] + jnp.where(at == 0, gain_row, 0.0)
    total = total + jnp.where(at == 1, column_sum(parts[0]), 0.0)
    total = total + jnp.where(at == 2, column_sum(parts[2]), 0.0)
    thirds = [grad[:, i * SPLIT : (i + 1) * SPLIT] for i in range(3)]
    for b in range(4):
        for c in range(2):
            block = []
            for part in thirds:
                starts = [b * 192 + j * 48 + c * 24 for j in range(4)]
                block.append(jnp.concatenate([part[s : s + 24] for s in starts], axis=1))
            zbuf[c ^ core, b ^ bucket, 0:72, :] = jnp.concatenate(block, axis=0)
    for r, p in enumerate((p0, p1, p2, p3)):
        out = tn(unpacked(p[...]).astype(low), branch_own[...])
        for j in range(4):
            for c in range(2):
                s = j * 48 + c * 24
                zbuf[c ^ core, me ^ r ^ bucket, 72 + j * 24 : 96 + j * 24, :] = out[s : s + 24]
    for d, c in enumerate((c0, c1)):
        cot = c[...].astype(wide)
        right[d * 160 : (d + 1) * 160, :] = jnp.concatenate([cot, jnp.zeros((160, 1), wide)], axis=1).astype(low)
    for half in range(2):
        left[0:160, :] = act_keep[half * 160 : half * 160 + 160, :]
        left[160:320, :] = act_came[half * 160 : half * 160 + 160, :]
        down = tn(left[0:320, :], right[0:320, :])
        for j in range(4):
            for c in range(2):
                s = j * 192 + c * 96
                xbuf[c ^ core, j ^ me, half * 96 : half * 96 + 96, :] = down[s : s + 96].astype(low)
    keep_x[...] = xbuf[0]
    for r in range(4):
        keep_z[r] = zbuf[0, r]
        send[r * 192 : (r + 1) * 192, :] = xbuf[1, r]
        block = jnp.concatenate([zbuf[1, r], jnp.zeros((8, D), wide)], axis=0)
        send[768 + r * 176 : 944 + r * 176, :] = block.astype(low)
    hi, lo = split_pair(total)
    send[1472:1488, :] = hi
    send[1488:1504, :] = lo


def late_sum_kernel(keep_x, keep_z, send, arrived, h0, h1, h2, h3, x0, x1, x2, x3, z_keep, z_send):
    own = send[1472:1488, :].astype(wide) + send[1488:1504, :].astype(wide)
    hi, lo = split_pair(own + (arrived[1472:1488, :].astype(wide) + arrived[1488:1504, :].astype(wide)))
    blocks = []
    for r in range(4):
        x, h = (x0, x1, x2, x3)[r], (h0, h1, h2, h3)[r]
        x[0:192, :] = (keep_x[r].astype(wide) + arrived[r * 192 : (r + 1) * 192, :].astype(wide)).astype(low)
        x[192:272, 0:384] = h[0:80, :]
        x[192:272, 384:768] = h[80:160, :]
        v = h[160:240, :].astype(wide)
        v = jnp.concatenate([v[:40], v[40:]], axis=1)
        x[272:320, :] = jnp.concatenate([v, jnp.zeros((8, D), wide)], axis=0).astype(low)
        came = arrived[768 + r * 176 : 944 + r * 176, :].astype(wide)
        blocks.append(keep_z[r] + came[0:168])
    z_keep[0:168, :] = blocks[0]
    z_keep[168:336, :] = blocks[2]
    sums = [hi.astype(wide)[0:12], lo.astype(wide)[0:12], jnp.zeros((8, D), wide)]
    z_send[...] = jnp.concatenate([blocks[1], blocks[3]] + sums, axis=0).astype(low)


def pair_sum(own, came, start):
    a = own[start : start + 12] + own[start + 12 : start + 24]
    b = came[start : start + 12] + came[start + 12 : start + 24]
    return a + b


def late_mid_kernel(z_keep, z_send, came, z_own, z_next):
    came = came[...].astype(wide)
    hi, lo = split_pair(pair_sum(z_send[...].astype(wide), came, 336))
    z_own[...] = z_keep[0:168, :] + came[0:168]
    block = [z_keep[168:336, :] + came[168:336], hi.astype(wide), lo.astype(wide)]
    z_next[...] = jnp.concatenate(block, axis=0).astype(low)


def up_grad_kernel(n0, n1, n2, n3, keep, send_one, send_two, send_three, left, right, buf):
    me, bucket, core = here()
    for r in range(4):
        rows = slice(r * 160, (r + 1) * 160)
        n = (n0, n1, n2, n3)[r]
        left[rows, :] = n[0:160, :]
        right[rows, :] = n[160:320, :]
    up = tn(left[...], right[...])
    for b in range(4):
        for c in range(2):
            starts = [b * 192 + j * 48 + c * 24 for j in range(4)]
            block = jnp.concatenate([up[s : s + 24] for s in starts], axis=0)
            buf[c ^ core, b ^ bucket] = block.astype(low)
    keep[...] = buf[0]
    send_one[0:96, :] = buf[1, 0]
    send_one[96:128, :] = buf[1, 1, 0:32, :]
    send_two[0:64, :] = buf[1, 1, 32:96, :]
    send_two[64:128, :] = buf[1, 2, 0:64, :]
    send_three[0:32, :] = buf[1, 2, 64:96, :]
    send_three[32:128, :] = buf[1, 3]


def up_sum_kernel(keep, arrive_one, arrive_two, arrive_three, w_keep, w_send):
    parts = [a[...].astype(wide) for a in (arrive_one, arrive_two, arrive_three)]
    arrived = jnp.concatenate(parts, axis=0)
    for d in range(4):
        total = keep[d].astype(wide) + arrived[d * 96 : (d + 1) * 96]
        if d % 2 == 0:
            w_keep[d // 2] = total
        else:
            w_send[d // 2] = total.astype(low)


def up_mid_kernel(w_keep, came, w_own, w_next):
    w_own[...] = w_keep[0] + came[0].astype(wide)
    w_next[...] = (w_keep[1] + came[1].astype(wide)).astype(low)


def final_send_kernel(z_own, z_next, z_came, w_own, w_came, f0, f1, f2, f3, buf):
    me = here()[0]
    came = z_came[...].astype(wide)
    ins = z_own[...] + came[0:168]
    ups = w_own[...] + w_came[...].astype(wide)
    hi, lo = split_pair(pair_sum(z_next[...].astype(wide), came, 168))
    sums = [hi.astype(wide), lo.astype(wide)]
    rest = jnp.zeros((24, SPLIT), wide)
    for j in range(4):
        lanes = slice(j * SPLIT, (j + 1) * SPLIT)
        wide_rows = [ins[i * 24 : (i + 1) * 24, lanes] for i in range(3)] + [rest]
        block = [ups[j * 24 : (j + 1) * 24], jnp.concatenate(wide_rows, axis=1)]
        block += [ins[72 + j * 24 : 96 + j * 24]] + sums
        buf[j ^ me] = jnp.concatenate(block, axis=0).astype(low)
    for r, f in enumerate((f0, f1, f2, f3)):
        f[...] = buf[r]


def final_kernel(
    lengths, f0, f1, f2, f3, in_total, up_total, out_total, first, query, value, output, second, up_bias, down, stats, buf
):
    me = here()[0]
    for r, f in enumerate((f0, f1, f2, f3)):
        buf[r ^ me] = f[...].astype(wide)
    total = buf[0, 72:84] + buf[0, 84:96]
    for j in (1, 2, 3):
        total = total + (buf[j, 72:84] + buf[j, 84:96])
    first[...] = total[0]
    query[...] = total[1]
    value[...] = total[2]
    output[...] = total[3, :DC]
    second[...] = total[4]
    for i in range(4):
        up_bias[i * D : (i + 1) * D] = total[5 + i]
    down[...] = total[9, :DC]
    count = lengths[0, 0] + lengths[0, 1]
    for b in (1, 2, 3):
        count = count + lengths[b, 0] + lengths[b, 1]
    stats[...] = total[10, :2] / count.astype(wide)
    out_total[...] = (buf[0, 48:72] + buf[1, 48:72] + buf[2, 48:72] + buf[3, 48:72])[:, :DC]
    for j in range(4):
        up_total[:, j * D : (j + 1) * D] = buf[j, 0:24, :]
    for i in range(3):
        piece = jnp.concatenate([buf[j, 24:48, i * SPLIT : (i + 1) * SPLIT] for j in range(4)], axis=1)
        in_total[:, i * D : (i + 1) * D] = piece


def home_kernel(x0, x1, x2, x3, weight, resid, gain, middle_grad, out, buf):
    me = here()[0]
    for r, x in enumerate((x0, x1, x2, x3)):
        buf[r ^ me, 0:80, :] = x[192:272, 0:384]
        buf[r ^ me, 80:160, :] = x[192:272, 384:768]
        v = x[272:320, :].astype(wide)
        buf[r ^ me, 160:240, :] = jnp.concatenate([v[:40, :384], v[:40, 384:]], axis=0).astype(low)
    e = jnp.zeros((160, D), wide)
    for i in range(3):
        g = jnp.concatenate([unpacked(buf[j, i * 80 : (i + 1) * 80, :]) for j in range(4)], axis=1)
        e = e + nt(g.astype(low), weight[:, i * D : (i + 1) * D])
    full = full_of(resid[...].astype(wide))
    root = jnp.sqrt(jnp.mean(full * full, axis=1, keepdims=True) + epsilon)
    n = full / root
    eg = e * row(gain)
    f = (eg - n * jnp.mean(eg * n, axis=1, keepdims=True)) / root
    lane = lax.broadcasted_iota(jnp.int32, (160, D), 1)
    last = jnp.sum(jnp.where(lane == D - 1, f, 0.0), axis=1, keepdims=True)
    out[...] = (middle_grad[...] + f - last)[:, :DC].astype(low)


def down_sum_kernel(x0, x1, x2, x3, own, other):
    total = x0[0:192, :].astype(wide)
    for x in (x1, x2, x3):
        total = total + x[0:192, :].astype(wide)
    own[...] = total[0:96]
    other[...] = total[96:192].astype(low)


def down_final_kernel(own, came, down_total):
    down_total[...] = (own[...] + came[...].astype(wide))[:, :DC]

def swap_chip(block, step):
    return lax.ppermute(block, "blk", [(k, k ^ (2 * step)) for k in range(8)])


def swap_core(block):
    return lax.ppermute(block, "blk", [(k, k ^ 1) for k in range(8)])


def shift_bucket(block, step):
    return lax.ppermute(block, "bucket", [(b, b ^ step) for b in range(4)])


def exchange(blocks):
    got = {r: swap_chip(blocks[r], r) for r in (3, 1, 2)}
    return [blocks[0], got[1], got[2], got[3]]


def after(values, *others):
    return lax.optimization_barrier((tuple(values), others))[0]


def body(
    residual_in,
    out_cotangent,
    first_gain,
    input_weight,
    query_bias,
    value_bias,
    output_weight,
    output_bias,
    second_gain,
    up_weight,
    up_bias,
    down_weight,
    down_bias,
    lengths,
    offsets,
    span_order,
):
    where = [span_order, offsets, lengths]
    packed_block = ((240, 2 * SPLIT), low)
    token = ((160, D), low)
    s0, s1, s2, s3, hidden, root_one = call(
        entry_kernel,
        [packed_block] * 4 + [token, ((160, 1), wide)],
        [residual_in, first_gain, input_weight, query_bias, value_bias],
        [
            pltpu.VMEM((4, 240, 2 * SPLIT), low),
            pltpu.VMEM((160, DC), low),
            pltpu.VMEM((D,), wide),
            pltpu.VMEM((3, D, D), low),
            pltpu.VMEM((D,), wide),
            pltpu.VMEM((D,), wide),
            pltpu.SemaphoreType.DMA((7,)),
        ],
        extra=60,
        far=range(5),
    )
    got = exchange([s0, s1, s2, s3])
    push, bounds, places = call(
        push_kernel,
        [((160, FF), wide), ((640, 2), jnp.int32), ((1, 1280), jnp.int32)],
        where + [out_cotangent, down_weight],
        small=3,
    )
    hiddens = exchange([hidden] * 4)
    got = list(after(got, push))
    query, own_both = call(assemble_kernel, [((640, SPLIT), low), ((640, 2 * SPLIT), low)], got)
    sib_both = swap_core(own_both)
    backed = ((80, 2 * SPLIT), low)
    chance, attended, b0, b1, b2, b3 = call(
        forward_kernel,
        [((3, 640, 1280), low), ((640, SPLIT), wide)] + [backed] * 4,
        [bounds, places, query, own_both, sib_both],
        [pltpu.VMEM((1280, SPLIT), low), pltpu.VMEM((3, 1280, SPLIT), low), pltpu.VMEM((640, 1280), wide)],
        work=7,
    )
    back = exchange([b0, b1, b2, b3])
    (cot,) = after([out_cotangent], b0)
    cots = [out_cotangent, shift_bucket(cot, 1)]
    back = list(after(back, *hiddens[1:]))
    (columns,) = call(columns_kernel, [((D, 3 * SPLIT), low)], after([input_weight], b0))
    outs = call(
        middle_kernel,
        [backed] * 4
        + [((320, D), low)] * 6
        + [token, ((160, DC), wide), ((160, D), wide), ((16, D), wide)],
        [bounds]
        + back
        + [output_weight, output_bias, residual_in, root_one, out_cotangent, second_gain]
        + [up_weight, up_bias, push],
        [pltpu.VMEM((4, 80, 2 * SPLIT), low), pltpu.VMEM((4, 160, D), low), pltpu.VMEM((4, 320, D), low)],
    )
    act_keep, act_send = outs[4:6]
    lates = list(outs[6:10])
    branch_own, middle, middle_grad, vector = outs[10:]
    grads = exchange(outs[:4])
    grads = list(after(grads, cots[1]))
    (residual_out,) = call(
        closing_kernel,
        [((160, DC), low)],
        [act_keep, act_send, down_weight, middle, down_bias],
    )
    act_came = shift_bucket(act_send, 1)
    lates = exchange(after(lates, *grads[1:]))
    query_grad, both_grad, *away = call(
        backward_kernel,
        [((640, SPLIT), low), ((640, 2 * SPLIT), wide)] + [((320, 2 * SPLIT), low)] * 2,
        grads + [query, own_both, sib_both, chance, attended],
        [
            pltpu.VMEM((3, 1280, SPLIT), low),
            pltpu.VMEM((1280, SPLIT), low),
            pltpu.VMEM((640, SPLIT), low),
            pltpu.VMEM((640, 1280), low),
            pltpu.VMEM((SPLIT, 1280), wide),
            pltpu.VMEM((SPLIT, 1280), wide),
            pltpu.VMEM((640, 1280), wide),
        ],
    )
    arrived = [swap_core(x) for x in after(away, act_came)]
    arrived = list(after(arrived, lates[1], lates[2]))
    outs = call(
        late_kernel,
        [packed_block] * 4 + [((4, 192, D), low), ((4, 168, D), wide), ((1504, D), low)],
        [query_grad, both_grad] + arrived + hiddens + [act_keep, act_came] + cots + back + [branch_own, columns, first_gain, vector],
        [
            pltpu.VMEM((640, D), low),
            pltpu.VMEM((640, D), low),
            pltpu.VMEM((640, 3 * SPLIT), low),
            pltpu.VMEM((2, 4, 192, D), low),
            pltpu.VMEM((2, 4, 168, D), wide),
        ],
    )
    homes = list(outs[:4])
    keep_x, keep_z, send = outs[4:]
    outs = call(
        late_sum_kernel,
        [((320, D), low)] * 4 + [((336, D), wide), ((368, D), low)],
        [keep_x, keep_z, send, swap_core(send)] + homes,
    )
    home = exchange(outs[:4])
    z_keep, z_send = outs[4:]
    z_own, z_next = call(
        late_mid_kernel,
        [((168, D), wide), ((192, D), low)],
        [z_keep, z_send, shift_bucket(z_send, 1)],
    )
    z_came = shift_bucket(z_next, 2)
    keep, *send = call(
        up_grad_kernel,
        [((4, 96, D), low)] + [((128, D), low)] * 3,
        lates,
        [pltpu.VMEM((640, D), low), pltpu.VMEM((640, D), low), pltpu.VMEM((2, 4, 96, D), low)],
    )
    w_keep, w_send = call(
        up_sum_kernel,
        [((2, 96, D), wide), ((2, 96, D), low)],
        [keep] + [swap_core(x) for x in send],
    )
    w_own, w_next = call(
        up_mid_kernel,
        [((96, D), wide), ((96, D), low)],
        [w_keep, shift_bucket(w_send, 1)],
    )
    w_came = shift_bucket(w_next, 2)
    finals = call(
        final_send_kernel,
        [((96, D), low)] * 4,
        [z_own, z_next, z_came, w_own, w_came],
        [pltpu.VMEM((4, 96, D), low)],
    )
    down_own, down_other = call(down_sum_kernel, [((96, D), wide), ((96, D), low)], home)
    (down_total,) = call(
        down_final_kernel, [((96, DC), wide)], [down_own, shift_bucket(down_other, 2)]
    )
    (residual_grad,) = call(
        home_kernel,
        [((160, DC), low)],
        home + [input_weight, residual_in, first_gain, middle_grad],
        [pltpu.VMEM((4, 240, 2 * SPLIT), low)],
    )
    in_total, up_total, out_total, first, query_sum, value_sum, output, second, up_sum_bias, down, stats = call(
        final_kernel,
        [((24, 3 * D), wide), ((24, FF), wide), ((24, DC), wide)]
        + [((D,), wide)] * 3
        + [((DC,), wide), ((D,), wide), ((FF,), wide), ((DC,), wide), ((2,), wide)],
        [lengths] + exchange(finals),
        [pltpu.VMEM((4, 96, D), wide)],
        small=1,
    )
    return (
        residual_out,
        residual_grad,
        first,
        in_total,
        query_sum,
        value_sum,
        out_total,
        output,
        second,
        up_total,
        up_sum_bias,
        down_total,
        down,
        stats,
    )


def solution(mesh):
    placed = (
        P(("bucket", "blk"), None),
        P(("bucket", "blk"), None),
        P(),
        P(),
        P(),
        P(),
        P(),
        P(),
        P(),
        P(),
        P(),
        P(),
        P(),
        P(),
        P("bucket", None),
        P(),
    )
    return jax.shard_map(
        body if dict(mesh.shape) == {"bucket": 4, "blk": 8} else general_body,
        mesh=mesh,
        in_specs=placed,
        out_specs=(
            P(("bucket", "blk"), None),
            P(("bucket", "blk"), None),
            P(),
            P(("bucket", "blk"), None),
            P(),
            P(),
            P(("bucket", "blk"), None),
            P(),
            P(),
            P(("bucket", "blk"), None),
            P(),
            P(("bucket", "blk"), None),
            P(),
            P(),
        ),
        check_vma=False,
    )
```

```python
import jax
import jax.numpy as jnp
from jax import lax
from jax.experimental import pallas as pl
from jax.experimental.pallas import tpu as pltpu
from jax.sharding import PartitionSpec as P

D = 768
HEADS = 12
HEAD_DIM = 64


epsilon = 1e-05
masked_value = -1e30


def center_norm(resid, gain):
    full = jnp.concatenate([resid, -jnp.sum(resid, axis=1, keepdims=True)], axis=1)
    root = jnp.sqrt(jnp.mean(full * full, axis=1, keepdims=True) + epsilon)
    return (full / root * gain, root[:, 0])


def gelu_tanh(inputs):
    return jax.nn.gelu(inputs, approximate=True)


def heads_of(block):
    return block.reshape(block.shape[0], HEADS, HEAD_DIM)


def places_of(span_order, begin, count, half_rows):
    spans = lax.dynamic_slice_in_dim(span_order, begin // half_rows, count // half_rows)
    inner = jnp.arange(half_rows, dtype=jnp.int32)
    return (spans[:, None] * half_rows + inner[None, :]).reshape(count)


def documents_of(places, lengths, offsets):
    first_in = (places >= offsets[0, 0]) & (places < offsets[0, 0] + lengths[0, 0])
    second_in = (places >= offsets[0, 1]) & (places < offsets[0, 1] + lengths[0, 1])
    return jnp.where(first_in, 0, jnp.where(second_in, 1, -1)).astype(jnp.int32)


def allowed_of(query_places, query_docs, key_places, key_docs):
    same = (query_docs[:, None] == key_docs[None, :]) & (query_docs[:, None] >= 0)
    return (same & (key_places[None, :] <= query_places[:, None]))[None]


def block_shape(count, unit):
    shards = count // unit
    width = max(1, 1024 // unit)
    while shards % width != 0:
        width = width - 1
    return (shards // width, width * unit)


def general_body(
    residual_in,
    out_cotangent,
    first_gain,
    input_weight,
    query_bias,
    value_bias,
    output_weight,
    output_bias,
    second_gain,
    up_weight,
    up_bias,
    down_weight,
    down_bias,
    lengths,
    offsets,
    span_order,
):
    rows = residual_in.shape[0]
    half_rows = rows // 2
    score_scale = HEAD_DIM ** (-0.5)
    index = lax.axis_index("blk")
    bucket_index = lax.axis_index("bucket")
    own_lengths = lax.dynamic_slice_in_dim(lengths, bucket_index, 1, 0)
    valid_count = jnp.sum(lengths.astype(jnp.float32))
    query_places = places_of(span_order, index * rows, rows, half_rows)
    query_docs = documents_of(query_places, own_lengths, offsets)
    valid = (query_docs >= 0).astype(jnp.float32)
    resid = residual_in.astype(jnp.float32)
    normed, first_back, first_root = jax.vjp(center_norm, resid, first_gain, has_aux=True)
    hidden_in = normed.astype(jnp.bfloat16)
    projected = jnp.dot(hidden_in, input_weight, preferred_element_type=jnp.float32)
    query = (projected[:, :D] + query_bias).astype(jnp.bfloat16)
    keys = projected[:, D : 2 * D].astype(jnp.bfloat16)
    values = (projected[:, 2 * D :] + value_bias).astype(jnp.bfloat16)
    query_heads = heads_of(query)
    key_heads = heads_of(keys)
    value_heads = heads_of(values)
    initial = (
        jnp.full((HEADS, rows), masked_value, jnp.float32),
        jnp.zeros((HEADS, rows), jnp.float32),
        jnp.zeros((HEADS, rows, HEAD_DIM), jnp.float32),
    )
    state = initial
    key_piece = lax.all_gather(keys, "blk", axis=0, tiled=True)
    value_piece = lax.all_gather(values, "blk", axis=0, tiled=True)
    count = key_piece.shape[0]
    number, width = block_shape(count, rows)
    key_places = places_of(span_order, jnp.int32(0), count, half_rows)
    key_docs = documents_of(key_places, own_lengths, offsets)

    def forward_advance(state, parts):
        key_block, value_block, places_block, docs_block = parts
        peak, total, summed = state
        scores = (
            jnp.einsum(
                "qhd,khd->hqk", query_heads, heads_of(key_block), preferred_element_type=jnp.float32
            )
            * score_scale
        )
        allowed = allowed_of(query_places, query_docs, places_block, docs_block)
        masked = jnp.where(allowed, scores, masked_value)
        new_peak = jnp.maximum(peak, jnp.max(masked, axis=2))
        decay = jnp.exp(peak - new_peak)
        weights = jnp.where(allowed, jnp.exp(masked - new_peak[:, :, None]), 0.0)
        total = total * decay + jnp.sum(weights, axis=2)
        summed = summed * decay[:, :, None] + jnp.einsum(
            "hqk,khd->hqd",
            weights.astype(jnp.bfloat16),
            heads_of(value_block),
            preferred_element_type=jnp.float32,
        )
        return ((new_peak, total, summed), None)

    state, _ = lax.scan(
        forward_advance,
        state,
        (
            key_piece.reshape(number, width, D),
            value_piece.reshape(number, width, D),
            key_places.reshape(number, width),
            key_docs.reshape(number, width),
        ),
    )
    peak, total, summed = state
    denominator = total + 1.0 - valid[None, :]
    attended = summed / denominator[:, :, None]
    log_total = peak + jnp.log(denominator)
    mixed = attended.transpose(1, 0, 2).reshape(rows, D).astype(jnp.bfloat16)
    branch = jnp.dot(mixed, output_weight, preferred_element_type=jnp.float32) + output_bias
    middle = resid + branch
    normed_two, second_back, second_root = jax.vjp(center_norm, middle, second_gain, has_aux=True)
    hidden_two = normed_two.astype(jnp.bfloat16)
    upward = jnp.dot(hidden_two, up_weight, preferred_element_type=jnp.float32) + up_bias
    active_float, gelu_back = jax.vjp(gelu_tanh, upward)
    active = active_float.astype(jnp.bfloat16)
    closing = jnp.dot(active, down_weight, preferred_element_type=jnp.float32) + down_bias
    residual_out = (middle + closing).astype(jnp.bfloat16)
    stat_sums = jnp.stack([jnp.sum(valid * first_root), jnp.sum(valid * second_root)])
    stat_sums = lax.psum(stat_sums, ("bucket", "blk"))
    cotangent = out_cotangent.astype(jnp.float32)
    down_grad = jnp.einsum("rf,rc->fc", active, out_cotangent, preferred_element_type=jnp.float32)
    down_bias_grad = jnp.sum(cotangent, axis=0)
    active_grad = jnp.einsum(
        "rc,fc->rf", out_cotangent, down_weight, preferred_element_type=jnp.float32
    )
    (upward_float,) = gelu_back(active_grad)
    upward_grad = upward_float.astype(jnp.bfloat16)
    up_grad = jnp.einsum("rd,rf->df", hidden_two, upward_grad, preferred_element_type=jnp.float32)
    up_bias_grad = jnp.sum(upward_grad.astype(jnp.float32), axis=0)
    hidden_two_grad = jnp.einsum(
        "rf,df->rd", upward_grad, up_weight, preferred_element_type=jnp.float32
    )
    middle_part, second_gain_grad = second_back(hidden_two_grad)
    middle_grad = cotangent + middle_part
    branch_grad = middle_grad.astype(jnp.bfloat16)
    output_grad = jnp.einsum("rd,rc->dc", mixed, branch_grad, preferred_element_type=jnp.float32)
    output_bias_grad = jnp.sum(branch_grad.astype(jnp.float32), axis=0)
    attended_grad = jnp.einsum(
        "rc,dc->rd", branch_grad, output_weight, preferred_element_type=jnp.float32
    ).astype(jnp.bfloat16)
    grad_heads = heads_of(attended_grad)
    delta = jnp.einsum("rhd,hrd->hr", grad_heads.astype(jnp.float32), attended)
    query_zero = jnp.zeros((rows, HEADS, HEAD_DIM), jnp.float32)
    accum = query_zero
    key_piece = lax.all_gather(keys, "blk", axis=0, tiled=True)
    value_piece = lax.all_gather(values, "blk", axis=0, tiled=True)
    count = key_piece.shape[0]
    number, width = block_shape(count, rows)
    key_places = places_of(span_order, jnp.int32(0), count, half_rows)
    key_docs = documents_of(key_places, own_lengths, offsets)

    def query_advance(accum, parts):
        key_block, value_block, places_block, docs_block = parts
        block_keys = heads_of(key_block)
        scores = (
            jnp.einsum("qhd,khd->hqk", query_heads, block_keys, preferred_element_type=jnp.float32)
            * score_scale
        )
        allowed = allowed_of(query_places, query_docs, places_block, docs_block)
        chance = jnp.where(
            allowed, jnp.exp(jnp.where(allowed, scores, masked_value) - log_total[:, :, None]), 0.0
        )
        push = jnp.einsum(
            "qhd,khd->hqk", grad_heads, heads_of(value_block), preferred_element_type=jnp.float32
        )
        slope = (chance * (push - delta[:, :, None])).astype(jnp.bfloat16)
        accum = (
            accum
            + jnp.einsum("hqk,khd->qhd", slope, block_keys, preferred_element_type=jnp.float32)
            * score_scale
        )
        return (accum, None)

    accum, _ = lax.scan(
        query_advance,
        accum,
        (
            key_piece.reshape(number, width, D),
            value_piece.reshape(number, width, D),
            key_places.reshape(number, width),
            key_docs.reshape(number, width),
        ),
    )
    log_all, delta_all = (
        lax.all_gather(log_total.T, "blk", axis=0, tiled=True),
        lax.all_gather(delta.T, "blk", axis=0, tiled=True),
    )
    key_zero = jnp.zeros((rows, HEADS, HEAD_DIM), jnp.float32)
    state = (key_zero, key_zero)
    begin = jnp.int32(0)
    query_piece = lax.all_gather(query, "blk", axis=0, tiled=True)
    grad_piece = lax.all_gather(attended_grad, "blk", axis=0, tiled=True)
    count = query_piece.shape[0]
    number, width = block_shape(count, rows)
    piece_places = places_of(span_order, begin, count, half_rows)
    piece_docs = documents_of(piece_places, own_lengths, offsets)
    piece_log = lax.dynamic_slice_in_dim(log_all, begin, count, 0)
    piece_delta = lax.dynamic_slice_in_dim(delta_all, begin, count, 0)

    def key_advance(state, parts):
        query_block, grad_block, places_block, docs_block, log_block, delta_block = parts
        key_sum, value_sum = state
        block_query = heads_of(query_block)
        block_grad = heads_of(grad_block)
        scores = (
            jnp.einsum("qhd,khd->hqk", block_query, key_heads, preferred_element_type=jnp.float32)
            * score_scale
        )
        allowed = allowed_of(places_block, docs_block, query_places, query_docs)
        chance = jnp.where(
            allowed,
            jnp.exp(jnp.where(allowed, scores, masked_value) - log_block.T[:, :, None]),
            0.0,
        )
        value_sum = value_sum + jnp.einsum(
            "hqk,qhd->khd",
            chance.astype(jnp.bfloat16),
            block_grad,
            preferred_element_type=jnp.float32,
        )
        push = jnp.einsum(
            "qhd,khd->hqk", block_grad, value_heads, preferred_element_type=jnp.float32
        )
        slope = (chance * (push - delta_block.T[:, :, None])).astype(jnp.bfloat16)
        key_sum = (
            key_sum
            + jnp.einsum("hqk,qhd->khd", slope, block_query, preferred_element_type=jnp.float32)
            * score_scale
        )
        return ((key_sum, value_sum), None)

    state, _ = lax.scan(
        key_advance,
        state,
        (
            query_piece.reshape(number, width, D),
            grad_piece.reshape(number, width, D),
            piece_places.reshape(number, width),
            piece_docs.reshape(number, width),
            piece_log.reshape(number, width, HEADS),
            piece_delta.reshape(number, width, HEADS),
        ),
    )
    key_sum, value_sum = state
    query_low = accum.reshape(rows, D).astype(jnp.bfloat16)
    key_low = key_sum.reshape(rows, D).astype(jnp.bfloat16)
    value_low = value_sum.reshape(rows, D).astype(jnp.bfloat16)
    projected_grad = jnp.concatenate([query_low, key_low, value_low], axis=1)
    input_grad = jnp.einsum(
        "rd,re->de", hidden_in, projected_grad, preferred_element_type=jnp.float32
    )
    query_bias_grad = jnp.sum(query_low.astype(jnp.float32), axis=0)
    value_bias_grad = jnp.sum(value_low.astype(jnp.float32), axis=0)
    hidden_in_grad = jnp.einsum(
        "re,de->rd", projected_grad, input_weight, preferred_element_type=jnp.float32
    )
    resid_part, first_gain_grad = first_back(hidden_in_grad)
    residual_grad = (middle_grad + resid_part).astype(jnp.bfloat16)
    input_part, output_part, up_part, down_part = (
        lax.psum_scatter(input_grad, ("bucket", "blk"), scatter_dimension=0, tiled=True),
        lax.psum_scatter(output_grad, ("bucket", "blk"), scatter_dimension=0, tiled=True),
        lax.psum_scatter(up_grad, ("bucket", "blk"), scatter_dimension=0, tiled=True),
        lax.psum_scatter(down_grad, ("bucket", "blk"), scatter_dimension=0, tiled=True),
    )
    (
        first_sum,
        query_sum_bias,
        value_sum_bias,
        output_sum_bias,
        second_sum,
        up_sum_bias,
        down_sum_bias,
    ) = lax.psum(
        (
            first_gain_grad,
            query_bias_grad,
            value_bias_grad,
            output_bias_grad,
            second_gain_grad,
            up_bias_grad,
            down_bias_grad,
        ),
        ("bucket", "blk"),
    )
    mean_norms = stat_sums / valid_count
    return (
        residual_out,
        residual_grad,
        first_sum,
        input_part,
        query_sum_bias,
        value_sum_bias,
        output_part,
        output_sum_bias,
        second_sum,
        up_part,
        up_sum_bias,
        down_part,
        down_sum_bias,
        mean_norms,
    )


DC = 767
SPLIT = 192
FF = 3072
low = jnp.bfloat16
wide = jnp.float32
VMEM = pl.BlockSpec(memory_space=pltpu.VMEM)
SMEM = pl.BlockSpec(memory_space=pltpu.SMEM)
HBM = pl.BlockSpec(memory_space=pltpu.HBM)

def padded_bytes(shape, dtype):
    shape = (1, 1) + tuple(shape)
    size = jnp.dtype(dtype).itemsize
    rows, lanes = -(-shape[-2] // 16) * 16, -(-shape[-1] // 128) * 128
    for d in shape[:-2]:
        rows = rows * d
    return rows * lanes * size


def call(kernel, outs, ins, scratch=(), extra=6, small=0, far=(), work=0):
    shapes = [jax.ShapeDtypeStruct(s, d) for s, d in outs]
    held = [(s, d) for s, d in outs]
    held += [(x.shape, x.dtype) for i, x in enumerate(ins) if i >= small and i not in far]
    held += [(s.shape, s.dtype) for s in scratch if s.memory_space == pltpu.VMEM]
    limit = sum(padded_bytes(s, d) for s, d in held) + extra * 2**20
    return pl.pallas_call(
        kernel,
        out_shape=shapes,
        in_specs=[SMEM if i < small else HBM if i in far else VMEM for i in range(len(ins))],
        out_specs=[VMEM] * len(outs),
        scratch_shapes=list(scratch),
        compiler_params=pltpu.CompilerParams(vmem_limit_bytes=min(limit, 60 * 2**20)),
        cost_estimate=pl.CostEstimate(
            flops=int(1000 + work * 1.1e9),
            bytes_accessed=1000,
            transcendentals=0,
        ),
    )(*ins)


def here():
    index = lax.axis_index("blk")
    return index // 2, lax.axis_index("bucket"), index % 2


def full_of(x):
    rows=x.shape[0]
    wide_x=jnp.concatenate([x,jnp.zeros((rows,1),x.dtype)],axis=1)
    last=lax.broadcasted_iota(jnp.int32,(rows,D),1)==D-1
    return jnp.where(last,-jnp.sum(x,axis=1,keepdims=True),wide_x)

def row(ref):
    return ref[...].reshape(1, ref.shape[0])


def nt(a, b):
    return lax.dot_general(a, b, (((1,), (1,)), ((), ())), preferred_element_type=wide)


def tn(a, b):
    return lax.dot_general(a, b, (((0,), (0,)), ((), ())), preferred_element_type=wide)


def packed(x):
    half = x.shape[0] // 2
    return jnp.concatenate([x[:half], x[half:]], axis=1).astype(low)


def unpacked(x):
    x = x.astype(wide)
    half = x.shape[1] // 2
    return jnp.concatenate([x[:, :half], x[:, half:]], axis=0)


def split_pair(x):
    hi = x.astype(low)
    return hi, (x - hi.astype(wide)).astype(low)


def head_mask(x, h):
    lane = lax.broadcasted_iota(jnp.int32, x.shape, 1)
    return jnp.where((lane >= h * 64) & (lane < (h + 1) * 64), x, jnp.zeros_like(x))


def limits(spans, offsets, lengths, bucket, chip, core, half):
    place = spans[chip * 4 + core * 2 + half] * 80 + lax.broadcasted_iota(jnp.int32, (80, 1), 0)
    one, two = offsets[0, 0], offsets[0, 1]
    first = (place >= one) & (place < one + lengths[bucket, 0])
    second = (place >= two) & (place < two + lengths[bucket, 1])
    return jnp.where(first, one, two), jnp.where(first | second, place, -1)


def entry_kernel(
    resid_far, gain_far, weight_far, qbias_far, vbias_far, s0, s1, s2, s3, hidden_out, root_out,
    buf, resid, gain, weight, qbias, vbias, sems,
):
    me = here()[0]
    copies = [
        pltpu.make_async_copy(a, b, sems.at[i])
        for i, (a, b) in enumerate(
            [(resid_far, resid), (gain_far, gain), (qbias_far, qbias), (vbias_far, vbias)]
            + [(weight_far.at[:, pl.ds(i * D, D)], weight.at[i]) for i in range(3)]
        )
    ]
    for copy in copies:
        copy.start()
    copies[0].wait()
    full = full_of(resid[...].astype(wide))
    root = jnp.sqrt(jnp.mean(full * full, axis=1, keepdims=True) + epsilon)
    root_out[...] = root
    copies[1].wait()
    hidden = (full / root * row(gain)).astype(low)
    hidden_out[...] = hidden
    copies[2].wait()
    copies[3].wait()
    for i in range(3):
        copies[4 + i].wait()
        p = jnp.dot(hidden, weight[i], preferred_element_type=wide)
        if i == 0:
            p = (p + row(qbias)) * 0.125
        if i == 2:
            p = p + row(vbias)
        for j in range(4):
            buf[j ^ me, i * 80 : (i + 1) * 80, :] = packed(p[:, j * SPLIT : (j + 1) * SPLIT])
    for r, s in enumerate((s0, s1, s2, s3)):
        s[...] = buf[r]


def push_kernel(spans, offsets, lengths, cot, weight, out, bounds, places):
    me, bucket, core = here()
    for i in range(4):
        out[:, i * D : (i + 1) * D] = nt(cot[...], weight[i * D : (i + 1) * D, :])
    lane = lax.broadcasted_iota(jnp.int32, (1, 1280), 1)
    place = lane
    for blk in range(16):
        chip = ((blk % 8) // 2) ^ me
        span = spans[chip * 4 + (core ^ (blk // 8)) * 2 + blk % 2]
        place = jnp.where((lane >= blk * 80) & (lane < (blk + 1) * 80), lane + (span - blk) * 80, place)
    places[...] = place
    for blk in range(8):
        lo, hi = limits(spans, offsets, lengths, bucket, (blk // 2) ^ me, core, blk % 2)
        bounds[blk * 80 : (blk + 1) * 80, 0:1] = lo
        bounds[blk * 80 : (blk + 1) * 80, 1:2] = hi


def columns_kernel(weight, out):
    me = here()[0]
    for j in range(4):

        @pl.when(me == j)
        def _():
            for i in range(3):
                piece = weight[:, i * D + j * SPLIT : i * D + (j + 1) * SPLIT].astype(wide)
                out[:, i * SPLIT : (i + 1) * SPLIT] = piece.astype(low)


def assemble_kernel(p0, p1, p2, p3, query, both):
    for r, p in enumerate((p0, p1, p2, p3)):
        rows = slice(r * 160, (r + 1) * 160)
        query[rows, :] = unpacked(p[0:80, :]).astype(low)
        both[rows, :SPLIT] = unpacked(p[80:160, :]).astype(low)
        both[rows, SPLIT:] = unpacked(p[160:240, :]).astype(low)


def forward_kernel(
    bounds, places, query, own, sib, chance, attended, b0, b1, b2, b3, keys, vals, scores
):
    keys[:640, :] = own[:, :SPLIT]
    keys[640:, :] = sib[:, :SPLIT]
    v = jnp.concatenate([own[:, SPLIT:].astype(wide), sib[:, SPLIT:].astype(wide)], axis=0)
    for h in range(3):
        vals[h] = head_mask(v, h).astype(low)
    place = places[...]
    q = query[...].astype(wide)
    for h in range(3):
        scores[...] = nt(head_mask(q, h).astype(low), keys[...])
        for blk in range(8):
            rows = slice(blk * 80, (blk + 1) * 80)
            lo, hi = bounds[rows, 0:1], bounds[rows, 1:2]
            s = jnp.where((place >= lo) & (place <= hi), scores[rows, :], masked_value)
            peak = jnp.max(s, axis=1, keepdims=True)
            w = jnp.exp(s - peak)
            total = jnp.sum(w, axis=1, keepdims=True)
            chance[h, rows, :] = (w * jnp.where(hi >= 0, 1.0 / total, 0.0)).astype(low)
        part = jnp.dot(chance[h], vals[h], preferred_element_type=wide)
        if h == 0:
            attended[...] = part
        else:
            attended[...] += part
    acc = attended[...]
    for r, b in enumerate((b0, b1, b2, b3)):
        b[...] = packed(acc[r * 160 : (r + 1) * 160])


def middle_kernel(
    bounds, p0, p1, p2, p3, out_weight, out_bias, resid, root_in, cot, gain, up_weight, up_bias, push,
    d0, d1, d2, d3, act_keep, act_send, n0, n1, n2, n3, branch_own, middle, middle_grad, vector,
    dbuf, abuf, nbuf,
):
    me, bucket, core = here()
    branch = row(out_bias)
    for r, p in enumerate((p0, p1, p2, p3)):
        w = out_weight[pl.ds(pl.multiple_of((me ^ r) * SPLIT, SPLIT), SPLIT), :]
        branch = branch + jnp.dot(unpacked(p[...]).astype(low), w, preferred_element_type=wide)
    mid = resid[...].astype(wide) + branch
    middle[...] = mid
    full = full_of(mid)
    root = jnp.sqrt(jnp.mean(full * full, axis=1, keepdims=True) + epsilon)
    n = full / root
    hidden = (n * row(gain)).astype(low)
    for r in range(4):
        nbuf[r, 0:160, :] = hidden
    e = jnp.zeros((160, D), wide)
    c = 0.7978845608028654
    up_sums = []
    for blk in range(4):
        cols = slice(blk * D, (blk + 1) * D)
        u = jnp.dot(hidden, up_weight[:, cols], preferred_element_type=wide) + up_bias[cols].reshape(1, D)
        square = u * u
        t = jnp.tanh(u * (c + (c * 0.044715) * square))
        gate = 0.5 + 0.5 * t
        act = u * gate
        abuf[blk ^ bucket] = act.astype(low)
        slope = gate + act * (1.0 - t) * (c + (3 * c * 0.044715) * square)
        g = (push[:, cols] * slope).astype(low)
        nbuf[blk ^ me, 160:320, :] = g
        up_sums.append(jnp.sum(g.astype(wide), axis=0, keepdims=True))
        e = e + nt(g, up_weight[:, cols])
    gain_sum = jnp.sum(e * n, axis=0, keepdims=True)
    eg = e * row(gain)
    f = (eg - n * jnp.mean(eg * n, axis=1, keepdims=True)) / root
    cot_wide = jnp.concatenate([cot[...].astype(wide), jnp.zeros((160, 1), wide)], axis=1)
    lane = lax.broadcasted_iota(jnp.int32, (160, D), 1)
    last = jnp.sum(jnp.where(lane == D - 1, f, 0.0), axis=1, keepdims=True)
    grad = jnp.where(lane == D - 1, 0.0, cot_wide + f - last)
    middle_grad[...] = grad
    grad_low = grad.astype(low)
    grad_wide = grad_low.astype(wide)
    branch_own[...] = grad_low
    back = nt(grad_wide[:, :DC].astype(low), out_weight[...])
    for j in range(4):
        dbuf[j ^ me] = packed(back[:, j * SPLIT : (j + 1) * SPLIT])
    for r in range(4):
        (d0, d1, d2, d3)[r][...] = dbuf[r]
        (act_keep, act_send)[r % 2][r // 2 * 160 : r // 2 * 160 + 160, :] = abuf[r]
        (n0, n1, n2, n3)[r][...] = nbuf[r]
    valid = jnp.where(bounds[0:160, 1:2] >= 0, 1.0, 0.0)
    one = jnp.sum(valid * root_in[...], axis=0, keepdims=True)
    two = jnp.sum(valid * root, axis=0, keepdims=True)
    at = lax.broadcasted_iota(jnp.int32, (1, D), 1)
    stats = jnp.where(at == 0, one, jnp.where(at == 1, two, 0.0))
    zero = jnp.zeros((1, D), wide)
    sums = [zero, zero, zero, jnp.sum(grad_wide, axis=0, keepdims=True), gain_sum] + up_sums
    sums += [jnp.sum(cot_wide, axis=0, keepdims=True), stats] + [zero] * 5
    vector[...] = jnp.concatenate(sums, axis=0)


def closing_kernel(act_keep, act_send, weight, middle, bias, out):
    bucket = here()[1]
    acc = middle[...] + row(bias)
    for d in range(4):
        w = weight[pl.ds(pl.multiple_of((bucket ^ d) * D, D), D), :]
        a = (act_keep, act_send)[d % 2][d // 2 * 160 : d // 2 * 160 + 160, :]
        acc = acc + jnp.dot(a, w, preferred_element_type=wide)
    out[...] = acc.astype(low)


def backward_kernel(
    d0, d1, d2, d3, query, own, sib, chance, attended, query_grad, both_grad, away_one, away_two,
    keys, vals, grads, slopes, keys_turned, vals_turned, pushes,
):
    for r, d in enumerate((d0, d1, d2, d3)):
        grads[r * 160 : (r + 1) * 160, :] = unpacked(d[...]).astype(low)
    k = jnp.concatenate([own[:, :SPLIT], sib[:, :SPLIT]], axis=0).astype(wide)
    for h in range(3):
        keys[h] = head_mask(k, h).astype(low)
    vals[:640, :] = own[:, SPLIT:].astype(wide).astype(low)
    vals[640:, :] = sib[:, SPLIT:].astype(wide).astype(low)
    g = grads[...].astype(wide)
    q_turned = jnp.transpose(query[...].astype(wide)).astype(low)
    g_turned = jnp.transpose(g).astype(low)
    dq = jnp.zeros((640, SPLIT), wide)
    for h in range(3):
        gh = head_mask(g, h)
        delta = jnp.sum(gh * attended[...], axis=1, keepdims=True)
        pushes[...] = nt(gh.astype(low), vals[...])
        for r in range(8):
            rows = slice(r * 80, (r + 1) * 80)
            slopes[rows, :] = (chance[h, rows, :].astype(wide) * (pushes[rows, :] - delta[rows, :])).astype(low)
        dq = dq + jnp.dot(slopes[...], keys[h], preferred_element_type=wide)
        rows = slice(h * 64, (h + 1) * 64)
        keys_turned[rows, :] = jnp.dot(q_turned[rows], slopes[...], preferred_element_type=wide)
        vals_turned[rows, :] = jnp.dot(g_turned[rows], chance[h], preferred_element_type=wide)
    query_grad[...] = (dq * 0.125).astype(low)
    dk = jnp.transpose(keys_turned[...])
    dv = jnp.transpose(vals_turned[...])
    both_grad[:, :SPLIT] = dk[:640]
    both_grad[:, SPLIT:] = dv[:640]
    away_one[:, :SPLIT] = dk[640:960].astype(low)
    away_one[:, SPLIT:] = dv[640:960].astype(low)
    away_two[:, :SPLIT] = dk[960:].astype(low)
    away_two[:, SPLIT:] = dv[960:].astype(low)


def late_kernel(
    query_grad, both_grad, arrive_one, arrive_two, i0, i1, i2, i3, act_keep, act_came, c0, c1, p0, p1, p2, p3, branch_own, columns, gain, vector,
    h0, h1, h2, h3, keep_x, keep_z, send, left, right, heads, xbuf, zbuf,
):
    me, bucket, core = here()
    arrived = jnp.concatenate([arrive_one[...].astype(wide), arrive_two[...].astype(wide)], axis=0)
    both = both_grad[...] + arrived
    parts = [query_grad[...].astype(wide), both[:, :SPLIT], both[:, SPLIT:]]
    parts = [p.astype(low).astype(wide) for p in parts]
    for r, h in enumerate((h0, h1, h2, h3)):
        left[r * 160 : (r + 1) * 160, :] = (i0, i1, i2, i3)[r][...]
        for i in range(3):
            h[i * 80 : (i + 1) * 80, :] = packed(parts[i][r * 160 : (r + 1) * 160])
    heads[...] = jnp.concatenate(parts, axis=1).astype(low)
    grad = tn(left[...], heads[...])
    sums = jnp.sum(grad * columns[...].astype(wide), axis=1, keepdims=True)
    gain_row = jnp.transpose(jnp.broadcast_to(sums, (D, 128)))[0:1] / row(gain)
    lane = lax.broadcasted_iota(jnp.int32, (1, D), 1)
    mine = (lane >= me * SPLIT) & (lane < (me + 1) * SPLIT)

    def column_sum(x):
        s = jnp.sum(x, axis=0, keepdims=True)
        return jnp.where(mine, jnp.concatenate([s] * 4, axis=1), 0.0)

    at = lax.broadcasted_iota(jnp.int32, (16, D), 0)
    total = vector[...] + jnp.where(at == 0, gain_row, 0.0)
    total = total + jnp.where(at == 1, column_sum(parts[0]), 0.0)
    total = total + jnp.where(at == 2, column_sum(parts[2]), 0.0)
    thirds = [grad[:, i * SPLIT : (i + 1) * SPLIT] for i in range(3)]
    for b in range(4):
        for c in range(2):
            block = []
            for part in thirds:
                starts = [b * 192 + j * 48 + c * 24 for j in range(4)]
                block.append(jnp.concatenate([part[s : s + 24] for s in starts], axis=1))
            zbuf[c ^ core, b ^ bucket, 0:72, :] = jnp.concatenate(block, axis=0)
    for r, p in enumerate((p0, p1, p2, p3)):
        out = tn(unpacked(p[...]).astype(low), branch_own[...])
        for j in range(4):
            for c in range(2):
                s = j * 48 + c * 24
                zbuf[c ^ core, me ^ r ^ bucket, 72 + j * 24 : 96 + j * 24, :] = out[s : s + 24]
    for d, c in enumerate((c0, c1)):
        cot = c[...].astype(wide)
        right[d * 160 : (d + 1) * 160, :] = jnp.concatenate([cot, jnp.zeros((160, 1), wide)], axis=1).astype(low)
    for half in range(2):
        left[0:160, :] = act_keep[half * 160 : half * 160 + 160, :]
        left[160:320, :] = act_came[half * 160 : half * 160 + 160, :]
        down = tn(left[0:320, :], right[0:320, :])
        for j in range(4):
            for c in range(2):
                s = j * 192 + c * 96
                xbuf[c ^ core, j ^ me, half * 96 : half * 96 + 96, :] = down[s : s + 96].astype(low)
    keep_x[...] = xbuf[0]
    for r in range(4):
        keep_z[r] = zbuf[0, r]
        send[r * 192 : (r + 1) * 192, :] = xbuf[1, r]
        block = jnp.concatenate([zbuf[1, r], jnp.zeros((8, D), wide)], axis=0)
        send[768 + r * 176 : 944 + r * 176, :] = block.astype(low)
    hi, lo = split_pair(total)
    send[1472:1488, :] = hi
    send[1488:1504, :] = lo


def late_sum_kernel(keep_x, keep_z, send, arrived, h0, h1, h2, h3, x0, x1, x2, x3, z_keep, z_send):
    own = send[1472:1488, :].astype(wide) + send[1488:1504, :].astype(wide)
    hi, lo = split_pair(own + (arrived[1472:1488, :].astype(wide) + arrived[1488:1504, :].astype(wide)))
    blocks = []
    for r in range(4):
        x, h = (x0, x1, x2, x3)[r], (h0, h1, h2, h3)[r]
        x[0:192, :] = (keep_x[r].astype(wide) + arrived[r * 192 : (r + 1) * 192, :].astype(wide)).astype(low)
        x[192:272, 0:384] = h[0:80, :]
        x[192:272, 384:768] = h[80:160, :]
        v = h[160:240, :].astype(wide)
        v = jnp.concatenate([v[:40], v[40:]], axis=1)
        x[272:320, :] = jnp.concatenate([v, jnp.zeros((8, D), wide)], axis=0).astype(low)
        came = arrived[768 + r * 176 : 944 + r * 176, :].astype(wide)
        blocks.append(keep_z[r] + came[0:168])
    z_keep[0:168, :] = blocks[0]
    z_keep[168:336, :] = blocks[2]
    sums = [hi.astype(wide)[0:12], lo.astype(wide)[0:12]]
    z_send[...] = jnp.concatenate([blocks[1], blocks[3]] + sums, axis=0).astype(low)


def pair_sum(own, came, start):
    a = own[start : start + 12] + own[start + 12 : start + 24]
    b = came[start : start + 12] + came[start + 12 : start + 24]
    return a + b


def late_mid_kernel(z_keep, z_send, came, z_own, z_next):
    came = came[...].astype(wide)
    hi, lo = split_pair(pair_sum(z_send[...].astype(wide), came, 336))
    z_own[...] = z_keep[0:168, :] + came[0:168]
    block = [z_keep[168:336, :] + came[168:336], hi.astype(wide), lo.astype(wide)]
    z_next[...] = jnp.concatenate(block, axis=0).astype(low)


def up_grad_kernel(n0, n1, n2, n3, keep, send_one, send_two, left, right, buf):
    me, bucket, core = here()
    for r in range(4):
        rows = slice(r * 160, (r + 1) * 160)
        n = (n0, n1, n2, n3)[r]
        left[rows, :] = n[0:160, :]
        right[rows, :] = n[160:320, :]
    up = tn(left[...], right[...])
    for b in range(4):
        for c in range(2):
            starts = [b * 192 + j * 48 + c * 24 for j in range(4)]
            block = jnp.concatenate([up[s : s + 24] for s in starts], axis=0)
            buf[c ^ core, b ^ bucket] = block.astype(low)
    keep[...] = buf[0]
    send_one[...] = buf[1, 0:2]
    send_two[...] = buf[1, 2:4]


def up_sum_kernel(keep, arrive_one, arrive_two, w_keep, w_send):
    for d in range(4):
        total = keep[d].astype(wide) + (arrive_one, arrive_two)[d // 2][d % 2].astype(wide)
        if d % 2 == 0:
            w_keep[d // 2] = total
        else:
            w_send[d // 2] = total.astype(low)


def up_mid_kernel(w_keep, came, w_own, w_next):
    w_own[...] = w_keep[0] + came[0].astype(wide)
    w_next[...] = (w_keep[1] + came[1].astype(wide)).astype(low)


def final_send_kernel(z_own, z_next, z_came, w_own, w_came, f0, f1, f2, f3, buf):
    me = here()[0]
    came = z_came[...].astype(wide)
    ins = z_own[...] + came[0:168]
    ups = w_own[...] + w_came[...].astype(wide)
    hi, lo = split_pair(pair_sum(z_next[...].astype(wide), came, 168))
    sums = [hi.astype(wide), lo.astype(wide)]
    rest = jnp.zeros((24, SPLIT), wide)
    for j in range(4):
        lanes = slice(j * SPLIT, (j + 1) * SPLIT)
        wide_rows = [ins[i * 24 : (i + 1) * 24, lanes] for i in range(3)] + [rest]
        block = [ups[j * 24 : (j + 1) * 24], jnp.concatenate(wide_rows, axis=1)]
        block += [ins[72 + j * 24 : 96 + j * 24]] + sums
        buf[j ^ me] = jnp.concatenate(block, axis=0).astype(low)
    for r, f in enumerate((f0, f1, f2, f3)):
        f[...] = buf[r]


def final_kernel(
    lengths, f0, f1, f2, f3, in_total, up_total, out_total, first, query, value, output, second, up_bias, down, stats, buf
):
    me = here()[0]
    for r, f in enumerate((f0, f1, f2, f3)):
        buf[r ^ me] = f[...].astype(wide)
    total = buf[0, 72:84] + buf[0, 84:96]
    for j in (1, 2, 3):
        total = total + (buf[j, 72:84] + buf[j, 84:96])
    first[...] = total[0]
    query[...] = total[1]
    value[...] = total[2]
    output[...] = total[3, :DC]
    second[...] = total[4]
    for i in range(4):
        up_bias[i * D : (i + 1) * D] = total[5 + i]
    down[...] = total[9, :DC]
    count = lengths[0, 0] + lengths[0, 1]
    for b in (1, 2, 3):
        count = count + lengths[b, 0] + lengths[b, 1]
    stats[...] = total[10, :2] / count.astype(wide)
    out_total[...] = (buf[0, 48:72] + buf[1, 48:72] + buf[2, 48:72] + buf[3, 48:72])[:, :DC]
    for j in range(4):
        up_total[:, j * D : (j + 1) * D] = buf[j, 0:24, :]
    for i in range(3):
        piece = jnp.concatenate([buf[j, 24:48, i * SPLIT : (i + 1) * SPLIT] for j in range(4)], axis=1)
        in_total[:, i * D : (i + 1) * D] = piece


def home_kernel(x0, x1, x2, x3, weight, resid, gain, middle_grad, out, buf):
    me = here()[0]
    for r, x in enumerate((x0, x1, x2, x3)):
        buf[r ^ me, 0:80, :] = x[192:272, 0:384]
        buf[r ^ me, 80:160, :] = x[192:272, 384:768]
        v = x[272:320, :].astype(wide)
        buf[r ^ me, 160:240, :] = jnp.concatenate([v[:40, :384], v[:40, 384:]], axis=0).astype(low)
    e = jnp.zeros((160, D), wide)
    for i in range(3):
        g = jnp.concatenate([unpacked(buf[j, i * 80 : (i + 1) * 80, :]) for j in range(4)], axis=1)
        e = e + nt(g.astype(low), weight[:, i * D : (i + 1) * D])
    full = full_of(resid[...].astype(wide))
    root = jnp.sqrt(jnp.mean(full * full, axis=1, keepdims=True) + epsilon)
    n = full / root
    eg = e * row(gain)
    f = (eg - n * jnp.mean(eg * n, axis=1, keepdims=True)) / root
    lane = lax.broadcasted_iota(jnp.int32, (160, D), 1)
    last = jnp.sum(jnp.where(lane == D - 1, f, 0.0), axis=1, keepdims=True)
    out[...] = (middle_grad[...] + f - last)[:, :DC].astype(low)


def down_sum_kernel(x0, x1, x2, x3, own, other):
    total = x0[0:192, :].astype(wide)
    for x in (x1, x2, x3):
        total = total + x[0:192, :].astype(wide)
    own[...] = total[0:96]
    other[...] = total[96:192].astype(low)


def down_final_kernel(own, came, down_total):
    down_total[...] = (own[...] + came[...].astype(wide))[:, :DC]

def swap_chip(block, step):
    return lax.ppermute(block, "blk", [(k, k ^ (2 * step)) for k in range(8)])


def swap_core(block):
    return lax.ppermute(block, "blk", [(k, k ^ 1) for k in range(8)])


def shift_bucket(block, step):
    return lax.ppermute(block, "bucket", [(b, b ^ step) for b in range(4)])


def exchange(blocks):
    got = {r: swap_chip(blocks[r], r) for r in (3, 1, 2)}
    return [blocks[0], got[1], got[2], got[3]]


def after(values, *others):
    return lax.optimization_barrier((tuple(values), others))[0]


def body(
    residual_in,
    out_cotangent,
    first_gain,
    input_weight,
    query_bias,
    value_bias,
    output_weight,
    output_bias,
    second_gain,
    up_weight,
    up_bias,
    down_weight,
    down_bias,
    lengths,
    offsets,
    span_order,
):
    where = [span_order, offsets, lengths]
    packed_block = ((240, 2 * SPLIT), low)
    token = ((160, D), low)
    s0, s1, s2, s3, hidden, root_one = call(
        entry_kernel,
        [packed_block] * 4 + [token, ((160, 1), wide)],
        [residual_in, first_gain, input_weight, query_bias, value_bias],
        [
            pltpu.VMEM((4, 240, 2 * SPLIT), low),
            pltpu.VMEM((160, DC), low),
            pltpu.VMEM((D,), wide),
            pltpu.VMEM((3, D, D), low),
            pltpu.VMEM((D,), wide),
            pltpu.VMEM((D,), wide),
            pltpu.SemaphoreType.DMA((7,)),
        ],
        extra=60,
        far=range(5),
    )
    got = exchange([s0, s1, s2, s3])
    push, bounds, places = call(
        push_kernel,
        [((160, FF), wide), ((640, 2), jnp.int32), ((1, 1280), jnp.int32)],
        where + [out_cotangent, down_weight],
        small=3,
    )
    hiddens = exchange([hidden] * 4)
    got = list(after(got, push))
    query, own_both = call(assemble_kernel, [((640, SPLIT), low), ((640, 2 * SPLIT), low)], got)
    sib_both = swap_core(own_both)
    backed = ((80, 2 * SPLIT), low)
    chance, attended, b0, b1, b2, b3 = call(
        forward_kernel,
        [((3, 640, 1280), low), ((640, SPLIT), wide)] + [backed] * 4,
        [bounds, places, query, own_both, sib_both],
        [pltpu.VMEM((1280, SPLIT), low), pltpu.VMEM((3, 1280, SPLIT), low), pltpu.VMEM((640, 1280), wide)],
        work=7,
    )
    back = exchange([b0, b1, b2, b3])
    (cot,) = after([out_cotangent], b0)
    cots = [out_cotangent, shift_bucket(cot, 1)]
    back = list(after(back, *hiddens[1:]))
    (columns,) = call(columns_kernel, [((D, 3 * SPLIT), low)], after([input_weight], b0))
    outs = call(
        middle_kernel,
        [backed] * 4
        + [((320, D), low)] * 6
        + [token, ((160, DC), wide), ((160, D), wide), ((16, D), wide)],
        [bounds]
        + back
        + [output_weight, output_bias, residual_in, root_one, out_cotangent, second_gain]
        + [up_weight, up_bias, push],
        [pltpu.VMEM((4, 80, 2 * SPLIT), low), pltpu.VMEM((4, 160, D), low), pltpu.VMEM((4, 320, D), low)],
    )
    act_keep, act_send = outs[4:6]
    lates = list(outs[6:10])
    branch_own, middle, middle_grad, vector = outs[10:]
    grads = exchange(outs[:4])
    grads = list(after(grads, cots[1]))
    (residual_out,) = call(
        closing_kernel,
        [((160, DC), low)],
        [act_keep, act_send, down_weight, middle, down_bias],
    )
    act_came = shift_bucket(act_send, 1)
    lates = exchange(after(lates, *grads[1:]))
    query_grad, both_grad, *away = call(
        backward_kernel,
        [((640, SPLIT), low), ((640, 2 * SPLIT), wide)] + [((320, 2 * SPLIT), low)] * 2,
        grads + [query, own_both, sib_both, chance, attended],
        [
            pltpu.VMEM((3, 1280, SPLIT), low),
            pltpu.VMEM((1280, SPLIT), low),
            pltpu.VMEM((640, SPLIT), low),
            pltpu.VMEM((640, 1280), low),
            pltpu.VMEM((SPLIT, 1280), wide),
            pltpu.VMEM((SPLIT, 1280), wide),
            pltpu.VMEM((640, 1280), wide),
        ],
    )
    arrived = [swap_core(x) for x in after(away, act_came)]
    arrived = list(after(arrived, lates[1], lates[2]))
    outs = call(
        late_kernel,
        [packed_block] * 4 + [((4, 192, D), low), ((4, 168, D), wide), ((1504, D), low)],
        [query_grad, both_grad] + arrived + hiddens + [act_keep, act_came] + cots + back + [branch_own, columns, first_gain, vector],
        [
            pltpu.VMEM((640, D), low),
            pltpu.VMEM((640, D), low),
            pltpu.VMEM((640, 3 * SPLIT), low),
            pltpu.VMEM((2, 4, 192, D), low),
            pltpu.VMEM((2, 4, 168, D), wide),
        ],
    )
    homes = list(outs[:4])
    keep_x, keep_z, send = outs[4:]
    outs = call(
        late_sum_kernel,
        [((320, D), low)] * 4 + [((336, D), wide), ((360, D), low)],
        [keep_x, keep_z, send, swap_core(send)] + homes,
    )
    home = exchange(outs[:4])
    z_keep, z_send = outs[4:]
    z_own, z_next = call(
        late_mid_kernel,
        [((168, D), wide), ((192, D), low)],
        [z_keep, z_send, shift_bucket(z_send, 1)],
    )
    z_came = shift_bucket(z_next, 2)
    keep, *send = call(
        up_grad_kernel,
        [((4, 96, D), low)] + [((2, 96, D), low)] * 2,
        list(after(lates, z_send)),
        [pltpu.VMEM((640, D), low), pltpu.VMEM((640, D), low), pltpu.VMEM((2, 4, 96, D), low)],
    )
    w_keep, w_send = call(
        up_sum_kernel,
        [((2, 96, D), wide), ((2, 96, D), low)],
        [keep] + [swap_core(x) for x in send],
    )
    w_own, w_next = call(
        up_mid_kernel,
        [((96, D), wide), ((96, D), low)],
        [w_keep, shift_bucket(w_send, 1)],
    )
    w_came = shift_bucket(w_next, 2)
    finals = call(
        final_send_kernel,
        [((96, D), low)] * 4,
        [z_own, z_next, z_came, w_own, w_came],
        [pltpu.VMEM((4, 96, D), low)],
    )
    down_own, down_other = call(down_sum_kernel, [((96, D), wide), ((96, D), low)], home)
    (down_total,) = call(
        down_final_kernel, [((96, DC), wide)], [down_own, shift_bucket(down_other, 2)]
    )
    (residual_grad,) = call(
        home_kernel,
        [((160, DC), low)],
        home + [input_weight, residual_in, first_gain, middle_grad],
        [pltpu.VMEM((4, 240, 2 * SPLIT), low)],
    )
    in_total, up_total, out_total, first, query_sum, value_sum, output, second, up_sum_bias, down, stats = call(
        final_kernel,
        [((24, 3 * D), wide), ((24, FF), wide), ((24, DC), wide)]
        + [((D,), wide)] * 3
        + [((DC,), wide), ((D,), wide), ((FF,), wide), ((DC,), wide), ((2,), wide)],
        [lengths] + exchange(finals),
        [pltpu.VMEM((4, 96, D), wide)],
        small=1,
    )
    return (
        residual_out,
        residual_grad,
        first,
        in_total,
        query_sum,
        value_sum,
        out_total,
        output,
        second,
        up_total,
        up_sum_bias,
        down_total,
        down,
        stats,
    )


def solution(mesh):
    placed = (
        P(("bucket", "blk"), None),
        P(("bucket", "blk"), None),
        P(),
        P(),
        P(),
        P(),
        P(),
        P(),
        P(),
        P(),
        P(),
        P(),
        P(),
        P(),
        P("bucket", None),
        P(),
    )
    return jax.shard_map(
        body if dict(mesh.shape) == {"bucket": 4, "blk": 8} else general_body,
        mesh=mesh,
        in_specs=placed,
        out_specs=(
            P(("bucket", "blk"), None),
            P(("bucket", "blk"), None),
            P(),
            P(("bucket", "blk"), None),
            P(),
            P(),
            P(("bucket", "blk"), None),
            P(),
            P(),
            P(("bucket", "blk"), None),
            P(),
            P(("bucket", "blk"), None),
            P(),
            P(),
        ),
        check_vma=False,
    )
```
